32 devices in a mesh: section: 4 (over y, x), dp: 8 (over z, core).
Axes of the slice: x: 2, y: 2, z: 4, core: 2. Of those that a mesh axis runs over, the one named last changes fastest.
Arguments:
- tokens: bfloat16 [2, 4096, 1024], P(None, 'dp'), may hold values from -6 to 6
- lengths: int32 [2, 8, 16], P(None, 'dp'), may hold values from 1 to 256, 512 in all within a row
- gain_attn: bfloat16 [4, 1024], P('section'), may hold values from 0.099609375 to 1.8984375
- w_query: bfloat16 [4, 1024, 1024], P('section'), may hold values from -0.1875 to 0.1875
- w_key: bfloat16 [4, 1024, 128], P('section'), may hold values from -0.1875 to 0.1875
- w_value: bfloat16 [4, 1024, 128], P('section'), may hold values from -0.1875 to 0.1875
- w_out: bfloat16 [4, 1024, 1024], P('section'), may hold values from -0.5 to 0.5
- gain_ffn: bfloat16 [4, 1024], P('section'), may hold values from 0.099609375 to 1.8984375
- w_up: bfloat16 [4, 1024, 4096], P('section'), may hold values from -0.1875 to 0.1875
- w_down: bfloat16 [4, 4096, 1024], P('section'), may hold values from -0.09375 to 0.09375
- cotangent: bfloat16 [2, 4096, 1024], P(None, 'dp'), may hold values from -6 to 6
Outputs:
- layer_outputs: bfloat16 [4, 2, 4096, 1024], P('section', None, 'dp')
- input_grads: bfloat16 [4, 2, 4096, 1024], P('section', None, 'dp')
- grad_gain_attn: float32 [4, 1024], P('section', 'dp')
- grad_query: float32 [4, 1024, 1024], P('section', 'dp')
- grad_key: float32 [4, 1024, 128], P('section', 'dp')
- grad_value: float32 [4, 1024, 128], P('section', 'dp')
- grad_out: float32 [4, 1024, 1024], P('section', 'dp')
- grad_gain_ffn: float32 [4, 1024], P('section', 'dp')
- grad_up: float32 [4, 1024, 4096], P('section', 'dp')
- grad_down: float32 [4, 4096, 1024], P('section', 'dp')
The draws below stay inside these ranges and needn't reach their ends.
Inputs may be any that keep to these rules, and one draw needn't show every extreme that they name: The 16 lengths of a row sum to 512; the last counts the padding positions at the row's end.
All inputs are finite; a program needn't handle non-finite values.
Results may differ from the reference program's by a relative error of at most 0.029.
Values may be sent and summed in bfloat16 or wider, within the bound.
No kernel may reach another device: no remote copies, remote signals or barrier semaphores. Data moves between devices by JAX's collectives and lax.ppermute only.
A program may use at most 384 MiB of HBM per device.

```python
import math
import jax
import jax.numpy as jnp
import numpy as np
from jax import lax

D = 1024
HEADS = 8
HD = 128
FF = 4096
ROW = 512
SEQS = 16
MB = 2
LAYERS = 4
ROWS_MB = 8
TOKENS_MB = 4096


def level_of(key, shape, pieces, least, top_value):
    def one(dim, blocks):
        draws = jax.random.uniform(jax.random.fold_in(jax.random.fold_in(key, 6), dim), (blocks,), jnp.float32, least / len(pieces), top_value / len(pieces))
        return jnp.repeat(jnp.exp(draws), shape[dim] // blocks).reshape((-1,) + (1,) * (len(shape) - dim - 1))

    level = one(*pieces[0])
    for cut in pieces[1:]:
        level = level * one(*cut)
    return level


def split_up(number_of, total, most, lean):
    portions = [(1 << 20) // math.isqrt(rank ** lean) + 1 for rank in range(2, number_of + 1)]
    rest, counts = total - most - (number_of - 1), [1] * (number_of - 1)
    while rest > 0:
        movable = [i for i in range(number_of - 1) if counts[i] < most]
        mass, budget = sum([portions[i] for i in movable]), rest
        for i in movable:
            more = min(most - counts[i], max(1, budget * portions[i] // mass), rest)
            counts[i] = counts[i] + more
            rest = rest - more
    return np.array([most] + counts)


def ragged_sizes(key, number_of, total, limit, lean):
    if number_of == 2:
        one = jax.random.randint(key, (), max(1, total - limit), min(limit, total - 1) + 1)
        return jnp.stack([one, total - one])
    tallies = jnp.asarray(split_up(number_of, total, limit, lean), jnp.int32)
    twos = (number_of - 1) // 2
    source_of, receiver = tallies[1:1 + 2 * twos:2], tallies[2:2 + 2 * twos:2]
    room = jnp.minimum(source_of - 1, limit - receiver)
    shifted = jax.random.randint(jax.random.fold_in(key, 1), (twos,), 0, 1 << 20) % (room + 1)
    tallies = tallies.at[1:1 + 2 * twos:2].set(source_of - shifted).at[2:2 + 2 * twos:2].set(receiver + shifted)
    return tallies[jax.random.permutation(jax.random.fold_in(key, 2), number_of)]


def centred(key, dims, width, reach, split=(), kind=jnp.bfloat16):
    factor_of = level_of(key, dims, split, -0.22, 0.18) if split else 1.0
    entries = jax.random.normal(key, dims, jnp.float32) * width * factor_of
    return jnp.minimum(jnp.maximum(entries, -reach), reach).astype(kind)


def setup_inputs(seed: int = 0) -> dict:
    arg_keys = jax.random.split(jax.random.key(seed), 12)
    return {
        "tokens": centred(arg_keys[0], (MB, TOKENS_MB, D), 1.0, 6.0, ((1, 8),)),
        "lengths": jax.vmap(lambda own: ragged_sizes(own, SEQS, ROW, ROW // 2, 2))(jax.random.split(arg_keys[1], MB * ROWS_MB)).reshape((MB, ROWS_MB, SEQS)).astype(jnp.int32),
        "gain_attn": jnp.clip(1.0 + 0.18 * jax.random.normal(arg_keys[2], (LAYERS, D), jnp.float32), 0.099609375, 1.8984375).astype(jnp.bfloat16),
        "w_query": centred(arg_keys[3], (LAYERS, D, HEADS * HD), D ** -0.5, 0.1875, ((0, 4),)),
        "w_key": centred(arg_keys[4], (LAYERS, D, HD), D ** -0.5, 0.1875, ((0, 4),)),
        "w_value": centred(arg_keys[5], (LAYERS, D, HD), D ** -0.5, 0.1875, ((0, 4),)),
        "w_out": centred(arg_keys[6], (LAYERS, HEADS * HD, D), (HEADS * HD // 8) ** -0.5, 0.5, ((0, 4),)),
        "gain_ffn": jnp.clip(1.0 + 0.18 * jax.random.normal(arg_keys[7], (LAYERS, D), jnp.float32), 0.099609375, 1.8984375).astype(jnp.bfloat16),
        "w_up": centred(arg_keys[8], (LAYERS, D, FF), D ** -0.5, 0.1875, ((0, 4),)),
        "w_down": centred(arg_keys[9], (LAYERS, FF, D), FF ** -0.5, 0.09375, ((0, 4),)),
        "cotangent": centred(arg_keys[10], (MB, TOKENS_MB, D), 1.0, 6.0, ((1, 8),)),
    }


NORM_EPS = 1e-06
NEG_BIG = -1e+30
TOP_PRECISION = lax.Precision.HIGHEST

@jax.custom_vjp
def low(v):
    return lax.optimization_barrier(v.astype(jnp.bfloat16)).astype(jnp.float32)

@jax.custom_vjp
def low_back(v):
    return v

def low_keep(v):
    return (low(v), None)

def low_pass(kept, grad):
    return (grad,)

def back_keep(v):
    return (v, None)

def back_low(kept, grad):
    return (low(grad),)
low.defvjp(low_keep, low_pass)
low_back.defvjp(back_keep, back_low)

def both_ways(tensor):
    return low_back(low(tensor))

def rms_norm(tensor, gain):
    return tensor * lax.rsqrt(lax.optimization_barrier(jnp.mean(tensor * tensor, axis=-1, keepdims=True)) + NORM_EPS) * gain

def segment_mask(lengths_row):
    seq_ends = jnp.cumsum(lengths_row, dtype=jnp.int32)
    position = jnp.arange(ROW, dtype=jnp.int32)
    segment = lax.optimization_barrier(jnp.sum((position[:, None] >= seq_ends[None, :]).astype(jnp.int32), axis=1))
    same_seq = segment[:, None] == segment[None, :]
    causal = position[None, :] <= position[:, None]
    own_pos = position[None, :] == position[:, None]
    return same_seq & causal & ((segment[:, None] < SEQS - 1) | own_pos)

def attend_row(operands):
    query_heads, key_rows, value_rows, allowed = operands
    scores = jnp.einsum('qhe,ke->hqk', query_heads, key_rows, precision=TOP_PRECISION) * HD ** (-0.5)
    scores = low_back(scores)
    attn_probs = low(jax.nn.softmax(jnp.where(allowed[None], scores, NEG_BIG), axis=-1))
    return jnp.einsum('hqk,ke->qhe', attn_probs, value_rows, precision=TOP_PRECISION)

def layer_ref(source, params, allowed_rows):
    gain_attn, w_query, w_key, w_value, w_out, gain_ffn, w_up, w_down = params
    group = source.shape[0]
    normed_attn = low(rms_norm(source, gain_attn))
    queries = both_ways(jnp.einsum('rtd,dc->rtc', normed_attn, w_query, precision=TOP_PRECISION))
    key_rows = both_ways(jnp.einsum('rtd,dc->rtc', normed_attn, w_key, precision=TOP_PRECISION))
    value_rows = both_ways(jnp.einsum('rtd,dc->rtc', normed_attn, w_value, precision=TOP_PRECISION))
    mixed_heads = lax.map(jax.checkpoint(attend_row), (queries.reshape(group, ROW, HEADS, HD), key_rows, value_rows, allowed_rows))
    mixed_heads = both_ways(mixed_heads.reshape(group, ROW, HEADS * HD))
    middle = source + low_back(jnp.einsum('rtc,cd->rtd', mixed_heads, w_out, precision=TOP_PRECISION))
    normed_ffn = low(rms_norm(middle, gain_ffn))
    pre_act = low_back(jnp.einsum('rtd,df->rtf', normed_ffn, w_up, precision=TOP_PRECISION))
    activated = low(jax.nn.gelu(pre_act, approximate=False))
    return middle + low_back(jnp.einsum('rtf,fd->rtd', activated, w_down, precision=TOP_PRECISION))

def run_stack(params, perturb, block_in, allowed_rows):
    current = block_in
    layer_outs = []
    for layer_pos in range(LAYERS):
        layer_in = low_back(current + perturb[layer_pos])
        layer_params = tuple((param[layer_pos] for param in params))
        current = low(layer_ref(layer_in, layer_params, allowed_rows))
        layer_outs.append(current)
    return jnp.stack(layer_outs)

def reference(tokens, lengths, gain_attn, w_query, w_key, w_value, w_out, gain_ffn, w_up, w_down, cotangent):
    params = tuple((param.astype(jnp.float32) for param in (gain_attn, w_query, w_key, w_value, w_out, gain_ffn, w_up, w_down)))
    row_total = MB * ROWS_MB
    rows_grp = math.gcd(row_total, max(1, 4096 // ROW))
    groups = row_total // rows_grp
    token_rows = tokens.astype(jnp.float32).reshape(groups, rows_grp, ROW, D)
    cot_rows = cotangent.astype(jnp.float32).reshape(groups, rows_grp, ROW, D)
    length_rows = lengths.reshape(groups, rows_grp, SEQS)

    def group_step(totals, inputs):
        block_in, block_cot, block_len = inputs
        allowed_rows = jax.vmap(segment_mask)(block_len)
        perturb = jnp.zeros((LAYERS, rows_grp, ROW, D), jnp.float32)

        def stack_of(param_set, shift_set):
            return run_stack(param_set, shift_set, block_in, allowed_rows)
        layer_outs, pullback = jax.vjp(stack_of, params, perturb)
        cotangents = jnp.zeros_like(layer_outs).at[LAYERS - 1].set(block_cot)
        grad_params, grad_perturb = pullback(cotangents)
        totals = tuple((running + added for running, added in zip(totals, grad_params)))
        return (totals, (layer_outs, grad_perturb))
    start_totals = tuple((jnp.zeros(param.shape, jnp.float32) for param in params))
    totals, (layer_outs, grad_perturb) = lax.scan(group_step, start_totals, (token_rows, cot_rows, length_rows))
    layer_outputs = jnp.transpose(layer_outs, (1, 0, 2, 3, 4)).reshape(LAYERS, MB, ROWS_MB * ROW, D).astype(jnp.bfloat16)
    input_grads = jnp.transpose(grad_perturb, (1, 0, 2, 3, 4)).reshape(LAYERS, MB, ROWS_MB * ROW, D).astype(jnp.bfloat16)
    return (layer_outputs, input_grads, totals[0], totals[1], totals[2], totals[3], totals[4], totals[5], totals[6], totals[7])
```

```python
import functools

import jax
import jax.numpy as jnp
from jax import lax
from jax.experimental import pallas as pl
from jax.experimental.pallas import tpu as pltpu
from jax.sharding import PartitionSpec as P

NORM_EPS = 1e-06
MASKED = -1e30
LOG2E = 1.4426950408889634
FWD_ROWS = 128
BWD_ROWS = 256
FFN_TILE = 1024
SKEW = 2
MIB = 1 << 20

BF16 = jnp.bfloat16
F32 = jnp.float32


def in_hbm(array):
    return pltpu.with_memory_space_constraint(array, pltpu.HBM)


def in_vmem(array):
    return pltpu.with_memory_space_constraint(array, pltpu.VMEM)


def dot(left, right):
    return jnp.dot(left, right, preferred_element_type=F32)


def dot_t(left, right):
    return lax.dot_general(left, right, (((1,), (1,)), ((), ())), preferred_element_type=F32)


def inverse_rms(rows):
    return lax.rsqrt(jnp.mean(rows * rows, axis=-1, keepdims=True) + NORM_EPS)


def gelu_parts(u):
    t = pl.reciprocal(1.0 + jnp.abs(u) * 0.23164190, approx=True)
    bell = jnp.exp2(u * u * (-0.5 * LOG2E))
    poly = t * (0.127414796 + t * (-0.142248368 + t * (0.7107068705 + t * (-0.7265760135 + t * 0.5307027145))))
    tail = poly * bell
    cdf = jnp.where(u >= 0, 1.0 - tail, tail)
    return u * cdf, cdf + u * bell * 0.3989422804014327


def position_bias(start_col, first_row, rows, length):
    own = first_row + lax.broadcasted_iota(jnp.int32, (rows, length), 0)
    other = lax.broadcasted_iota(jnp.int32, (rows, length), 1)
    return jnp.where((other >= start_col) & (other <= own), 0.0, MASKED)


def forward_kernel(
    geometry, meta, starts, tokens, incoming, gain_attn, w_query, w_kv, w_out, gain_ffn, w_up, w_down,
    *refs,
):
    rows, row_len, heads, size = geometry
    saved = refs[len(FWD_SAVED):2 * len(FWD_SAVED) + 1]
    out, hs, n1s, qs, ks, vs, kts, vts, os_, mids, n2s, acts, slopes, lses, outs = saved
    (h_v, n1_v, q_v, k_v, v_v, kt_v, vt_v, o_v, mid_v, n2_v, act_v, slope_v, lse_v, out_v, bias_v, sems) = (
        refs[2 * len(FWD_SAVED) + 1:]
    )
    parts = row_len // rows
    active, chunk, first = meta[0], meta[1], meta[2]
    width = heads * size
    scale = size**-0.5 * LOG2E

    @pl.when(active == 1)
    def _():
        row = chunk // parts
        place = chunk % parts
        at = pl.ds(pl.multiple_of(chunk * rows, rows), rows)
        within = pl.ds(pl.multiple_of(place * rows, rows), rows)
        whole = pl.ds(pl.multiple_of(row * row_len, row_len), row_len)

        @pl.when(first == 1)
        def _():
            pltpu.make_async_copy(tokens.at[at], h_v, sems.at[0]).start()

        @pl.when(first == 0)
        def _():
            pltpu.make_async_copy(incoming, h_v, sems.at[0]).start()

        load_v = pltpu.make_async_copy(vs.at[whole], v_v, sems.at[1])
        load_kt = pltpu.make_async_copy(kts.at[row], kt_v, sems.at[2])
        load_v.start()
        load_kt.start()
        pending = []

        def keep(source, target, slot):
            copy = pltpu.make_async_copy(source, target, sems.at[slot])
            copy.start()
            pending.append(copy)

        start_col = starts[at, :]
        for step in range(parts):
            @pl.when(place == step)
            def _():
                bias_v[:, : (step + 1) * rows] = position_bias(start_col, step * rows, rows, (step + 1) * rows)

        pltpu.make_async_copy(incoming, h_v, sems.at[0]).wait()
        h = h_v[...].astype(F32)
        n1 = (h * inverse_rms(h) * gain_attn[...].astype(F32)).astype(BF16)
        n1_v[...] = n1
        keep(h_v, hs.at[at], 3)
        keep(n1_v, n1s.at[at], 4)
        kv = dot(n1, w_kv[...]).astype(BF16)
        q_v[...] = dot(n1, w_query[...]).astype(BF16)
        k_v[...] = kv[:, :size]
        keep(k_v, ks.at[at], 5)
        keep(q_v, qs.at[at], 6)
        load_v.wait()
        load_kt.wait()
        v_v[within, :] = kv[:, size:]
        kt_v[:, within] = kv[:, :size].T
        vt_v[...] = kv[:, size:].T
        keep(v_v.at[within], vs.at[at], 7)
        keep(kt_v.at[:, within], kts.at[row, :, within], 8)
        keep(vt_v, vts.at[row, :, within], 9)

        def attend(length):
            lane = lax.broadcasted_iota(jnp.int32, (rows, size), 1)
            stats = jnp.zeros((rows, size), F32)
            for head in range(heads):
                cols = slice(head * size, (head + 1) * size)
                scores = dot(q_v[:, cols], kt_v[:, :length]) * scale + bias_v[:, :length]
                top = jnp.max(scores, axis=1, keepdims=True)
                weights = jnp.exp2(scores - top)
                total = jnp.sum(weights, axis=1, keepdims=True)
                mixed = dot(weights.astype(BF16), v_v[:length, :]) * (1.0 / total)
                o_v[:, cols] = mixed.astype(BF16)
                stats = jnp.where(lane == head, top + jnp.log2(total), stats)
            lse_v[...] = stats

        for step in range(parts):
            pl.when(place == step)(functools.partial(attend, (step + 1) * rows))

        keep(lse_v, lses.at[at], 10)
        keep(o_v, os_.at[at], 11)
        mid = h + dot(o_v[...], w_out[...])
        mid_v[...] = mid
        keep(mid_v, mids.at[at], 12)
        n2 = (mid * inverse_rms(mid) * gain_ffn[...].astype(F32)).astype(BF16)
        n2_v[...] = n2
        keep(n2_v, n2s.at[at], 13)
        ffn = w_up.shape[1]
        tile = min(FFN_TILE, ffn)
        total = mid
        for f in range(ffn // tile):
            cols = slice(f * tile, (f + 1) * tile)
            act, slope = gelu_parts(dot(n2, w_up[:, cols]))
            act = act.astype(BF16)
            act_v[:, cols] = act
            slope_v[:, cols] = slope.astype(BF16)
            total = total + dot(act, w_down[cols, :])
        keep(act_v, acts.at[at], 14)
        keep(slope_v, slopes.at[at], 15)
        result = total.astype(BF16)
        out[...] = result
        out_v[...] = result
        keep(out_v, outs.at[at], 16)
        for copy in pending:
            copy.wait()


FWD_SAVED = ("hs", "n1s", "qs", "ks", "vs", "kts", "vts", "os", "mids", "n2s", "acts", "slopes", "lses", "outs")


def forward_chunk(geometry, meta, starts, tokens, incoming, weights, saved):
    rows, row_len, heads, size = geometry
    width = tokens.shape[1]
    ffn = weights[5].shape[1]
    vmem = pl.BlockSpec(memory_space=pltpu.VMEM)
    anywhere = pl.BlockSpec(memory_space=pltpu.HBM)
    lead = 5 + len(weights)
    flops = 2 * rows * (2 * width * heads * size + 2 * width * size + 2 * width * ffn + row_len * heads * size)
    return pl.pallas_call(
        functools.partial(forward_kernel, geometry),
        out_shape=[jax.ShapeDtypeStruct((rows, width), BF16)]
        + [pltpu.HBM(array.shape, array.dtype) for array in saved],
        in_specs=[pl.BlockSpec(memory_space=pltpu.SMEM), vmem, anywhere, anywhere]
        + [vmem] * len(weights) + [anywhere] * len(saved),
        out_specs=[vmem] + [anywhere] * len(saved),
        input_output_aliases={4 + len(weights) + i: 1 + i for i in range(len(saved))},
        scratch_shapes=[
            pltpu.VMEM((rows, width), BF16),
            pltpu.VMEM((rows, width), BF16),
            pltpu.VMEM((rows, heads * size), BF16),
            pltpu.VMEM((rows, size), BF16),
            pltpu.VMEM((row_len, size), BF16),
            pltpu.VMEM((size, row_len), BF16),
            pltpu.VMEM((size, rows), BF16),
            pltpu.VMEM((rows, heads * size), BF16),
            pltpu.VMEM((rows, width), F32),
            pltpu.VMEM((rows, width), BF16),
            pltpu.VMEM((rows, ffn), BF16),
            pltpu.VMEM((rows, ffn), BF16),
            pltpu.VMEM((rows, size), F32),
            pltpu.VMEM((rows, width), BF16),
            pltpu.VMEM((rows, row_len), F32),
            pltpu.SemaphoreType.DMA((17,)),
        ],
        compiler_params=pltpu.CompilerParams(vmem_limit_bytes=16 * MIB),
        cost_estimate=pl.CostEstimate(flops=flops, bytes_accessed=8 * MIB, transcendentals=0),
        name="forward_chunk",
    )(meta, starts, in_hbm(tokens), incoming, *map(in_vmem, weights), *saved)


BWD_SAVED = ("gbs", "dus", "gms", "dqs", "dkvs", "igs", "gains", "carry")


def norm_backward(rows, gain, upstream):
    inverse = inverse_rms(rows)
    unit = rows * inverse
    steered = upstream * gain
    grad = inverse * (steered - unit * jnp.mean(steered * unit, axis=-1, keepdims=True))
    return grad, jnp.sum(upstream * unit, axis=0, keepdims=True)


def backward_kernel(
    geometry, meta, starts, cotangent, incoming, hs, qs, ks, kts, vts, mids, slopes, lses,
    gain_attn, w_query, w_kv, w_out, gain_ffn, w_up, w_down, *refs,
):
    rows, row_len, heads, size = geometry
    count = len(BWD_SAVED)
    out, gbs, dus, gms, dqs, dkvs, igs, gains, carry = refs[count:2 * count + 1]
    (g_v, h_v, q_v, k_v, kt_v, vt_v, mid_v, slope_v, lse_v, du_v, gm_v, do_v, dq_v, dkv_v, ig_v, gain_v, carry_v,
     bias_v, p_v, ds_v, qt_v, dot_v, sems) = refs[2 * count + 1:]
    parts = row_len // rows
    active, chunk, first = meta[0], meta[1], meta[2]
    scale = size**-0.5

    @pl.when(active == 1)
    def _():
        row = chunk // parts
        place = chunk % parts
        at = pl.ds(pl.multiple_of(chunk * rows, rows), rows)
        within = pl.ds(pl.multiple_of(place * rows, rows), rows)
        whole = pl.ds(pl.multiple_of(row * row_len, row_len), row_len)

        @pl.when(first == 1)
        def _():
            pltpu.make_async_copy(cotangent.at[at], g_v, sems.at[0]).start()

        @pl.when(first == 0)
        def _():
            pltpu.make_async_copy(incoming, g_v, sems.at[0]).start()

        loads = [
            pltpu.make_async_copy(source, target, sems.at[1 + i])
            for i, (source, target) in enumerate((
                (slopes.at[at], slope_v),
                (mids.at[at], mid_v),
                (qs.at[at], q_v),
                (lses.at[at], lse_v),
                (kts.at[row], kt_v),
                (vts.at[row], vt_v),
                (ks.at[whole], k_v),
                (carry, carry_v),
                (hs.at[at], h_v),
            ))
        ]
        for load in loads:
            load.start()
        pending = []

        def keep(source, target, slot):
            copy = pltpu.make_async_copy(source, target, sems.at[slot])
            copy.start()
            pending.append(copy)

        start_col = starts[at, :]
        for step in range(parts):
            @pl.when(place == step)
            def _():
                bias_v[:, : (step + 1) * rows] = position_bias(start_col, step * rows, rows, (step + 1) * rows)

        pltpu.make_async_copy(incoming, g_v, sems.at[0]).wait()
        g = g_v[...]
        keep(g_v, gbs.at[at], 10)
        loads[0].wait()
        ffn = w_up.shape[1]
        tile = min(FFN_TILE, ffn)
        dn2 = None
        for f in range(ffn // tile):
            cols = slice(f * tile, (f + 1) * tile)
            du = (slope_v[:, cols].astype(F32) * dot_t(g, w_down[cols, :])).astype(BF16)
            du_v[:, cols] = du
            part = dot_t(du, w_up[:, cols])
            dn2 = part if dn2 is None else dn2 + part
        keep(du_v, dus.at[at], 11)
        loads[1].wait()
        dv, dgain_ffn = norm_backward(mid_v[...], gain_ffn[...].astype(F32), dn2)
        dmid = g.astype(F32) + dv
        mid_v[...] = dmid
        gm = dmid.astype(BF16)
        gm_v[...] = gm
        keep(gm_v, gms.at[at], 12)
        do_v[...] = dot_t(gm, w_out[...]).astype(BF16)
        for load in loads[2:8]:
            load.wait()

        def attend(length, last):
            for head in range(heads):
                cols = slice(head * size, (head + 1) * size)
                span = slice(head * rows, (head + 1) * rows)
                q_h = q_v[:, cols]
                do_h = do_v[:, cols]
                qt_v[:, span] = q_h.T
                dot_v[:, span] = do_h.T
                scores = dot(q_h, kt_v[:, :length]) * (scale * LOG2E) + bias_v[:, :length]
                probs = jnp.exp2(scores - lse_v[:, head:head + 1])
                p_v[span, :length] = probs.astype(BF16)
                dprobs = dot(do_h, vt_v[:, :length])
                mean = jnp.sum(probs * dprobs, axis=1, keepdims=True)
                dscores = (probs * (dprobs - mean)).astype(BF16)
                ds_v[span, :length] = dscores
                dq_v[:, cols] = (dot(dscores, k_v[:length, :]) * scale).astype(BF16)
            dkt = dot(qt_v[...], ds_v[:, :length])
            dvt = dot(dot_v[...], p_v[:, :length])
            if not last:
                dkt = dkt + carry_v[:size, :length]
                dvt = dvt + carry_v[size:, :length]
            if length > rows:
                carry_v[:size, :length - rows] = dkt[:, :length - rows]
                carry_v[size:, :length - rows] = dvt[:, :length - rows]
            dkv_v[:, :size] = (dkt[:, length - rows:].T * scale).astype(BF16)
            dkv_v[:, size:] = dvt[:, length - rows:].T.astype(BF16)

        for step in range(parts):
            pl.when(place == step)(functools.partial(attend, (step + 1) * rows, step == parts - 1))

        keep(carry_v, carry, 13)
        keep(dq_v, dqs.at[at], 14)
        keep(dkv_v, dkvs.at[at], 15)
        dn1 = dot_t(dq_v[...], w_query[...]) + dot_t(dkv_v[...], w_kv[...])
        loads[8].wait()
        dv, dgain_attn = norm_backward(h_v[...].astype(F32), gain_attn[...].astype(F32), dn1)
        result = (mid_v[...] + dv).astype(BF16)
        out[...] = result
        ig_v[...] = result
        keep(ig_v, igs.at[at], 16)
        gain_v[...] = jnp.concatenate([dgain_attn, dgain_ffn, jnp.zeros((6, dgain_attn.shape[1]), F32)], axis=0)
        keep(gain_v, gains.at[chunk], 17)
        for copy in pending:
            copy.wait()


def backward_chunk(geometry, meta, starts, cotangent, incoming, kept, weights, saved):
    rows, row_len, heads, size = geometry
    width = cotangent.shape[1]
    ffn = weights[5].shape[1]
    vmem = pl.BlockSpec(memory_space=pltpu.VMEM)
    anywhere = pl.BlockSpec(memory_space=pltpu.HBM)
    lead = 4 + len(kept) + len(weights)
    flops = 2 * rows * (2 * width * heads * size + 2 * width * size + 2 * width * ffn + 3 * row_len * heads * size)
    return pl.pallas_call(
        functools.partial(backward_kernel, geometry),
        out_shape=[jax.ShapeDtypeStruct((rows, width), BF16)]
        + [pltpu.HBM(array.shape, array.dtype) for array in saved],
        in_specs=[pl.BlockSpec(memory_space=pltpu.SMEM), vmem, anywhere, anywhere]
        + [anywhere] * len(kept) + [vmem] * len(weights) + [anywhere] * len(saved),
        out_specs=[vmem] + [anywhere] * len(saved),
        input_output_aliases={lead + i: 1 + i for i in range(len(saved))},
        scratch_shapes=[
            pltpu.VMEM((rows, width), BF16),
            pltpu.VMEM((rows, width), BF16),
            pltpu.VMEM((rows, heads * size), BF16),
            pltpu.VMEM((row_len, size), BF16),
            pltpu.VMEM((size, row_len), BF16),
            pltpu.VMEM((size, row_len), BF16),
            pltpu.VMEM((rows, width), F32),
            pltpu.VMEM((rows, ffn), BF16),
            pltpu.VMEM((rows, size), F32),
            pltpu.VMEM((rows, ffn), BF16),
            pltpu.VMEM((rows, width), BF16),
            pltpu.VMEM((rows, heads * size), BF16),
            pltpu.VMEM((rows, heads * size), BF16),
            pltpu.VMEM((rows, 2 * size), BF16),
            pltpu.VMEM((rows, width), BF16),
            pltpu.VMEM((8, width), F32),
            pltpu.VMEM((2 * size, row_len), F32),
            pltpu.VMEM((rows, row_len), F32),
            pltpu.VMEM((heads * rows, row_len), BF16),
            pltpu.VMEM((heads * rows, row_len), BF16),
            pltpu.VMEM((size, heads * rows), BF16),
            pltpu.VMEM((size, heads * rows), BF16),
            pltpu.SemaphoreType.DMA((18,)),
        ],
        compiler_params=pltpu.CompilerParams(vmem_limit_bytes=30 * MIB),
        cost_estimate=pl.CostEstimate(flops=flops, bytes_accessed=8 * MIB, transcendentals=0),
        name="backward_chunk",
    )(meta, starts, in_hbm(cotangent), incoming, *map(in_hbm, kept), *map(in_vmem, weights), *saved)


def unwritten(shapes):
    return pl.pallas_call(
        lambda *refs: None,
        out_shape=shapes,
        out_specs=[pl.BlockSpec(memory_space=pltpu.HBM)] * len(shapes),
        name="unwritten",
    )()


def segment_starts(lengths, row_len):
    count = lengths.shape[1]
    upto = jnp.arange(count)[:, None] <= jnp.arange(count)[None, :]
    ends = jnp.sum(jnp.where(upto[None], lengths[:, :, None], 0), axis=1)
    position = jnp.arange(row_len, dtype=jnp.int32)
    over = ends[:, None, :] <= position[None, :, None]
    start = jnp.sum(jnp.where(over, lengths[:, None, :], 0), axis=2)
    segment = jnp.sum(over.astype(jnp.int32), axis=2)
    return jnp.where(segment < count - 1, start, position[None]).astype(jnp.int32)


def contract_rows(left, right):
    return lax.dot_general(left, right, (((0,), (0,)), ((), ())), preferred_element_type=F32)


def body(
    tokens, lengths, gain_attn, w_query, w_key, w_value, w_out, gain_ffn, w_up, w_down, cotangent
):
    micro, row_len, width = tokens.shape
    size = w_key.shape[2]
    heads = w_query.shape[2] // size
    ffn = w_up.shape[2]
    count = micro * row_len
    sections = lax.axis_size("section")
    place = lax.axis_index("section")
    weights = (
        gain_attn, w_query[0], jnp.concatenate([w_key[0], w_value[0]], axis=1), w_out[0],
        gain_ffn, w_up[0], w_down[0],
    )
    token_rows = tokens.reshape(count, width)
    cotangent_rows = cotangent.reshape(count, width)
    starts = segment_starts(lengths[:, 0], row_len).reshape(count, 1)

    def empty(*shape, dtype=BF16):
        return pltpu.HBM(shape, dtype)

    def meta_of(tick, chunks, rank, order):
        step = tick - SKEW * rank
        active = (step >= 0) & (step < chunks)
        chunk = order(jnp.clip(step, 0, chunks - 1))
        return jnp.stack([active.astype(jnp.int32), chunk.astype(jnp.int32), (rank == 0).astype(jnp.int32)])

    def hop(block, tick, chunks, rank_of, shift):
        route = [
            (s, s + shift)
            for s in range(sections)
            if 0 <= s + shift < sections and 0 <= tick - SKEW * rank_of(s) < chunks
        ]
        return lax.ppermute(block, "section", route) if route else None

    fwd_geometry = (FWD_ROWS, row_len, heads, size)
    fwd_chunks = count // FWD_ROWS
    saved = [
        empty(count, width), empty(count, width), empty(count, heads * size), empty(count, size), empty(count, size),
        empty(micro, size, row_len), empty(micro, size, row_len), empty(count, heads * size),
        empty(count, width, dtype=F32), empty(count, width), empty(count, ffn), empty(count, ffn),
        empty(count, size, dtype=F32), empty(count, width),
    ]
    saved = unwritten(saved)
    received = {}
    nothing = jnp.zeros((FWD_ROWS, width), BF16)
    for tick in range(fwd_chunks + SKEW * (sections - 1)):
        meta = meta_of(tick, fwd_chunks, place, lambda step: step)
        incoming = received.pop(tick - SKEW, None)
        out, *saved = forward_chunk(
            fwd_geometry, meta, starts, token_rows, nothing if incoming is None else incoming, weights, saved
        )
        received[tick] = hop(out, tick, fwd_chunks, lambda s: s, 1)

    kept = dict(zip(FWD_SAVED, saved))
    layer_outs = kept["outs"]
    needed = [kept[name] for name in ("hs", "qs", "ks", "kts", "vts", "mids", "slopes", "lses")]
    bwd_geometry = (BWD_ROWS, row_len, heads, size)
    bwd_chunks = count // BWD_ROWS
    parts = row_len // BWD_ROWS
    saved = [
        empty(count, width), empty(count, ffn), empty(count, width), empty(count, heads * size),
        empty(count, 2 * size), empty(count, width), empty(bwd_chunks, 8, width, dtype=F32),
        empty(2 * size, row_len, dtype=F32),
    ]
    saved = unwritten(saved)
    received = {}
    nothing = jnp.zeros((BWD_ROWS, width), BF16)
    for tick in range(bwd_chunks + SKEW * (sections - 1)):
        meta = meta_of(
            tick, bwd_chunks, sections - 1 - place, lambda step: step // parts * parts + parts - 1 - step % parts
        )
        incoming = received.pop(tick - SKEW, None)
        out, *saved = backward_chunk(
            bwd_geometry, meta, starts, cotangent_rows, nothing if incoming is None else incoming, needed, weights,
            saved,
        )
        received[tick] = hop(out, tick, bwd_chunks, lambda s: sections - 1 - s, -1)
    done = dict(zip(BWD_SAVED, saved))

    gains = jnp.sum(done["gains"], axis=0)
    dkv = done["dkvs"]
    grads = (
        gains[0],
        contract_rows(kept["n1s"], done["dqs"]),
        contract_rows(kept["n1s"], dkv[:, :size]),
        contract_rows(kept["n1s"], dkv[:, size:]),
        contract_rows(kept["os"], done["gms"]),
        gains[1],
        contract_rows(kept["n2s"], done["dus"]),
        contract_rows(kept["acts"], done["gbs"]),
    )
    shares = tuple(
        lax.psum_scatter(grad.astype(BF16), "dp", scatter_dimension=0, tiled=True).astype(F32) for grad in grads
    )
    shape = (1, micro, row_len, width)
    return (layer_outs.reshape(shape), done["igs"].reshape(shape)) + tuple(share[None] for share in shares)


def solution(mesh):
    return jax.shard_map(
        body,
        mesh=mesh,
        in_specs=(
            P(None, "dp", None),
            P(None, "dp", None),
            P("section", None),
            P("section", None, None),
            P("section", None, None),
            P("section", None, None),
            P("section", None, None),
            P("section", None),
            P("section", None, None),
            P("section", None, None),
            P(None, "dp", None),
        ),
        out_specs=(
            P("section", None, "dp", None),
            P("section", None, "dp", None),
            P("section", "dp"),
            P("section", "dp", None),
            P("section", "dp", None),
            P("section", "dp", None),
            P("section", "dp", None),
            P("section", "dp"),
            P("section", "dp", None),
            P("section", "dp", None),
        ),
        check_vma=False,
    )
```

```python
import functools

import jax
import jax.numpy as jnp
from jax import lax
from jax.experimental import pallas as pl
from jax.experimental.pallas import tpu as pltpu
from jax.sharding import PartitionSpec as P

NORM_EPS = 1e-06
MASKED = -1e30
LOG2E = 1.4426950408889634
FWD_ROWS = 128
BWD_ROWS = 256
FFN_TILE = 1024
SKEW = 2
FWD_HEADS = 4
BWD_HEADS = 2
SIDE_TILE = 512
MIB = 1 << 20

BF16 = jnp.bfloat16
F32 = jnp.float32


def in_hbm(array):
    return pltpu.with_memory_space_constraint(array, pltpu.HBM)


def in_vmem(array):
    return pltpu.with_memory_space_constraint(array, pltpu.VMEM)


def dot(left, right):
    return jnp.dot(left, right, preferred_element_type=F32)


def dot_t(left, right):
    return lax.dot_general(left, right, (((1,), (1,)), ((), ())), preferred_element_type=F32)


def inverse_rms(rows):
    return lax.rsqrt(jnp.mean(rows * rows, axis=-1, keepdims=True) + NORM_EPS)


def gelu_parts(u):
    t = pl.reciprocal(1.0 + jnp.abs(u) * 0.23164190, approx=True)
    bell = jnp.exp2(u * u * (-0.5 * LOG2E))
    poly = t * (0.127414796 + t * (-0.142248368 + t * (0.7107068705 + t * (-0.7265760135 + t * 0.5307027145))))
    tail = poly * bell
    cdf = jnp.where(u >= 0, 1.0 - tail, tail)
    return u * cdf, cdf + u * bell * 0.3989422804014327


def position_bias(start_col, first_row, rows, length):
    own = first_row + lax.broadcasted_iota(jnp.int32, (rows, length), 0)
    other = lax.broadcasted_iota(jnp.int32, (rows, length), 1)
    return jnp.where((other >= start_col) & (other <= own), 0.0, MASKED)


def forward_kernel(
    geometry, meta, starts, tokens, incoming, gain_attn, w_query, w_kv, w_out, gain_ffn, w_up, w_down,
    *refs,
):
    rows, row_len, heads, size = geometry
    saved = refs[len(FWD_SAVED):2 * len(FWD_SAVED) + 1]
    out, hs, n1s, qs, ks, vs, kts, vts, os_, mids, n2s, acts, slopes, lses, outs = saved
    (h_v, n1_v, q_v, k_v, v_v, kt_v, vt_v, o_v, mid_v, n2_v, act_v, slope_v, lse_v, out_v, bias_v, total_v, sems) = (
        refs[2 * len(FWD_SAVED) + 1:]
    )
    parts = row_len // rows
    active, chunk, first = meta[0], meta[1], meta[2]
    width = heads * size
    scale = size**-0.5 * LOG2E

    @pl.when(active == 1)
    def _():
        row = chunk // parts
        place = chunk % parts
        at = pl.ds(pl.multiple_of(chunk * rows, rows), rows)
        within = pl.ds(pl.multiple_of(place * rows, rows), rows)
        whole = pl.ds(pl.multiple_of(row * row_len, row_len), row_len)

        @pl.when(first == 1)
        def _():
            pltpu.make_async_copy(tokens.at[at], h_v, sems.at[0]).start()

        load_v = pltpu.make_async_copy(vs.at[whole], v_v, sems.at[1])
        load_kt = pltpu.make_async_copy(kts.at[row], kt_v, sems.at[2])
        load_v.start()
        load_kt.start()
        pending = []

        def keep(source, target, slot):
            copy = pltpu.make_async_copy(source, target, sems.at[slot])
            copy.start()
            pending.append(copy)

        start_col = starts[at, :]
        bias_v[...] = position_bias(start_col, place * rows, rows, row_len)

        @pl.when(first == 1)
        def _():
            pltpu.make_async_copy(tokens.at[at], h_v, sems.at[0]).wait()

        @pl.when(first == 0)
        def _():
            h_v[...] = incoming[...]

        h = h_v[...].astype(F32)
        n1 = (h * inverse_rms(h) * gain_attn[...].astype(F32)).astype(BF16)
        n1_v[...] = n1
        keep(h_v, hs.at[at], 3)
        keep(n1_v, n1s.at[at], 4)
        kv = dot(n1, w_kv[...]).astype(BF16)
        q_v[...] = dot(n1, w_query[...]).astype(BF16)
        k_v[...] = kv[:, :size]
        keep(k_v, ks.at[at], 5)
        keep(q_v, qs.at[at], 6)
        load_v.wait()
        load_kt.wait()
        known = place * rows
        v_v[...] = jnp.where(lax.broadcasted_iota(jnp.int32, v_v.shape, 0) < known, v_v[...], 0.0).astype(BF16)
        kt_v[...] = jnp.where(lax.broadcasted_iota(jnp.int32, kt_v.shape, 1) < known, kt_v[...], 0.0).astype(BF16)
        v_v[within, :] = kv[:, size:]
        kt_v[:, within] = kv[:, :size].T
        vt_v[...] = kv[:, size:].T
        keep(v_v.at[within], vs.at[at], 7)
        keep(kt_v.at[:, within], kts.at[row, :, within], 8)
        keep(vt_v, vts.at[row, :, within], 9)

        lse_v[...] = jnp.zeros((rows, size), F32)

        def attend(length):
            lane = lax.broadcasted_iota(jnp.int32, (rows, size), 1)

            def some_heads(step, carry):
                for head in [step * FWD_HEADS + i for i in range(FWD_HEADS)]:
                    cols = pl.ds(pl.multiple_of(head * size, size), size)
                    scores = dot(q_v[:, cols], kt_v[:, :length]) * scale + bias_v[:, :length]
                    top = jnp.max(scores, axis=1, keepdims=True)
                    weights = jnp.exp2(scores - top)
                    total = jnp.sum(weights, axis=1, keepdims=True)
                    mixed = dot(weights.astype(BF16), v_v[:length, :]) * (1.0 / total)
                    o_v[:, cols] = mixed.astype(BF16)
                    lse_v[...] = jnp.where(lane == head, top + jnp.log2(total), lse_v[...])
                return carry

            lax.fori_loop(0, heads // FWD_HEADS, some_heads, 0)

        cases = [row_len // 2, row_len] if parts > 2 else [rows * (i + 1) for i in range(parts)]
        low = 0
        for length in cases:
            pl.when((place >= low) & (place < length // rows))(functools.partial(attend, length))
            low = length // rows

        keep(lse_v, lses.at[at], 10)
        keep(o_v, os_.at[at], 11)
        mid = h + dot(o_v[...], w_out[...])
        mid_v[...] = mid
        keep(mid_v, mids.at[at], 12)
        n2 = (mid * inverse_rms(mid) * gain_ffn[...].astype(F32)).astype(BF16)
        n2_v[...] = n2
        keep(n2_v, n2s.at[at], 13)
        ffn = w_up.shape[1]
        tile = min(FFN_TILE, ffn)
        total_v[...] = mid


        def columns(f):
            return pl.ds(pl.multiple_of(f * tile, tile), tile)

        def rise(f):
            return dot(n2_v[...], w_up[:, columns(f)])

        def bend(f, u):
            act, slope = gelu_parts(u)
            act_v[:, columns(f)] = act.astype(BF16)
            slope_v[:, columns(f)] = slope.astype(BF16)
            pltpu.make_async_copy(act_v.at[:, columns(f)], acts.at[at, columns(f)], sems.at[14]).start()
            pltpu.make_async_copy(slope_v.at[:, columns(f)], slopes.at[at, columns(f)], sems.at[15]).start()

        def fall(f):
            return dot(act_v[:, columns(f)], w_down[columns(f), :])

        def both(f, carry):
            u = rise(f)
            part = fall(f - 1)
            bend(f, u)
            total_v[...] += part
            return carry

        bend(0, rise(0))
        lax.fori_loop(1, ffn // tile, both, 0)
        total_v[...] += fall(ffn // tile - 1)
        total = total_v[...]
        pending.append(pltpu.make_async_copy(act_v, acts.at[at], sems.at[14]))
        pending.append(pltpu.make_async_copy(slope_v, slopes.at[at], sems.at[15]))
        result = total.astype(BF16)
        out[...] = result
        out_v[...] = result
        keep(out_v, outs.at[at], 16)
        for copy in pending:
            copy.wait()


FWD_SAVED = ("hs", "n1s", "qs", "ks", "vs", "kts", "vts", "os", "mids", "n2s", "acts", "slopes", "lses", "outs")


def forward_chunk(geometry, meta, starts, tokens, incoming, weights, saved):
    rows, row_len, heads, size = geometry
    width = tokens.shape[1]
    ffn = weights[5].shape[1]
    vmem = pl.BlockSpec(memory_space=pltpu.VMEM)
    anywhere = pl.BlockSpec(memory_space=pltpu.HBM)
    lead = 5 + len(weights)
    flops = 2 * rows * (2 * width * heads * size + 2 * width * size + 2 * width * ffn + row_len * heads * size)
    return pl.pallas_call(
        functools.partial(forward_kernel, geometry),
        out_shape=[jax.ShapeDtypeStruct((rows, width), BF16)]
        + [pltpu.HBM(array.shape, array.dtype) for array in saved],
        in_specs=[pl.BlockSpec(memory_space=pltpu.SMEM), vmem, anywhere, vmem]
        + [vmem] * len(weights) + [anywhere] * len(saved),
        out_specs=[vmem] + [anywhere] * len(saved),
        input_output_aliases={4 + len(weights) + i: 1 + i for i in range(len(saved))},
        scratch_shapes=[
            pltpu.VMEM((rows, width), BF16),
            pltpu.VMEM((rows, width), BF16),
            pltpu.VMEM((rows, heads * size), BF16),
            pltpu.VMEM((rows, size), BF16),
            pltpu.VMEM((row_len, size), BF16),
            pltpu.VMEM((size, row_len), BF16),
            pltpu.VMEM((size, rows), BF16),
            pltpu.VMEM((rows, heads * size), BF16),
            pltpu.VMEM((rows, width), F32),
            pltpu.VMEM((rows, width), BF16),
            pltpu.VMEM((rows, ffn), BF16),
            pltpu.VMEM((rows, ffn), BF16),
            pltpu.VMEM((rows, size), F32),
            pltpu.VMEM((rows, width), BF16),
            pltpu.VMEM((rows, row_len), F32),
            pltpu.VMEM((rows, width), F32),
            pltpu.SemaphoreType.DMA((17,)),
        ],
        compiler_params=pltpu.CompilerParams(vmem_limit_bytes=12 * MIB),
        cost_estimate=pl.CostEstimate(flops=flops, bytes_accessed=8 * MIB, transcendentals=0),
        name="forward_chunk",
    )(meta, starts, in_hbm(tokens), in_vmem(incoming), *map(in_vmem, weights), *saved)


BWD_SAVED = ("gbs", "dus", "gms", "dqkvs", "igs", "gains", "carry")


def norm_backward(rows, gain, upstream):
    inverse = inverse_rms(rows)
    unit = rows * inverse
    steered = upstream * gain
    grad = inverse * (steered - unit * jnp.mean(steered * unit, axis=-1, keepdims=True))
    return grad, jnp.sum(upstream * unit, axis=0, keepdims=True)


def backward_kernel(
    geometry, last_call, gates, meta, starts, cotangent, incoming, hs, qs, ks, kts, vts, mids, slopes, lses,
    gain_attn, w_query, w_kv, w_out, gain_ffn, w_up, w_down, *refs,
):
    rows, row_len, heads, size = geometry
    refs = refs[gates:]
    count = len(BWD_SAVED) - last_call
    out, *gbs, dus, gms, dqkvs, igs, gains, carry = refs[count:2 * count + 1]
    (g_v, h_v, q_v, k_v, kt_v, vt_v, mid_v, slope_v, lse_v, du_v, gm_v, do_v, dqkv_v, ig_v, gain_v, carry_v,
     bias_v, total_v, sems) = refs[2 * count + 1:]
    parts = row_len // rows
    active, chunk, first = meta[0], meta[1], meta[2]
    scale = size**-0.5
    width = heads * size

    @pl.when(active == 1)
    def _():
        row = chunk // parts
        place = chunk % parts
        at = pl.ds(pl.multiple_of(chunk * rows, rows), rows)
        within = pl.ds(pl.multiple_of(place * rows, rows), rows)
        whole = pl.ds(pl.multiple_of(row * row_len, row_len), row_len)

        @pl.when(first == 1)
        def _():
            pltpu.make_async_copy(cotangent.at[at], g_v, sems.at[0]).start()

        @pl.when(first == 0)
        def _():
            pltpu.make_async_copy(incoming, g_v, sems.at[0]).start()

        loads = [
            pltpu.make_async_copy(source, target, sems.at[1 + i])
            for i, (source, target) in enumerate((
                (slopes.at[at], slope_v),
                (mids.at[at], mid_v),
                (qs.at[at], q_v),
                (lses.at[at], lse_v),
                (kts.at[row], kt_v),
                (vts.at[row], vt_v),
                (ks.at[whole], k_v),
                (carry, carry_v),
                (hs.at[at], h_v),
            ))
        ]
        for load in loads:
            load.start()
        pending = []

        def keep(source, target, slot):
            copy = pltpu.make_async_copy(source, target, sems.at[slot])
            copy.start()
            pending.append(copy)

        start_col = starts[at, :]
        bias_v[...] = position_bias(start_col, place * rows, rows, row_len)
        pltpu.make_async_copy(incoming, g_v, sems.at[0]).wait()
        g = g_v[...]
        if not last_call:
            keep(g_v, gbs[0].at[at], 10)
        loads[0].wait()
        ffn = w_up.shape[1]
        tile = min(FFN_TILE, ffn)

        def rise(f):
            cols = pl.ds(pl.multiple_of(f * tile, tile), tile)
            du = slope_v[:, cols].astype(F32) * dot_t(g_v[...], w_down[cols, :])
            du_v[:, cols] = du.astype(BF16)

        def fall(f):
            cols = pl.ds(pl.multiple_of(f * tile, tile), tile)
            return dot_t(du_v[:, cols], w_up[:, cols])

        def both(f, carry):
            part = fall(f - 1)
            total_v[...] = jnp.where(f == 1, part, total_v[...] + part)
            rise(f)
            return carry

        rise(0)
        lax.fori_loop(1, ffn // tile, both, 0)
        dn2 = total_v[...] + fall(ffn // tile - 1)
        keep(du_v, dus.at[at], 11)
        loads[1].wait()
        dv, dgain_ffn = norm_backward(mid_v[...], gain_ffn[...].astype(F32), dn2)
        dmid = g.astype(F32) + dv
        mid_v[...] = dmid
        gm = dmid.astype(BF16)
        gm_v[...] = gm
        keep(gm_v, gms.at[at], 12)
        do_v[...] = dot_t(gm, w_out[...]).astype(BF16)
        for load in loads[2:8]:
            load.wait()

        @pl.when(place == parts - 1)
        def _():
            carry_v[...] = jnp.zeros(carry_v.shape, F32)

        def attend(length):
            def some_heads(step, unused):
                for head in [step * BWD_HEADS + i for i in range(BWD_HEADS)]:
                    cols = pl.ds(pl.multiple_of(head * size, size), size)
                    q_h = q_v[:, cols]
                    do_h = do_v[:, cols]
                    lane = lax.broadcasted_iota(jnp.int32, (rows, size), 1)
                    lse = jnp.sum(jnp.where(lane == head, lse_v[...], 0.0), axis=1, keepdims=True)
                    scores = dot(q_h, kt_v[:, :length]) * (scale * LOG2E) + bias_v[:, :length]
                    probs = jnp.exp2(scores - lse)
                    dprobs = dot(do_h, vt_v[:, :length])
                    mean = jnp.sum(probs * dprobs, axis=1, keepdims=True)
                    dscores = (probs * (dprobs - mean)).astype(BF16)
                    dqkv_v[:, cols] = (dot(dscores, k_v[:length, :]) * scale).astype(BF16)
                    carry_v[:size, :length] += dot(q_h.T, dscores)
                    carry_v[size:, :length] += dot(do_h.T, probs.astype(BF16))
                return unused

            lax.fori_loop(0, heads // BWD_HEADS, some_heads, 0)
            own = slice(length - rows, length)
            dqkv_v[:, width:width + size] = (carry_v[:size, own].T * scale).astype(BF16)
            dqkv_v[:, width + size:] = carry_v[size:, own].T.astype(BF16)

        for step in range(parts):
            pl.when(place == step)(functools.partial(attend, (step + 1) * rows))

        keep(carry_v, carry, 13)
        keep(dqkv_v, dqkvs.at[at], 14)
        dn1 = dot_t(dqkv_v[:, :width], w_query[...]) + dot_t(dqkv_v[:, width:], w_kv[...])
        loads[8].wait()
        dv, dgain_attn = norm_backward(h_v[...].astype(F32), gain_attn[...].astype(F32), dn1)
        result = (mid_v[...] + dv).astype(BF16)
        out[...] = result
        ig_v[...] = result
        keep(ig_v, igs.at[at], 16)
        gain_v[...] = jnp.concatenate([dgain_attn, dgain_ffn, jnp.zeros((6, dgain_attn.shape[1]), F32)], axis=0)
        keep(gain_v, gains.at[chunk], 17)
        for copy in pending:
            copy.wait()


def backward_chunk(geometry, last_call, meta, starts, cotangent, incoming, kept, weights, saved, gates=()):
    rows, row_len, heads, size = geometry
    width = cotangent.shape[1]
    ffn = weights[5].shape[1]
    vmem = pl.BlockSpec(memory_space=pltpu.VMEM)
    anywhere = pl.BlockSpec(memory_space=pltpu.HBM)
    lead = 4 + len(kept) + len(weights) + len(gates)
    flops = 2 * rows * (2 * width * heads * size + 2 * width * size + 2 * width * ffn + 3 * row_len * heads * size)
    return pl.pallas_call(
        functools.partial(backward_kernel, geometry, last_call, len(gates)),
        out_shape=[jax.ShapeDtypeStruct((rows, width), BF16)]
        + [pltpu.HBM(array.shape, array.dtype) for array in saved],
        in_specs=[pl.BlockSpec(memory_space=pltpu.SMEM), vmem, anywhere, anywhere]
        + [anywhere] * len(kept) + [vmem] * len(weights) + [pl.BlockSpec(memory_space=pl.ANY)] * len(gates)
        + [anywhere] * len(saved),
        out_specs=[vmem] + [anywhere] * len(saved),
        input_output_aliases={lead + i: 1 + i for i in range(len(saved))},
        scratch_shapes=[
            pltpu.VMEM((rows, width), BF16),
            pltpu.VMEM((rows, width), BF16),
            pltpu.VMEM((rows, heads * size), BF16),
            pltpu.VMEM((row_len, size), BF16),
            pltpu.VMEM((size, row_len), BF16),
            pltpu.VMEM((size, row_len), BF16),
            pltpu.VMEM((rows, width), F32),
            pltpu.VMEM((rows, ffn), BF16),
            pltpu.VMEM((rows, size), F32),
            pltpu.VMEM((rows, ffn), BF16),
            pltpu.VMEM((rows, width), BF16),
            pltpu.VMEM((rows, heads * size), BF16),
            pltpu.VMEM((rows, (heads + 2) * size), BF16),
            pltpu.VMEM((rows, width), BF16),
            pltpu.VMEM((8, width), F32),
            pltpu.VMEM((2 * size, row_len), F32),
            pltpu.VMEM((rows, row_len), F32),
            pltpu.VMEM((rows, width), F32),
            pltpu.SemaphoreType.DMA((18,)),
        ],
        compiler_params=pltpu.CompilerParams(vmem_limit_bytes=20 * MIB),
        cost_estimate=pl.CostEstimate(
            flops=1024 if last_call else flops, bytes_accessed=1024 if last_call else 8 * MIB, transcendentals=0
        ),
        name="backward_chunk",
    )(meta, starts, in_hbm(cotangent), incoming, *map(in_hbm, kept), *map(in_vmem, weights), *gates, *saved)


def unwritten(shapes):
    return pl.pallas_call(
        lambda *refs: None,
        out_shape=shapes,
        out_specs=[pl.BlockSpec(memory_space=pltpu.HBM)] * len(shapes),
        compiler_params=pltpu.CompilerParams(vmem_limit_bytes=2 * MIB),
        name="unwritten",
    )()


def load_kernel(*refs):
    count = (len(refs) - 1) // 2
    sources, targets, sems = refs[:count + 1], refs[count + 1:-1], refs[-1]
    gain_attn, w_query, w_key, w_value, w_out, gain_ffn, w_up, w_down = sources
    gain_attn_v, w_query_v, w_kv_v, w_out_v, gain_ffn_v, w_up_v, w_down_v = targets
    size = w_key.shape[1]
    gain_attn_v[...] = gain_attn[...]
    gain_ffn_v[...] = gain_ffn[...]
    copies = [
        pltpu.make_async_copy(source, target, sems.at[i])
        for i, (source, target) in enumerate((
            (w_query, w_query_v),
            (w_key, w_kv_v.at[:, :size]),
            (w_value, w_kv_v.at[:, size:]),
            (w_out, w_out_v),
            (w_up, w_up_v),
            (w_down, w_down_v),
        ))
    ]
    for copy in copies:
        copy.start()
    for copy in copies:
        copy.wait()


def load_weights(gain_attn, w_query, w_key, w_value, w_out, gain_ffn, w_up, w_down):
    vmem = pl.BlockSpec(memory_space=pltpu.VMEM)
    hbm = pl.BlockSpec(memory_space=pltpu.HBM)
    shapes = [
        gain_attn.shape, w_query.shape, (w_key.shape[0], w_key.shape[1] + w_value.shape[1]), w_out.shape,
        gain_ffn.shape, w_up.shape, w_down.shape,
    ]
    return pl.pallas_call(
        load_kernel,
        out_shape=[pltpu.VMEM(shape, BF16) for shape in shapes],
        in_specs=[vmem, hbm, hbm, hbm, hbm, vmem, hbm, hbm],
        out_specs=[vmem] * len(shapes),
        scratch_shapes=[pltpu.SemaphoreType.DMA((6,))],
        compiler_params=pltpu.CompilerParams(vmem_limit_bytes=2 * MIB),
        name="load_weights",
    )(gain_attn, *map(in_hbm, (w_query, w_key, w_value, w_out)), gain_ffn, *map(in_hbm, (w_up, w_down)))


def segment_starts(lengths, row_len):
    count = lengths.shape[1]
    upto = jnp.arange(count)[:, None] <= jnp.arange(count)[None, :]
    ends = jnp.sum(jnp.where(upto[None], lengths[:, :, None], 0), axis=1)
    position = jnp.arange(row_len, dtype=jnp.int32)
    over = ends[:, None, :] <= position[None, :, None]
    start = jnp.sum(jnp.where(over, lengths[:, None, :], 0), axis=2)
    segment = jnp.sum(over.astype(jnp.int32), axis=2)
    return jnp.where(segment < count - 1, start, position[None]).astype(jnp.int32)


def dest_chip(step):
    chips = lax.axis_size("dp") // 2
    return lax.rem(lax.axis_index("dp") // 2 + 2 * chips - 1 - step, chips)


def swap_cores(block):
    return lax.ppermute(block, "dp", [(i, i ^ 1) for i in range(lax.axis_size("dp"))])


def next_chip(block):
    devices = lax.axis_size("dp")
    return lax.ppermute(block, "dp", [(i, (i + 2) % devices) for i in range(devices)])


def largest_tile(width, most):
    return max(tile for tile in range(128, most + 1, 128) if width % tile == 0)


def product_kernel(pairs, offsets, gates, share, meta, *refs):
    refs = refs[gates:]
    lefts, rights, refs = refs[:pairs], refs[pairs:2 * pairs], refs[2 * pairs:]
    extras = refs[:1] if pairs > 1 else ()
    refs = refs[len(extras):]
    added, refs = refs[:len(offsets)], refs[len(offsets):]
    outs, refs = refs[:len(refs) - 2 * pairs - 2], refs[len(refs) - 2 * pairs - 2:]
    lefts_v, rights_v, left_sems, right_sems = refs[:pairs], refs[pairs:2 * pairs], refs[-2], refs[-1]
    blocks = lefts_v[0].shape[0]
    left_copies, right_copies = [], []
    for i in range(pairs):
        for b in range(blocks):
            source = lefts[i]
            if source.shape[1] != share:
                source = source.at[:, pl.ds(pl.multiple_of(meta[b], 128), share)]
            left_copies.append(pltpu.make_async_copy(source, lefts_v[i].at[b], left_sems.at[i * blocks + b]))
            left_copies[-1].start()
        wide = largest_tile(rights[i].shape[1], 1280)
        for n in range(rights[i].shape[1] // wide):
            cols = slice(n * wide, (n + 1) * wide)
            copy = pltpu.make_async_copy(rights[i].at[:, cols], rights_v[i].at[:, cols], right_sems.at[len(right_copies)])
            copy.start()
            right_copies.append((copy, i, n, wide))

    def put(row, depth, col, value):
        for more, offset in zip(added, offsets):
            value = value + more[offset + row:offset + row + depth, col:col + value.shape[1]].astype(F32)
        start = 0
        for out in outs:
            low, high = max(col, start), min(col + value.shape[1], start + out.shape[1])
            if low < high:
                out[row:row + depth, low - start:high - start] = value[:, low - col:high - col].astype(out.dtype)
            start += out.shape[1]

    deep = min(share, 256)
    first_col = 0
    for copy, i, n, wide in right_copies:
        copy.wait()
        for b in range(blocks):
            if n == 0:
                left_copies[i * blocks + b].wait()
            for m in range(share // deep):
                value = lax.dot_general(
                    lefts_v[i][b, :, m * deep:(m + 1) * deep], rights_v[i][:, n * wide:(n + 1) * wide],
                    (((0,), (0,)), ((), ())), preferred_element_type=F32,
                )
                put(b * share + m * deep, deep, first_col, value)
        first_col += wide
    if extras:
        for b in range(blocks):
            put(b * share, share, first_col, extras[0][pl.ds(pl.multiple_of(meta[b], 8), share), :])


def products(share, firsts, lefts, rights, extra, added, dtype, gates, widths):
    vmem = pl.BlockSpec(memory_space=pltpu.VMEM)
    hbm = pl.BlockSpec(memory_space=pltpu.HBM)
    count = len(firsts)
    if share % 128:
        blocks = [[lax.dynamic_slice_in_dim(left, first, share, 1) for first in firsts] for left in lefts]
        if count > 1:
            parts = [
                products(
                    share, firsts[b:b + 1], lefts, rights, extra, [(more, at + b * share) for more, at in added], dtype,
                    gates, widths,
                )
                for b in range(count)
            ]
            return [jnp.concatenate(part, axis=0) for part in zip(*parts)]
        lefts = [block[0] for block in blocks]
    depth = lefts[0].shape[0]
    extras = [] if extra is None else [extra]
    total = sum(right.shape[1] for right in rights) + sum(more.shape[1] for more in extras)
    return pl.pallas_call(
        functools.partial(product_kernel, len(lefts), tuple(at for unused, at in added), len(gates), share),
        out_shape=[jax.ShapeDtypeStruct((count * share, width), dtype) for width in widths or [total]],
        in_specs=[pl.BlockSpec(memory_space=pltpu.SMEM)] + [pl.BlockSpec(memory_space=pl.ANY)] * len(gates)
        + [hbm] * (2 * len(lefts)) + [vmem] * (len(extras) + len(added)),
        out_specs=[vmem] * len(widths or [total]),
        scratch_shapes=[pltpu.VMEM((count, depth, share), BF16) for _ in lefts]
        + [pltpu.VMEM(right.shape, BF16) for right in rights]
        + [pltpu.SemaphoreType.DMA((len(lefts) * count,)), pltpu.SemaphoreType.DMA((8,))],
        compiler_params=pltpu.CompilerParams(vmem_limit_bytes=24 * MIB),
        cost_estimate=pl.CostEstimate(flops=10**11, bytes_accessed=1024, transcendentals=0),
        name="products",
    )(
        jnp.stack(firsts).astype(jnp.int32), *gates, *map(in_hbm, lefts), *map(in_hbm, rights), *extras,
        *(more for more, unused in added),
    )


def add_kernel(offset, kept, come, *outs):
    start = 0
    for out in outs:
        cols = slice(start, start + out.shape[1])
        out[...] = (kept[offset:offset + out.shape[0], cols].astype(F32) + come[:, cols].astype(F32)).astype(out.dtype)
        start += out.shape[1]


def add(kept, offset, come, dtype, widths):
    vmem = pl.BlockSpec(memory_space=pltpu.VMEM)
    return pl.pallas_call(
        functools.partial(add_kernel, offset),
        out_shape=[jax.ShapeDtypeStruct((come.shape[0], width), dtype) for width in widths or [come.shape[1]]],
        in_specs=[vmem, vmem],
        out_specs=[vmem] * len(widths or [1]),
        compiler_params=pltpu.CompilerParams(vmem_limit_bytes=4 * MIB),
        cost_estimate=pl.CostEstimate(flops=10**11, bytes_accessed=1024, transcendentals=0),
        name="add",
    )(kept, come)


class RowSums:
    def __init__(self, lefts, rights, extra=None):
        self.lefts, self.rights, self.extra = lefts, rights, extra
        self.share = lefts[0].shape[1] // lax.axis_size("dp")

    def blocks(self, steps, half, gates, added, dtype, widths=None):
        firsts = [(dest_chip(step) * 2 + half) * self.share for step in steps]
        return products(self.share, firsts, self.lefts, self.rights, self.extra, added, dtype, gates, widths)

    def other(self, steps, gates=()):
        return self.blocks(steps, 1 - lax.axis_index("dp") % 2, gates, [], BF16)[0]

    def own(self, steps, gates, added, dtype=BF16):
        return self.blocks(steps, lax.axis_index("dp") % 2, gates, added, dtype)[0]


def keep_last_kernel(rows, meta, incoming, unused, gbs, sem):
    @pl.when(meta[0] == 1)
    def _():
        at = pl.ds(pl.multiple_of(meta[1] * rows, rows), rows)
        copy = pltpu.make_async_copy(incoming, gbs.at[at], sem)
        copy.start()
        copy.wait()


def keep_last(meta, incoming, gbs):
    anywhere = pl.BlockSpec(memory_space=pltpu.HBM)
    return pl.pallas_call(
        functools.partial(keep_last_kernel, incoming.shape[0]),
        out_shape=pltpu.HBM(gbs.shape, gbs.dtype),
        in_specs=[pl.BlockSpec(memory_space=pltpu.SMEM), pl.BlockSpec(memory_space=pl.ANY), anywhere],
        out_specs=anywhere,
        input_output_aliases={2: 0},
        scratch_shapes=[pltpu.SemaphoreType.DMA],
        compiler_params=pltpu.CompilerParams(vmem_limit_bytes=2 * MIB),
        name="keep_last",
    )(meta, incoming, gbs)


def body(
    tokens, lengths, gain_attn, w_query, w_key, w_value, w_out, gain_ffn, w_up, w_down, cotangent
):
    micro, row_len, width = tokens.shape
    size = w_key.shape[2]
    heads = w_query.shape[2] // size
    ffn = w_up.shape[2]
    count = micro * row_len
    sections = lax.axis_size("section")
    place = lax.axis_index("section")
    weights = load_weights(gain_attn, w_query[0], w_key[0], w_value[0], w_out[0], gain_ffn, w_up[0], w_down[0])
    token_rows = tokens.reshape(count, width)
    cotangent_rows = cotangent.reshape(count, width)
    starts = segment_starts(lengths[:, 0], row_len).reshape(count, 1)

    def empty(*shape, dtype=BF16):
        return pltpu.HBM(shape, dtype)

    def meta_of(tick, chunks, rank, order):
        step = tick - SKEW * rank
        active = (step >= 0) & (step < chunks)
        chunk = order(jnp.clip(step, 0, chunks - 1))
        return jnp.stack([active.astype(jnp.int32), chunk.astype(jnp.int32), (rank == 0).astype(jnp.int32)])

    def hop(block, tick, chunks, rank_of, shift):
        route = [
            (s, s + shift)
            for s in range(sections)
            if 0 <= s + shift < sections and 0 <= tick - SKEW * rank_of(s) < chunks
        ]
        return lax.ppermute(block, "section", route) if route else None

    fwd_geometry = (FWD_ROWS, row_len, heads, size)
    fwd_chunks = count // FWD_ROWS
    saved = [
        empty(count, width), empty(count, width), empty(count, heads * size), empty(count, size), empty(count, size),
        empty(micro, size, row_len), empty(micro, size, row_len), empty(count, heads * size),
        empty(count, width, dtype=F32), empty(count, width), empty(count, ffn), empty(count, ffn),
        empty(count, size, dtype=F32), empty(count, width),
    ]
    saved = unwritten(saved)
    received = {}
    nothing = jnp.zeros((FWD_ROWS, width), BF16)
    for tick in range(fwd_chunks + SKEW * (sections - 1)):
        meta = meta_of(tick, fwd_chunks, place, lambda step: step)
        incoming = received.pop(tick - SKEW, None)
        out, *saved = forward_chunk(
            fwd_geometry, meta, starts, token_rows, nothing if incoming is None else incoming, weights, saved
        )
        received[tick] = hop(out, tick, fwd_chunks, lambda s: s, 1)

    kept = dict(zip(FWD_SAVED, saved))
    layer_outs = kept["outs"]
    needed = [kept[name] for name in ("hs", "qs", "ks", "kts", "vts", "mids", "slopes", "lses")]
    bwd_geometry = (BWD_ROWS, row_len, heads, size)
    bwd_chunks = count // BWD_ROWS
    parts = row_len // BWD_ROWS
    saved = unwritten([
        empty(count, width), empty(count, ffn), empty(count, width), empty(count, (heads + 2) * size),
        empty(count, width), empty(bwd_chunks, 8, width, dtype=F32), empty(2 * size, row_len, dtype=F32),
    ])
    received = {}
    nothing = jnp.zeros((BWD_ROWS, width), BF16)
    ticks = bwd_chunks + SKEW * (sections - 1)
    down_sums = None
    for tick in range(ticks):
        meta = meta_of(
            tick, bwd_chunks, sections - 1 - place, lambda step: step // parts * parts + parts - 1 - step % parts
        )
        incoming = received.pop(tick - SKEW, None)
        if incoming is None:
            incoming = nothing
        if tick == ticks - 1:
            gbs = keep_last(meta, incoming, saved[0])
            down_sums = RowSums([kept["acts"]], [gbs])
            swapped = swap_cores(down_sums.other([0]))
            first_total = down_sums.own([0], (), [(swapped, 0)])
            down_ring = next_chip(first_total)
            ready = down_sums.other([1], [first_total])
            swapped = swap_cores(ready)
            out, *rest = backward_chunk(
                bwd_geometry, True, meta, starts, cotangent_rows, incoming, needed, weights, saved[1:],
                [first_total, ready],
            )
            saved = [gbs] + rest
            continue
        out, *saved = backward_chunk(
            bwd_geometry, False, meta, starts, cotangent_rows, incoming, needed, weights, saved
        )
        received[tick] = hop(out, tick, bwd_chunks, lambda s: sections - 1 - s, -1)
    done = dict(zip(BWD_SAVED, saved))

    gains = jnp.sum(done["gains"], axis=0)
    gains = jnp.pad(gains.T, ((0, 0), (0, 128 - gains.shape[0])))
    rest_sums = RowSums([kept["n2s"], kept["n1s"], kept["os"]], [done["dus"], done["dqkvs"], done["gms"]], gains)
    chips = lax.axis_size("dp") // 2
    later = list(range(1, chips))
    widths = [ffn, heads * size, size, size, width, 128]

    down = down_sums.own([1], [out], [(swapped, 0), (down_ring, 0)], BF16 if chips > 2 else F32)
    if chips > 2:
        down_ring = next_chip(down)
    swapped = swap_cores(rest_sums.other([0], [down]))
    down_others = down_sums.other(later[1:], [down]) if chips > 2 else None
    rest = rest_sums.own([0], [down] if down_others is None else [down_others], [(swapped, 0)])
    rest_ring = next_chip(rest)
    if chips > 2:
        down_swapped = swap_cores(down_others)
    rest_others = rest_sums.other(later, [rest])
    rest_swapped = swap_cores(rest_others)
    if chips > 2:
        down_kept = down_sums.own(later[1:], [rest_others], [(down_swapped, 0)])
    rest_kept = None
    for step in range(1, chips):
        if step + 1 < chips:
            last = step + 1 == chips - 1
            down = add(down_kept, (step - 1) * down_sums.share, down_ring, F32 if last else BF16, None)[0]
            if not last:
                down_ring = next_chip(down)
        if rest_kept is None:
            rest_kept = rest_sums.own(later, [down], [(rest_swapped, 0)])
        last = step == chips - 1
        rest = add(
            rest_kept, (step - 1) * rest_sums.share, rest_ring, F32 if last else BF16, widths if last else None
        )
        if not last:
            rest_ring = next_chip(rest[0])
    up, query, key, value, out, gains = rest
    shares = (gains[:, 0], query, key, value, out, gains[:, 1], up, down)
    shape = (1, micro, row_len, width)
    return (layer_outs.reshape(shape), done["igs"].reshape(shape)) + tuple(share[None] for share in shares)


def solution(mesh):
    return jax.shard_map(
        body,
        mesh=mesh,
        in_specs=(
            P(None, "dp", None),
            P(None, "dp", None),
            P("section", None),
            P("section", None, None),
            P("section", None, None),
            P("section", None, None),
            P("section", None, None),
            P("section", None),
            P("section", None, None),
            P("section", None, None),
            P(None, "dp", None),
        ),
        out_specs=(
            P("section", None, "dp", None),
            P("section", None, "dp", None),
            P("section", "dp"),
            P("section", "dp", None),
            P("section", "dp", None),
            P("section", "dp", None),
            P("section", "dp", None),
            P("section", "dp"),
            P("section", "dp", None),
            P("section", "dp", None),
        ),
        check_vma=False,
    )
```

```python
import functools

import jax
import jax.numpy as jnp
from jax import lax
from jax.experimental import pallas as pl
from jax.experimental.pallas import tpu as pltpu
from jax.sharding import PartitionSpec as P

NORM_EPS = 1e-06
MASKED = -1e30
LOG2E = 1.4426950408889634
FWD_ROWS = 128
BWD_ROWS = 256
FFN_TILE = 2048
BWD_TILE = 2048
SKEW = 2
FWD_HEADS = 4
BWD_HEADS = 2
NORM_BLOCK = 128
NORM_UNROLL = 2
SOFTMAX_BLOCK = 128
SOFTMAX_UNROLL = 2
SIDE_TILE = 512
MIB = 1 << 20
LIGHT = 5 * 10**9
HEAVY = 10**11

BF16 = jnp.bfloat16
F32 = jnp.float32


def in_hbm(array):
    return pltpu.with_memory_space_constraint(array, pltpu.HBM)


def in_vmem(array):
    return pltpu.with_memory_space_constraint(array, pltpu.VMEM)


def dot(left, right):
    return jnp.dot(left, right, preferred_element_type=F32)


def dot_t(left, right):
    return lax.dot_general(left, right, (((1,), (1,)), ((), ())), preferred_element_type=F32)


def inverse_rms(rows):
    return lax.rsqrt(jnp.mean(rows * rows, axis=-1, keepdims=True) + NORM_EPS)


def gelu_parts(u):
    t = pl.reciprocal(1.0 + jnp.abs(u) * 0.23164190, approx=True)
    bell = jnp.exp2(u * u * (-0.5 * LOG2E))
    poly = t * (0.127414796 + t * (-0.142248368 + t * (0.7107068705 + t * (-0.7265760135 + t * 0.5307027145))))
    tail = poly * bell
    cdf = jnp.where(u >= 0, 1.0 - tail, tail)
    return u * cdf, cdf + u * bell * 0.3989422804014327


def each_block(rows, block, work, unroll=1):
    def step(i, unused):
        work(pl.ds(pl.multiple_of(i * block, block), block))
        return unused

    lax.fori_loop(0, rows // block, step, 0, unroll=unroll)


def weight_copies(sources, targets, sems):
    w_query, w_key, w_value, w_out, w_up, w_down = sources
    w_query_v, w_kv_v, w_out_v, w_up_v, w_down_v = targets
    size = w_key.shape[1]
    half = w_up.shape[1] // 2
    low, high = slice(0, half), slice(half, 2 * half)
    pieces = {
        "query": (w_query, w_query_v),
        "key": (w_key, w_kv_v.at[:, :size]),
        "value": (w_value, w_kv_v.at[:, size:]),
        "out": (w_out, w_out_v),
        "up0": (w_up.at[:, low], w_up_v.at[:, low]),
        "up1": (w_up.at[:, high], w_up_v.at[:, high]),
        "down0": (w_down.at[low, :], w_down_v.at[low, :]),
        "down1": (w_down.at[high, :], w_down_v.at[high, :]),
    }
    return {name: pltpu.make_async_copy(*piece, sems.at[i]) for i, (name, piece) in enumerate(pieces.items())}


FWD_LOADS = ("query", "key", "value", "out", "up0", "up1", "down0", "down1")
BWD_LOADS = ("down0", "up0", "down1", "up1", "out", "query", "key", "value")


def position_bias(meta, spot, count, first_row, rows, length):
    place = first_row + lax.broadcasted_iota(jnp.int32, (rows, 1), 0)
    start = jnp.zeros((rows, 1), jnp.int32)
    end = 0
    for i in range(count - 1):
        end = end + meta[spot + i]
        start = jnp.where(place >= end, end, start)
    start = jnp.where(place >= end, place, start)
    own = first_row + lax.broadcasted_iota(jnp.int32, (rows, length), 0)
    other = lax.broadcasted_iota(jnp.int32, (rows, length), 1)
    return jnp.where((other >= start) & (other <= own), 0.0, MASKED)


def forward_kernel(geometry, loading, places, spots, meta, tokens, incoming, gain_attn, gain_ffn, *refs):
    rows, row_len, heads, size, segments = geometry
    spot, lengths_spot = spots
    if loading:
        sources, refs = refs[:6], refs[6:]
        load_sems = refs[-1]
        w_query, w_kv, w_out, w_up, w_down = refs[2 * len(FWD_SAVED) + 1:2 * len(FWD_SAVED) + 6]
        refs = refs[:2 * len(FWD_SAVED) + 1] + refs[2 * len(FWD_SAVED) + 6:-1]
        weight_loads = weight_copies(sources, (w_query, w_kv, w_out, w_up, w_down), load_sems)
        for name in FWD_LOADS:
            weight_loads[name].start()
    else:
        w_query, w_kv, w_out, w_up, w_down = refs[:5]
        refs = refs[5:]

    def loaded(*names):
        for name in names if loading else ():
            weight_loads[name].wait()

    saved = refs[len(FWD_SAVED):2 * len(FWD_SAVED) + 1]
    out, hs, n1s, qs, ks, vs, kts, vts, os_, mids, n2s, acts, slopes, lses, outs = saved
    (h_v, n1_v, q_v, k_v, v_v, kt_v, vt_v, o_v, mid_v, n2_v, act_v, slope_v, lse_v, out_v, bias_v, total_v, s_v, p_v, sems) = (
        refs[2 * len(FWD_SAVED) + 1:]
    )
    parts = row_len // rows
    active, chunk, first = meta[spot], meta[spot + 1], meta[spot + 2]
    width = heads * size
    scale = size**-0.5 * LOG2E

    @pl.when(active == 0)
    def _():
        loaded(*FWD_LOADS)

    @pl.when(active == 1)
    def _():
        row = chunk // parts
        place = chunk % parts
        at = pl.ds(pl.multiple_of(chunk * rows, rows), rows)
        within = pl.ds(pl.multiple_of(place * rows, rows), rows)
        whole = pl.ds(pl.multiple_of(row * row_len, row_len), row_len)

        @pl.when(first == 1)
        def _():
            pltpu.make_async_copy(tokens.at[at], h_v, sems.at[0]).start()

        load_v = pltpu.make_async_copy(vs.at[whole], v_v, sems.at[1])
        load_kt = pltpu.make_async_copy(kts.at[row], kt_v, sems.at[2])
        load_v.start()
        load_kt.start()
        pending = []

        def keep(source, target, slot):
            copy = pltpu.make_async_copy(source, target, sems.at[slot])
            copy.start()
            pending.append(copy)

        @pl.when(first == 1)
        def _():
            pltpu.make_async_copy(tokens.at[at], h_v, sems.at[0]).wait()

        @pl.when(first == 0)
        def _():
            h_v[...] = incoming[...]

        keep(h_v, hs.at[at], 3)

        def norm_attn(block):
            h = h_v[block, :].astype(F32)
            n1_v[block, :] = (h * inverse_rms(h) * gain_attn[...].astype(F32)).astype(BF16)

        each_block(rows, NORM_BLOCK, norm_attn, rows // NORM_BLOCK)
        keep(n1_v, n1s.at[at], 4)
        loaded("query", "key", "value")
        kv = dot(n1_v[...], w_kv[...]).astype(BF16)
        q_v[...] = dot(n1_v[...], w_query[...]).astype(BF16)
        k_v[...] = kv[:, :size]
        keep(k_v, ks.at[at], 5)
        keep(q_v, qs.at[at], 6)
        load_v.wait()
        load_kt.wait()
        v_v[within, :] = kv[:, size:]
        kt_v[:, within] = kv[:, :size].T
        vt_v[...] = kv[:, size:].T
        keep(v_v.at[within], vs.at[at], 7)
        keep(kt_v.at[:, within], kts.at[row, :, within], 8)
        keep(vt_v, vts.at[row, :, within], 9)

        lse_v[...] = jnp.zeros((rows, size), F32)

        def attend(static_place):
            length = (static_place + 1) * rows
            lane = lax.broadcasted_iota(jnp.int32, (SOFTMAX_BLOCK, size), 1)
            bias_v[:, :length] = position_bias(
                meta, lengths_spot + row * segments, segments, static_place * rows, rows, length
            )

            def some_heads(step, carry):
                group = [step * FWD_HEADS + i for i in range(FWD_HEADS)]
                for i, head in enumerate(group):
                    cols = pl.ds(pl.multiple_of(head * size, size), size)
                    s_v[i, :, :length] = dot(q_v[:, cols], kt_v[:, :length])
                for i, head in enumerate(group):
                    cols = pl.ds(pl.multiple_of(head * size, size), size)

                    def soften(block, i=i, head=head):
                        scores = s_v[i, block, :length] * scale + bias_v[block, :length]
                        top = jnp.max(scores, axis=1, keepdims=True)
                        weights = jnp.exp2(scores - top)
                        total = jnp.sum(weights, axis=1, keepdims=True)
                        p_v[i, block, :length] = (weights * (1.0 / total)).astype(BF16)
                        lse_v[block, :] = jnp.where(lane == head, top + jnp.log2(total), lse_v[block, :])

                    each_block(rows, SOFTMAX_BLOCK, soften, rows // SOFTMAX_BLOCK)
                    o_v[:, cols] = dot(p_v[i, :, :length], v_v[:length, :]).astype(BF16)
                return carry

            lax.fori_loop(0, heads // FWD_HEADS, some_heads, 0)

        for static_place in places:
            if len(places) == 1:
                attend(static_place)
            else:
                pl.when(place == static_place)(functools.partial(attend, static_place))

        keep(lse_v, lses.at[at], 10)
        keep(o_v, os_.at[at], 11)
        loaded("out")
        total_v[...] = dot(o_v[...], w_out[...])

        def norm_ffn(block):
            mid = h_v[block, :].astype(F32) + total_v[block, :]
            mid_v[block, :] = mid
            total_v[block, :] = mid
            n2_v[block, :] = (mid * inverse_rms(mid) * gain_ffn[...].astype(F32)).astype(BF16)

        each_block(rows, NORM_BLOCK, norm_ffn, rows // NORM_BLOCK)
        keep(mid_v, mids.at[at], 12)
        keep(n2_v, n2s.at[at], 13)
        ffn = w_up.shape[1]
        tile = min(FFN_TILE, ffn)


        def columns(f):
            return pl.ds(pl.multiple_of(f * tile, tile), tile)

        def rise(f):
            return dot(n2_v[...], w_up[:, columns(f)])

        def bend(f, u):
            act, slope = gelu_parts(u)
            act_v[:, columns(f)] = act.astype(BF16)
            slope_v[:, columns(f)] = slope.astype(BF16)
            pltpu.make_async_copy(act_v.at[:, columns(f)], acts.at[at, columns(f)], sems.at[14]).start()
            pltpu.make_async_copy(slope_v.at[:, columns(f)], slopes.at[at, columns(f)], sems.at[15]).start()

        def fall(f):
            return dot(act_v[:, columns(f)], w_down[columns(f), :])

        def both(f, carry):
            u = rise(f)
            part = fall(f - 1)
            bend(f, u)
            total_v[...] += part
            return carry

        loaded("up0")
        bend(0, rise(0))
        loaded("up1", "down0")
        lax.fori_loop(1, ffn // tile, both, 0)
        loaded("down1")
        total_v[...] += fall(ffn // tile - 1)
        total = total_v[...]
        pending.append(pltpu.make_async_copy(act_v, acts.at[at], sems.at[14]))
        pending.append(pltpu.make_async_copy(slope_v, slopes.at[at], sems.at[15]))
        result = total.astype(BF16)
        out[...] = result
        out_v[...] = result
        keep(out_v, outs.at[at], 16)
        for copy in pending:
            copy.wait()


FWD_SAVED = ("hs", "n1s", "qs", "ks", "vs", "kts", "vts", "os", "mids", "n2s", "acts", "slopes", "lses", "outs")


def forward_chunk(geometry, places, spots, meta, tokens, incoming, weights, saved, given=None):
    rows, row_len, heads, size, unused = geometry
    gain_attn, gain_ffn, *matrices = weights
    loading = given is not None
    width = tokens.shape[1]
    ffn = (given[4] if loading else matrices[3]).shape[1]
    vmem = pl.BlockSpec(memory_space=pltpu.VMEM)
    hbm = pl.BlockSpec(memory_space=pltpu.HBM)
    loads = [pltpu.VMEM(shape, BF16) for shape in weight_shapes(given)] if loading else []
    operands = list(map(in_hbm, given)) if loading else list(map(in_vmem, matrices))
    lead = 5 + len(operands)
    flops = 2 * rows * (2 * width * heads * size + 2 * width * size + 2 * width * ffn + row_len * heads * size)
    out, *rest = pl.pallas_call(
        functools.partial(forward_kernel, geometry, loading, places, spots),
        out_shape=[jax.ShapeDtypeStruct((rows, width), BF16)]
        + [pltpu.HBM(array.shape, array.dtype) for array in saved] + loads,
        in_specs=[pl.BlockSpec(memory_space=pltpu.SMEM), hbm, vmem, vmem, vmem]
        + [hbm if loading else vmem] * len(operands) + [hbm] * len(saved),
        out_specs=[vmem] + [hbm] * len(saved) + [vmem] * len(loads),
        input_output_aliases={lead + i: 1 + i for i in range(len(saved))},
        scratch_shapes=[
            pltpu.VMEM((rows, width), BF16),
            pltpu.VMEM((rows, width), BF16),
            pltpu.VMEM((rows, heads * size), BF16),
            pltpu.VMEM((rows, size), BF16),
            pltpu.VMEM((row_len, size), BF16),
            pltpu.VMEM((size, row_len), BF16),
            pltpu.VMEM((size, rows), BF16),
            pltpu.VMEM((rows, heads * size), BF16),
            pltpu.VMEM((rows, width), F32),
            pltpu.VMEM((rows, width), BF16),
            pltpu.VMEM((rows, ffn), BF16),
            pltpu.VMEM((rows, ffn), BF16),
            pltpu.VMEM((rows, size), F32),
            pltpu.VMEM((rows, width), BF16),
            pltpu.VMEM((rows, row_len), F32),
            pltpu.VMEM((rows, width), F32),
            pltpu.VMEM((FWD_HEADS, rows, row_len), F32),
            pltpu.VMEM((FWD_HEADS, rows, row_len), BF16),
            pltpu.SemaphoreType.DMA((17,)),
        ]
        + [pltpu.SemaphoreType.DMA((8,))] * loading,
        compiler_params=pltpu.CompilerParams(vmem_limit_bytes=12 * MIB),
        cost_estimate=pl.CostEstimate(flops=flops, bytes_accessed=8 * MIB, transcendentals=0),
        name="forward_chunk",
    )(meta, in_hbm(tokens), in_vmem(incoming), gain_attn, gain_ffn, *operands, *saved)
    return out, rest[:len(saved)], rest[len(saved):]


def weight_shapes(given):
    w_query, w_key, w_value, w_out, w_up, w_down = given
    return w_query.shape, (w_key.shape[0], 2 * w_key.shape[1]), w_out.shape, w_up.shape, w_down.shape


BWD_SAVED = ("gbs", "dus", "gms", "dqkvs", "igs", "gains", "carry")


def norm_backward(rows, gain, upstream):
    inverse = inverse_rms(rows)
    unit = rows * inverse
    steered = upstream * gain
    grad = inverse * (steered - unit * jnp.mean(steered * unit, axis=-1, keepdims=True))
    return grad, jnp.sum((upstream * unit).reshape(-1, 8, rows.shape[1]), axis=0)


def backward_kernel(
    geometry, last_call, gates, static_place, spots, meta, cotangent, incoming, hs, qs, ks, kts, vts, mids, slopes, lses,
    gain_attn, gain_ffn, *refs,
):
    rows, row_len, heads, size, segments = geometry
    spot, lengths_spot = spots
    if last_call:
        sources, refs = refs[:6], refs[6:]
        w_query, w_kv, w_out, w_up, w_down, load_sems = refs[-6:]
        refs = refs[:-6]
        weight_loads = weight_copies(sources, (w_query, w_kv, w_out, w_up, w_down), load_sems)
    else:
        w_query, w_kv, w_out, w_up, w_down = refs[:5]
        refs = refs[5:]

    def loaded(*names):
        for name in names if last_call else ():
            weight_loads[name].wait()

    refs = refs[gates:]
    count = len(BWD_SAVED) - last_call
    out, *gbs, dus, gms, dqkvs, igs, gains, carry = refs[count:2 * count + 1]
    (g_v, h_v, q_v, k_v, kt_v, vt_v, mid_v, slope_v, lse_v, du_v, gm_v, do_v, dqkv_v, ig_v, gain_v, carry_v,
     bias_v, total_v, s_v, dp_v, p_v, ds_v, sems) = refs[2 * count + 1:]
    parts = row_len // rows
    active, chunk, first = meta[spot], meta[spot + 1], meta[spot + 2]
    scale = size**-0.5
    width = heads * size

    @pl.when(active == 1)
    def _():
        row = chunk // parts
        at = pl.ds(pl.multiple_of(chunk * rows, rows), rows)
        whole = pl.ds(pl.multiple_of(row * row_len, row_len), row_len)

        @pl.when(first == 1)
        def _():
            pltpu.make_async_copy(cotangent.at[at], g_v, sems.at[0]).start()

        loads = [
            pltpu.make_async_copy(source, target, sems.at[1 + i])
            for i, (source, target) in enumerate((
                (slopes.at[at], slope_v),
                (mids.at[at], mid_v),
                (qs.at[at], q_v),
                (lses.at[at], lse_v),
                (kts.at[row], kt_v),
                (vts.at[row], vt_v),
                (ks.at[whole], k_v),
                (carry, carry_v),
                (hs.at[at], h_v),
            ))
        ]
        for load in loads[:1]:
            load.start()
        for name in BWD_LOADS[:2] if last_call else ():
            weight_loads[name].start()
        for load in loads[1:]:
            load.start()
        for name in BWD_LOADS[2:] if last_call else ():
            weight_loads[name].start()
        pending = []

        def keep(source, target, slot):
            copy = pltpu.make_async_copy(source, target, sems.at[slot])
            copy.start()
            pending.append(copy)

        length = (static_place + 1) * rows
        bias_v[:, :length] = position_bias(
            meta, lengths_spot + row * segments, segments, static_place * rows, rows, length
        )
        @pl.when(first == 1)
        def _():
            pltpu.make_async_copy(cotangent.at[at], g_v, sems.at[0]).wait()

        @pl.when(first == 0)
        def _():
            g_v[...] = incoming[...]

        if not last_call:
            keep(g_v, gbs[0].at[at], 10)
        loads[0].wait()
        ffn = w_up.shape[1]
        tile = min(BWD_TILE, ffn)

        def rise(f):
            cols = pl.ds(pl.multiple_of(f * tile, tile), tile)
            return dot_t(g_v[...], w_down[cols, :])

        def bend(f, da):
            cols = pl.ds(pl.multiple_of(f * tile, tile), tile)
            du_v[:, cols] = (slope_v[:, cols].astype(F32) * da).astype(BF16)

        def fall(f):
            cols = pl.ds(pl.multiple_of(f * tile, tile), tile)
            return dot_t(du_v[:, cols], w_up[:, cols])

        def both(f, carry):
            da = rise(f)
            part = fall(f - 1)
            bend(f, da)
            total_v[...] = jnp.where(f == 1, part, total_v[...] + part)
            return carry

        loaded("down0")
        bend(0, rise(0))
        loaded("up0", "down1")
        lax.fori_loop(1, ffn // tile, both, 0)
        loaded("up1")
        total_v[...] += fall(ffn // tile - 1)
        keep(du_v, dus.at[at], 11)
        loads[1].wait()
        gain_v[...] = jnp.zeros(gain_v.shape, F32)

        def norm_ffn(block):
            dv, dgain = norm_backward(mid_v[block, :], gain_ffn[...].astype(F32), total_v[block, :])
            dmid = g_v[block, :].astype(F32) + dv
            mid_v[block, :] = dmid
            gm_v[block, :] = dmid.astype(BF16)
            gain_v[8:, :] += dgain

        each_block(rows, NORM_BLOCK, norm_ffn, rows // NORM_BLOCK)
        keep(gm_v, gms.at[at], 12)
        loaded("out")
        do_v[...] = dot_t(gm_v[...], w_out[...]).astype(BF16)
        for load in loads[2:8]:
            load.wait()

        if static_place == parts - 1:
            carry_v[...] = jnp.zeros(carry_v.shape, F32)

        def attend():
            lane = lax.broadcasted_iota(jnp.int32, (SOFTMAX_BLOCK, size), 1)

            def some_heads(step, unused):
                group = [step * BWD_HEADS + i for i in range(BWD_HEADS)]
                for i, head in enumerate(group):
                    cols = pl.ds(pl.multiple_of(head * size, size), size)
                    s_v[i, :, :length] = dot(q_v[:, cols], kt_v[:, :length])
                    dp_v[i, :, :length] = dot(do_v[:, cols], vt_v[:, :length])
                for i, head in enumerate(group):
                    cols = pl.ds(pl.multiple_of(head * size, size), size)

                    def steepen(block, i=i, head=head):
                        lse = jnp.sum(jnp.where(lane == head, lse_v[block, :], 0.0), axis=1, keepdims=True)
                        scores = s_v[i, block, :length] * (scale * LOG2E) + bias_v[block, :length]
                        probs = jnp.exp2(scores - lse)
                        p_v[i, block, :length] = probs.astype(BF16)
                        dprobs = dp_v[i, block, :length]
                        mean = jnp.sum(probs * dprobs, axis=1, keepdims=True)
                        ds_v[i, block, :length] = (probs * (dprobs - mean)).astype(BF16)

                    each_block(rows, SOFTMAX_BLOCK, steepen, rows // SOFTMAX_BLOCK)
                    dqkv_v[:, cols] = (dot(ds_v[i, :, :length], k_v[:length, :]) * scale).astype(BF16)
                    carry_v[:size, :length] += dot(q_v[:, cols].T, ds_v[i, :, :length])
                    carry_v[size:, :length] += dot(do_v[:, cols].T, p_v[i, :, :length])
                return unused

            lax.fori_loop(0, heads // BWD_HEADS, some_heads, 0)
            own = slice(length - rows, length)
            dqkv_v[:, width:width + size] = (carry_v[:size, own].T * scale).astype(BF16)
            dqkv_v[:, width + size:] = carry_v[size:, own].T.astype(BF16)

        attend()

        keep(carry_v, carry, 13)
        keep(dqkv_v, dqkvs.at[at], 14)
        loaded("query", "key", "value")
        dn1 = dot_t(dqkv_v[:, :width], w_query[...]) + dot_t(dqkv_v[:, width:], w_kv[...])
        loads[8].wait()
        total_v[...] = dn1

        def norm_attn(block):
            dv, dgain = norm_backward(h_v[block, :].astype(F32), gain_attn[...].astype(F32), total_v[block, :])
            ig_v[block, :] = (mid_v[block, :] + dv).astype(BF16)
            gain_v[:8, :] += dgain

        each_block(rows, NORM_BLOCK, norm_attn, rows // NORM_BLOCK)
        out[...] = ig_v[...]
        keep(ig_v, igs.at[at], 16)
        keep(gain_v, gains.at[chunk], 17)
        for copy in pending:
            copy.wait()


def backward_chunk(geometry, last_call, static_place, spots, meta, cotangent, incoming, kept, weights, saved, gates=()):
    rows, row_len, heads, size, unused = geometry
    gain_attn, gain_ffn, *matrices = weights
    width = cotangent.shape[1]
    ffn = matrices[4 if last_call else 3].shape[1]
    vmem = pl.BlockSpec(memory_space=pltpu.VMEM)
    hbm = pl.BlockSpec(memory_space=pltpu.HBM)
    lead = 3 + len(kept) + len(weights) + len(gates)
    flops = 2 * rows * (2 * width * heads * size + 2 * width * size + 2 * width * ffn + 3 * row_len * heads * size)
    return pl.pallas_call(
        functools.partial(backward_kernel, geometry, last_call, len(gates), static_place, spots),
        out_shape=[jax.ShapeDtypeStruct((rows, width), BF16)]
        + [pltpu.HBM(array.shape, array.dtype) for array in saved],
        in_specs=[pl.BlockSpec(memory_space=pltpu.SMEM), hbm, vmem]
        + [hbm] * len(kept) + [vmem] * 2 + [hbm if last_call else vmem] * len(matrices)
        + [pl.BlockSpec(memory_space=pl.ANY)] * len(gates) + [hbm] * len(saved),
        out_specs=[vmem] + [hbm] * len(saved),
        input_output_aliases={lead + i: 1 + i for i in range(len(saved))},
        scratch_shapes=[
            pltpu.VMEM((rows, width), BF16),
            pltpu.VMEM((rows, width), BF16),
            pltpu.VMEM((rows, heads * size), BF16),
            pltpu.VMEM((row_len, size), BF16),
            pltpu.VMEM((size, row_len), BF16),
            pltpu.VMEM((size, row_len), BF16),
            pltpu.VMEM((rows, width), F32),
            pltpu.VMEM((rows, ffn), BF16),
            pltpu.VMEM((rows, size), F32),
            pltpu.VMEM((rows, ffn), BF16),
            pltpu.VMEM((rows, width), BF16),
            pltpu.VMEM((rows, heads * size), BF16),
            pltpu.VMEM((rows, (heads + 2) * size), BF16),
            pltpu.VMEM((rows, width), BF16),
            pltpu.VMEM((16, width), F32),
            pltpu.VMEM((2 * size, row_len), F32),
            pltpu.VMEM((rows, row_len), F32),
            pltpu.VMEM((rows, width), F32),
            pltpu.VMEM((BWD_HEADS, rows, row_len), F32),
            pltpu.VMEM((BWD_HEADS, rows, row_len), F32),
            pltpu.VMEM((BWD_HEADS, rows, row_len), BF16),
            pltpu.VMEM((BWD_HEADS, rows, row_len), BF16),
            pltpu.SemaphoreType.DMA((18,)),
        ]
        + [pltpu.VMEM(shape, BF16) for shape in (weight_shapes(matrices) if last_call else ())]
        + [pltpu.SemaphoreType.DMA((8,))] * last_call,
        compiler_params=pltpu.CompilerParams(vmem_limit_bytes=(42 if last_call else 20) * MIB),
        cost_estimate=pl.CostEstimate(
            flops=1024 if last_call else flops, bytes_accessed=1024 if last_call else 8 * MIB, transcendentals=0
        ),
        name="backward_chunk",
    )(
        meta, in_hbm(cotangent), in_vmem(incoming), *map(in_hbm, kept), gain_attn, gain_ffn,
        *map(in_hbm if last_call else in_vmem, matrices), *gates, *saved,
    )


def unwritten(shapes):
    return pl.pallas_call(
        lambda *refs: None,
        out_shape=shapes,
        out_specs=[pl.BlockSpec(memory_space=pltpu.HBM)] * len(shapes),
        compiler_params=pltpu.CompilerParams(vmem_limit_bytes=2 * MIB),
        name="unwritten",
    )()


def dest_chip(step):
    chips = lax.axis_size("dp") // 2
    return lax.rem(lax.axis_index("dp") // 2 + 2 * chips - 1 - step, chips)


def swap_cores(block):
    return lax.ppermute(block, "dp", [(i, i ^ 1) for i in range(lax.axis_size("dp"))])


def next_chip(block):
    devices = lax.axis_size("dp")
    return lax.ppermute(block, "dp", [(i, (i + 2) % devices) for i in range(devices)])


def largest_tile(width, most):
    return max(tile for tile in range(128, most + 1, 128) if width % tile == 0)


def product_kernel(pairs, offsets, gates, share, spots, meta, *refs):
    refs = refs[gates:]
    lefts, rights, refs = refs[:pairs], refs[pairs:2 * pairs], refs[2 * pairs:]
    extras = refs[:1] if pairs > 1 else ()
    refs = refs[len(extras):]
    added, refs = refs[:len(offsets)], refs[len(offsets):]
    outs, refs = refs[:len(refs) - 2 * pairs - 2], refs[len(refs) - 2 * pairs - 2:]
    lefts_v, rights_v, left_sems, right_sems = refs[:pairs], refs[pairs:2 * pairs], refs[-2], refs[-1]
    blocks = lefts_v[0].shape[0]
    left_copies, right_copies = [], []
    for i in range(pairs):
        for b in range(blocks):
            source = lefts[i]
            if source.shape[1] != share:
                source = source.at[:, pl.ds(pl.multiple_of(meta[spots[b]] * share, 128), share)]
            left_copies.append(pltpu.make_async_copy(source, lefts_v[i].at[b], left_sems.at[i * blocks + b]))
            left_copies[-1].start()
        wide = largest_tile(rights[i].shape[1], 1280)
        for n in range(rights[i].shape[1] // wide):
            cols = slice(n * wide, (n + 1) * wide)
            copy = pltpu.make_async_copy(rights[i].at[:, cols], rights_v[i].at[:, cols], right_sems.at[len(right_copies)])
            copy.start()
            right_copies.append((copy, i, n, wide))

    def put(row, depth, col, value):
        for more, offset in zip(added, offsets):
            value = value + more[offset + row:offset + row + depth, col:col + value.shape[1]].astype(F32)
        start = 0
        for out in outs:
            low, high = max(col, start), min(col + value.shape[1], start + out.shape[1])
            if low < high:
                out[row:row + depth, low - start:high - start] = value[:, low - col:high - col].astype(out.dtype)
            start += out.shape[1]

    deep = min(share, 256)
    first_col = 0
    for copy, i, n, wide in right_copies:
        copy.wait()
        for b in range(blocks):
            if n == 0:
                left_copies[i * blocks + b].wait()
            for m in range(share // deep):
                value = lax.dot_general(
                    lefts_v[i][b, :, m * deep:(m + 1) * deep], rights_v[i][:, n * wide:(n + 1) * wide],
                    (((0,), (0,)), ((), ())), preferred_element_type=F32,
                )
                put(b * share + m * deep, deep, first_col, value)
        first_col += wide
    if extras:
        for b in range(blocks):
            put(b * share, share, first_col, extras[0][pl.ds(pl.multiple_of(meta[spots[b]] * share, 8), share), :])


def products(share, spots, meta, lefts, rights, extra, added, dtype, gates, widths, cost):
    vmem = pl.BlockSpec(memory_space=pltpu.VMEM)
    hbm = pl.BlockSpec(memory_space=pltpu.HBM)
    count = len(spots)
    if share % 128:
        blocks = [[lax.dynamic_slice_in_dim(left, meta[spot] * share, share, 1) for spot in spots] for left in lefts]
        if count > 1:
            parts = [
                products(
                    share, spots[b:b + 1], meta, lefts, rights, extra, [(more, at + b * share) for more, at in added], dtype,
                    gates, widths, cost,
                )
                for b in range(count)
            ]
            return [jnp.concatenate(part, axis=0) for part in zip(*parts)]
        lefts = [block[0] for block in blocks]
    depth = lefts[0].shape[0]
    extras = [] if extra is None else [extra]
    total = sum(right.shape[1] for right in rights) + sum(more.shape[1] for more in extras)
    return pl.pallas_call(
        functools.partial(product_kernel, len(lefts), tuple(at for unused, at in added), len(gates), share, spots),
        out_shape=[jax.ShapeDtypeStruct((count * share, width), dtype) for width in widths or [total]],
        in_specs=[pl.BlockSpec(memory_space=pltpu.SMEM)] + [pl.BlockSpec(memory_space=pl.ANY)] * len(gates)
        + [hbm] * (2 * len(lefts)) + [vmem] * (len(extras) + len(added)),
        out_specs=[vmem] * len(widths or [total]),
        scratch_shapes=[pltpu.VMEM((count, depth, share), BF16) for _ in lefts]
        + [pltpu.VMEM(right.shape, BF16) for right in rights]
        + [pltpu.SemaphoreType.DMA((len(lefts) * count,)), pltpu.SemaphoreType.DMA((8,))],
        compiler_params=pltpu.CompilerParams(vmem_limit_bytes=24 * MIB),
        cost_estimate=pl.CostEstimate(flops=cost, bytes_accessed=1024, transcendentals=0),
        name="products",
    )(
        meta, *gates, *map(in_hbm, lefts), *map(in_hbm, rights), *extras,
        *(more for more, unused in added),
    )


def add_kernel(offset, kept, come, *outs):
    start = 0
    for out in outs:
        cols = slice(start, start + out.shape[1])
        out[...] = (kept[offset:offset + out.shape[0], cols].astype(F32) + come[:, cols].astype(F32)).astype(out.dtype)
        start += out.shape[1]


def add(kept, offset, come, dtype, widths):
    vmem = pl.BlockSpec(memory_space=pltpu.VMEM)
    return pl.pallas_call(
        functools.partial(add_kernel, offset),
        out_shape=[jax.ShapeDtypeStruct((come.shape[0], width), dtype) for width in widths or [come.shape[1]]],
        in_specs=[vmem, vmem],
        out_specs=[vmem] * len(widths or [1]),
        compiler_params=pltpu.CompilerParams(vmem_limit_bytes=4 * MIB),
        cost_estimate=pl.CostEstimate(flops=10**11, bytes_accessed=1024, transcendentals=0),
        name="add",
    )(kept, come)


class RowSums:
    def __init__(self, meta, spot, lefts, rights, extra=None):
        self.meta, self.spot, self.lefts, self.rights, self.extra = meta, spot, lefts, rights, extra
        self.share = lefts[0].shape[1] // lax.axis_size("dp")

    def blocks(self, steps, half, gates, added, dtype, cost):
        spots = [self.spot + 2 * step + half for step in steps]
        return products(self.share, spots, self.meta, self.lefts, self.rights, self.extra, added, dtype, gates, None, cost)

    def other(self, steps, gates=(), cost=LIGHT):
        return self.blocks(steps, 1, gates, [], BF16, cost)[0]

    def own(self, steps, gates, added, dtype=BF16, cost=LIGHT):
        return self.blocks(steps, 0, gates, added, dtype, cost)[0]


def keep_last_kernel(rows, spot, meta, incoming, unused, gbs, sem):
    @pl.when(meta[spot] == 1)
    def _():
        at = pl.ds(pl.multiple_of(meta[spot + 1] * rows, rows), rows)
        copy = pltpu.make_async_copy(incoming, gbs.at[at], sem)
        copy.start()
        copy.wait()


def keep_last(spot, meta, incoming, gbs):
    anywhere = pl.BlockSpec(memory_space=pltpu.HBM)
    return pl.pallas_call(
        functools.partial(keep_last_kernel, incoming.shape[0], spot),
        out_shape=pltpu.HBM(gbs.shape, gbs.dtype),
        in_specs=[pl.BlockSpec(memory_space=pltpu.SMEM), pl.BlockSpec(memory_space=pl.ANY), anywhere],
        out_specs=anywhere,
        input_output_aliases={2: 0},
        scratch_shapes=[pltpu.SemaphoreType.DMA],
        compiler_params=pltpu.CompilerParams(vmem_limit_bytes=2 * MIB),
        name="keep_last",
    )(meta, incoming, gbs)


def body(
    tokens, lengths, gain_attn, w_query, w_key, w_value, w_out, gain_ffn, w_up, w_down, cotangent
):
    micro, row_len, width = tokens.shape
    size = w_key.shape[2]
    heads = w_query.shape[2] // size
    ffn = w_up.shape[2]
    count = micro * row_len
    sections = lax.axis_size("section")
    place = lax.axis_index("section")
    gains = [gain_attn, gain_ffn]
    given = [w_query[0], w_key[0], w_value[0], w_out[0], w_up[0], w_down[0]]
    weights = gains
    token_rows = tokens.reshape(count, width)
    cotangent_rows = cotangent.reshape(count, width)
    segments = lengths.shape[2]

    def empty(*shape, dtype=BF16):
        return pltpu.HBM(shape, dtype)

    def meta_of(tick, chunks, rank, order):
        step = tick - SKEW * rank
        active = (step >= 0) & (step < chunks)
        return [active, order(jnp.clip(step, 0, chunks - 1)), rank == 0]

    def hop(block, tick, chunks, rank_of, shift):
        route = [
            (s, s + shift)
            for s in range(sections)
            if 0 <= s + shift < sections and 0 <= tick - SKEW * rank_of(s) < chunks
        ]
        return lax.ppermute(block, "section", route) if route else None

    fwd_geometry = (FWD_ROWS, row_len, heads, size, segments)
    fwd_chunks = count // FWD_ROWS
    fwd_ticks = fwd_chunks + SKEW * (sections - 1)
    bwd_geometry = (BWD_ROWS, row_len, heads, size, segments)
    bwd_chunks = count // BWD_ROWS
    bwd_ticks = bwd_chunks + SKEW * (sections - 1)
    parts = row_len // BWD_ROWS
    chips = lax.axis_size("dp") // 2
    core = lax.axis_index("dp") % 2
    meta = []
    for tick in range(fwd_ticks):
        meta += meta_of(tick, fwd_chunks, place, lambda step: step)
    for tick in range(bwd_ticks):
        meta += meta_of(
            tick, bwd_chunks, sections - 1 - place, lambda step: step // parts * parts + parts - 1 - step % parts
        )
    for step in range(chips):
        meta += [dest_chip(step) * 2 + core, dest_chip(step) * 2 + 1 - core]
    blocks_spot = 3 * (fwd_ticks + bwd_ticks)
    lengths_spot = len(meta)
    meta = jnp.concatenate([jnp.stack([jnp.asarray(entry, jnp.int32) for entry in meta]), lengths.reshape(-1)])
    saved = [
        empty(count, width), empty(count, width), empty(count, heads * size), empty(count, size), empty(count, size),
        empty(micro, size, row_len), empty(micro, size, row_len), empty(count, heads * size),
        empty(count, width, dtype=F32), empty(count, width), empty(count, ffn), empty(count, ffn),
        empty(count, size, dtype=F32), empty(count, width),
    ]
    saved = unwritten(saved)
    received = {}
    nothing = jnp.zeros((FWD_ROWS, width), BF16)
    for tick in range(fwd_ticks):
        incoming = received.pop(tick - SKEW, None)
        at_work = [tick - SKEW * s for s in range(sections) if 0 <= tick - SKEW * s < fwd_chunks]
        places = sorted({chunk % (row_len // FWD_ROWS) for chunk in at_work})
        out, saved, loads = forward_chunk(
            fwd_geometry, places, (3 * tick, lengths_spot), meta, token_rows, nothing if incoming is None else incoming, weights, saved,
            None if tick else given,
        )
        weights = weights + loads
        received[tick] = hop(out, tick, fwd_chunks, lambda s: s, 1)

    kept = dict(zip(FWD_SAVED, saved))
    layer_outs = kept["outs"]
    needed = [kept[name] for name in ("hs", "qs", "ks", "kts", "vts", "mids", "slopes", "lses")]
    saved = unwritten([
        empty(count, width), empty(count, ffn), empty(count, width), empty(count, (heads + 2) * size),
        empty(count, width), empty(bwd_chunks, 16, width, dtype=F32), empty(2 * size, row_len, dtype=F32),
    ])
    received = {}
    nothing = jnp.zeros((BWD_ROWS, width), BF16)
    down_sums = None
    for tick in range(bwd_ticks):
        spot = 3 * (fwd_ticks + tick)
        static_place = parts - 1 - tick % parts
        incoming = received.pop(tick - SKEW, None)
        if incoming is None:
            incoming = nothing
        if tick == bwd_ticks - 1:
            gbs = keep_last(spot, meta, incoming, saved[0])
            down_sums = RowSums(meta, blocks_spot, [kept["acts"]], [gbs])
            swapped = swap_cores(down_sums.other([0]))
            first_total = down_sums.own([0], (), [(swapped, 0)])
            down_ring = next_chip(first_total)
            ready = down_sums.other([1], [first_total])
            swapped = swap_cores(ready)
            out, *rest = backward_chunk(
                bwd_geometry, True, static_place, (spot, lengths_spot), meta, cotangent_rows, incoming, needed, gains + given, saved[1:],
                [first_total, ready],
            )
            saved = [gbs] + rest
            continue
        out, *saved = backward_chunk(
            bwd_geometry, False, static_place, (spot, lengths_spot), meta, cotangent_rows, incoming, needed, weights, saved
        )
        received[tick] = hop(out, tick, bwd_chunks, lambda s: sections - 1 - s, -1)
    done = dict(zip(BWD_SAVED, saved))

    gains = jnp.sum(done["gains"].reshape(bwd_chunks, 2, 8, width), axis=(0, 2))
    gains = jnp.pad(gains.T, ((0, 0), (0, 128 - gains.shape[0])))
    rest_sums = RowSums(
        meta, blocks_spot, [kept["n2s"], kept["n1s"], kept["os"]], [done["dus"], done["dqkvs"], done["gms"]], gains
    )
    later = list(range(1, chips))
    widths = [ffn, heads * size, size, size, width, 128]

    rest_other = rest_sums.other([0])
    down = down_sums.own([1], [rest_other], [(swapped, 0), (down_ring, 0)], BF16 if chips > 2 else F32)
    if chips > 2:
        down_ring = next_chip(down)
    swapped = swap_cores(rest_other)
    down_others = down_sums.other(later[1:], [down]) if chips > 2 else None
    rest = rest_sums.own([0], [down] if down_others is None else [down_others], [(swapped, 0)], cost=HEAVY)
    rest_ring = next_chip(rest)
    if chips > 2:
        down_swapped = swap_cores(down_others)
    if chips > 2:
        down_kept = down_sums.own(later[1:], [rest], [(down_swapped, 0)], cost=HEAVY)
    rest_others = rest_sums.other(later, [rest, down_ring], cost=HEAVY)
    rest_swapped = swap_cores(rest_others)
    rest_kept = None
    for step in range(1, chips):
        if step + 1 < chips:
            last = step + 1 == chips - 1
            down = add(down_kept, (step - 1) * down_sums.share, down_ring, F32 if last else BF16, None)[0]
            if not last:
                down_ring = next_chip(down)
        if rest_kept is None:
            rest_kept = rest_sums.own(later, [down], [(rest_swapped, 0)], cost=HEAVY)
        last = step == chips - 1
        rest = add(
            rest_kept, (step - 1) * rest_sums.share, rest_ring, F32 if last else BF16, widths if last else None
        )
        if not last:
            rest_ring = next_chip(rest[0])
    up, query, key, value, out, gains = rest
    shares = (gains[:, 0], query, key, value, out, gains[:, 1], up, down)
    shape = (1, micro, row_len, width)
    return (layer_outs.reshape(shape), done["igs"].reshape(shape)) + tuple(share[None] for share in shares)


def solution(mesh):
    return jax.shard_map(
        body,
        mesh=mesh,
        in_specs=(
            P(None, "dp", None),
            P(None, "dp", None),
            P("section", None),
            P("section", None, None),
            P("section", None, None),
            P("section", None, None),
            P("section", None, None),
            P("section", None),
            P("section", None, None),
            P("section", None, None),
            P(None, "dp", None),
        ),
        out_specs=(
            P("section", None, "dp", None),
            P("section", None, "dp", None),
            P("section", "dp"),
            P("section", "dp", None),
            P("section", "dp", None),
            P("section", "dp", None),
            P("section", "dp", None),
            P("section", "dp"),
            P("section", "dp", None),
            P("section", "dp", None),
        ),
        check_vma=False,
    )
```

```python
import functools

import jax
import jax.numpy as jnp
from jax import lax
from jax.experimental import pallas as pl
from jax.experimental.pallas import tpu as pltpu
from jax.sharding import PartitionSpec as P

NORM_EPS = 1e-06
MASKED = -1e30
LOG2E = 1.4426950408889634
FWD_ROWS = 128
BWD_ROWS = 256
FFN_TILE = 2048
BWD_TILE = 2048
SKEW = 2
FWD_HEADS = 8
BWD_HEADS = 2
NORM_BLOCK = 128
NORM_UNROLL = 2
SOFTMAX_BLOCK = 128
SOFTMAX_UNROLL = 2
SIDE_TILE = 512
MIB = 1 << 20
GAIN_COLS = 128
LIGHT = 5 * 10**9
HEAVY = 10**11

BF16 = jnp.bfloat16
F32 = jnp.float32


def in_hbm(array):
    return pltpu.with_memory_space_constraint(array, pltpu.HBM)


def in_vmem(array):
    return pltpu.with_memory_space_constraint(array, pltpu.VMEM)


def dot(left, right):
    return jnp.dot(left, right, preferred_element_type=F32)


def dot_t(left, right):
    return lax.dot_general(left, right, (((1,), (1,)), ((), ())), preferred_element_type=F32)


def inverse_rms(rows):
    return lax.rsqrt(jnp.mean(rows * rows, axis=-1, keepdims=True) + NORM_EPS)


def gelu_parts(u):
    t = pl.reciprocal(1.0 + jnp.abs(u) * 0.23164190, approx=True)
    bell = jnp.exp2(u * u * (-0.5 * LOG2E))
    poly = t * (0.127414796 + t * (-0.142248368 + t * (0.7107068705 + t * (-0.7265760135 + t * 0.5307027145))))
    tail = poly * bell
    cdf = jnp.where(u >= 0, 1.0 - tail, tail)
    return u * cdf, cdf + u * bell * 0.3989422804014327


def each_block(rows, block, work, unroll=1):
    def step(i, unused):
        work(pl.ds(pl.multiple_of(i * block, block), block))
        return unused

    lax.fori_loop(0, rows // block, step, 0, unroll=unroll)


def weight_copies(sources, targets, sems):
    w_query, w_key, w_value, w_out, w_up, w_down = sources
    w_query_v, w_kv_v, w_out_v, w_up_v, w_down_v = targets
    size = w_key.shape[1]
    half = w_up.shape[1] // 2
    low, high = slice(0, half), slice(half, 2 * half)
    pieces = {
        "query": (w_query, w_query_v),
        "key": (w_key, w_kv_v.at[:, :size]),
        "value": (w_value, w_kv_v.at[:, size:]),
        "out": (w_out, w_out_v),
        "up0": (w_up.at[:, low], w_up_v.at[:, low]),
        "up1": (w_up.at[:, high], w_up_v.at[:, high]),
        "down0": (w_down.at[low, :], w_down_v.at[low, :]),
        "down1": (w_down.at[high, :], w_down_v.at[high, :]),
    }
    return {name: pltpu.make_async_copy(*piece, sems.at[i]) for i, (name, piece) in enumerate(pieces.items())}


FWD_LOADS = ("query", "key", "value", "out", "up0", "up1", "down0", "down1")
BWD_LOADS = ("down0", "up0", "down1", "up1", "out", "query", "key", "value")


def position_bias(meta, spot, count, first_row, rows, length):
    place = first_row + lax.broadcasted_iota(jnp.int32, (rows, 1), 0)
    start = jnp.zeros((rows, 1), jnp.int32)
    end = 0
    for i in range(count - 1):
        end = end + meta[spot + i]
        start = jnp.where(place >= end, end, start)
    start = jnp.where(place >= end, place, start)
    own = first_row + lax.broadcasted_iota(jnp.int32, (rows, length), 0)
    other = lax.broadcasted_iota(jnp.int32, (rows, length), 1)
    return jnp.where((other >= start) & (other <= own), 0.0, MASKED)


def forward_kernel(geometry, loading, places, spots, meta, tokens, incoming, gain_attn, gain_ffn, *refs):
    rows, row_len, heads, size, segments = geometry
    spot, lengths_spot = spots
    if loading:
        sources, refs = refs[:6], refs[6:]
        load_sems = refs[-1]
        w_query, w_kv, w_out, w_up, w_down = refs[2 * len(FWD_SAVED) + 1:2 * len(FWD_SAVED) + 6]
        refs = refs[:2 * len(FWD_SAVED) + 1] + refs[2 * len(FWD_SAVED) + 6:-1]
        weight_loads = weight_copies(sources, (w_query, w_kv, w_out, w_up, w_down), load_sems)
        for name in FWD_LOADS:
            weight_loads[name].start()
    else:
        w_query, w_kv, w_out, w_up, w_down = refs[:5]
        refs = refs[5:]

    def loaded(*names):
        for name in names if loading else ():
            weight_loads[name].wait()

    saved = refs[len(FWD_SAVED):2 * len(FWD_SAVED) + 1]
    out, hs, n1s, qs, ks, vs, kts, vts, os_, mids, n2s, acts, slopes, lses, outs = saved
    (h_v, n1_v, q_v, k_v, v_v, kt_v, vt_v, o_v, mid_v, n2_v, act_v, slope_v, lse_v, out_v, bias_v, total_v, s_v, p_v, sems) = (
        refs[2 * len(FWD_SAVED) + 1:]
    )
    parts = row_len // rows
    active, chunk, first = meta[spot], meta[spot + 1], meta[spot + 2]
    width = heads * size
    scale = size**-0.5 * LOG2E

    @pl.when(active == 0)
    def _():
        loaded(*FWD_LOADS)

    @pl.when(active == 1)
    def _():
        row = chunk // parts
        place = chunk % parts
        at = pl.ds(pl.multiple_of(chunk * rows, rows), rows)
        within = pl.ds(pl.multiple_of(place * rows, rows), rows)
        whole = pl.ds(pl.multiple_of(row * row_len, row_len), row_len)

        @pl.when(first == 1)
        def _():
            pltpu.make_async_copy(tokens.at[at], h_v, sems.at[0]).start()

        load_v = pltpu.make_async_copy(vs.at[whole], v_v, sems.at[1])
        load_kt = pltpu.make_async_copy(kts.at[row], kt_v, sems.at[2])
        load_v.start()
        load_kt.start()
        pending = []

        def keep(source, target, slot):
            copy = pltpu.make_async_copy(source, target, sems.at[slot])
            copy.start()
            pending.append(copy)

        @pl.when(first == 1)
        def _():
            pltpu.make_async_copy(tokens.at[at], h_v, sems.at[0]).wait()

        @pl.when(first == 0)
        def _():
            h_v[...] = incoming[...]

        keep(h_v, hs.at[at], 3)

        def norm_attn(block):
            h = h_v[block, :].astype(F32)
            n1_v[block, :] = (h * inverse_rms(h) * gain_attn[...].astype(F32)).astype(BF16)

        each_block(rows, NORM_BLOCK, norm_attn, rows // NORM_BLOCK)
        keep(n1_v, n1s.at[at], 4)
        loaded("query", "key", "value")
        kv = dot(n1_v[...], w_kv[...]).astype(BF16)
        q_v[...] = dot(n1_v[...], w_query[...]).astype(BF16)
        k_v[...] = kv[:, :size]
        keep(k_v, ks.at[at], 5)
        keep(q_v, qs.at[at], 6)
        load_v.wait()
        load_kt.wait()
        v_v[within, :] = kv[:, size:]
        kt_v[:, within] = kv[:, :size].T
        vt_v[...] = kv[:, size:].T
        keep(v_v.at[within], vs.at[at], 7)
        keep(kt_v.at[:, within], kts.at[row, :, within], 8)
        keep(vt_v, vts.at[row, :, within], 9)

        lse_v[...] = jnp.zeros((rows, size), F32)

        def attend(static_place):
            length = (static_place + 1) * rows
            lane = lax.broadcasted_iota(jnp.int32, (SOFTMAX_BLOCK, size), 1)
            bias_v[:, :length] = position_bias(
                meta, lengths_spot + row * segments, segments, static_place * rows, rows, length
            )

            def some_heads(step, carry):
                group = [step * FWD_HEADS + i for i in range(FWD_HEADS)]
                for i, head in enumerate(group):
                    cols = pl.ds(pl.multiple_of(head * size, size), size)
                    s_v[i, :, :length] = dot(q_v[:, cols], kt_v[:, :length])
                for i, head in enumerate(group):
                    cols = pl.ds(pl.multiple_of(head * size, size), size)

                    def soften(block, i=i, head=head):
                        scores = s_v[i, block, :length] * scale + bias_v[block, :length]
                        top = jnp.max(scores, axis=1, keepdims=True)
                        weights = jnp.exp2(scores - top)
                        total = jnp.sum(weights, axis=1, keepdims=True)
                        p_v[i, block, :length] = (weights * (1.0 / total)).astype(BF16)
                        lse_v[block, :] = jnp.where(lane == head, top + jnp.log2(total), lse_v[block, :])

                    each_block(rows, SOFTMAX_BLOCK, soften, rows // SOFTMAX_BLOCK)
                    o_v[:, cols] = dot(p_v[i, :, :length], v_v[:length, :]).astype(BF16)
                return carry

            lax.fori_loop(0, heads // FWD_HEADS, some_heads, 0)

        for static_place in places:
            if len(places) == 1:
                attend(static_place)
            else:
                pl.when(place == static_place)(functools.partial(attend, static_place))

        keep(lse_v, lses.at[at], 10)
        keep(o_v, os_.at[at], 11)
        loaded("out")
        total_v[...] = dot(o_v[...], w_out[...])

        def norm_ffn(block):
            mid = h_v[block, :].astype(F32) + total_v[block, :]
            mid_v[block, :] = mid
            total_v[block, :] = mid
            n2_v[block, :] = (mid * inverse_rms(mid) * gain_ffn[...].astype(F32)).astype(BF16)

        each_block(rows, NORM_BLOCK, norm_ffn, rows // NORM_BLOCK)
        keep(mid_v, mids.at[at], 12)
        keep(n2_v, n2s.at[at], 13)
        ffn = w_up.shape[1]
        tile = min(FFN_TILE, ffn)


        def columns(f):
            return pl.ds(pl.multiple_of(f * tile, tile), tile)

        def rise(f):
            return dot(n2_v[...], w_up[:, columns(f)])

        def bend(f, u):
            act, slope = gelu_parts(u)
            act_v[:, columns(f)] = act.astype(BF16)
            slope_v[:, columns(f)] = slope.astype(BF16)
            pltpu.make_async_copy(act_v.at[:, columns(f)], acts.at[at, columns(f)], sems.at[14]).start()
            pltpu.make_async_copy(slope_v.at[:, columns(f)], slopes.at[at, columns(f)], sems.at[15]).start()

        def fall(f):
            return dot(act_v[:, columns(f)], w_down[columns(f), :])

        def both(f, carry):
            u = rise(f)
            part = fall(f - 1)
            bend(f, u)
            total_v[...] += part
            return carry

        loaded("up0")
        bend(0, rise(0))
        loaded("up1", "down0")
        lax.fori_loop(1, ffn // tile, both, 0)
        loaded("down1")
        total_v[...] += fall(ffn // tile - 1)
        total = total_v[...]
        pending.append(pltpu.make_async_copy(act_v, acts.at[at], sems.at[14]))
        pending.append(pltpu.make_async_copy(slope_v, slopes.at[at], sems.at[15]))
        result = total.astype(BF16)
        out[...] = result
        out_v[...] = result
        keep(out_v, outs.at[at], 16)
        for copy in pending:
            copy.wait()


FWD_SAVED = ("hs", "n1s", "qs", "ks", "vs", "kts", "vts", "os", "mids", "n2s", "acts", "slopes", "lses", "outs")


def forward_chunk(geometry, places, spots, meta, tokens, incoming, weights, saved, given=None):
    rows, row_len, heads, size, unused = geometry
    gain_attn, gain_ffn, *matrices = weights
    loading = given is not None
    width = tokens.shape[1]
    ffn = (given[4] if loading else matrices[3]).shape[1]
    vmem = pl.BlockSpec(memory_space=pltpu.VMEM)
    hbm = pl.BlockSpec(memory_space=pltpu.HBM)
    loads = [pltpu.VMEM(shape, BF16) for shape in weight_shapes(given)] if loading else []
    operands = list(map(in_hbm, given)) if loading else list(map(in_vmem, matrices))
    lead = 5 + len(operands)
    flops = 2 * rows * (2 * width * heads * size + 2 * width * size + 2 * width * ffn + row_len * heads * size)
    out, *rest = pl.pallas_call(
        functools.partial(forward_kernel, geometry, loading, places, spots),
        out_shape=[jax.ShapeDtypeStruct((rows, width), BF16)]
        + [pltpu.HBM(array.shape, array.dtype) for array in saved] + loads,
        in_specs=[pl.BlockSpec(memory_space=pltpu.SMEM), hbm, vmem, vmem, vmem]
        + [hbm if loading else vmem] * len(operands) + [hbm] * len(saved),
        out_specs=[vmem] + [hbm] * len(saved) + [vmem] * len(loads),
        input_output_aliases={lead + i: 1 + i for i in range(len(saved))},
        scratch_shapes=[
            pltpu.VMEM((rows, width), BF16),
            pltpu.VMEM((rows, width), BF16),
            pltpu.VMEM((rows, heads * size), BF16),
            pltpu.VMEM((rows, size), BF16),
            pltpu.VMEM((row_len, size), BF16),
            pltpu.VMEM((size, row_len), BF16),
            pltpu.VMEM((size, rows), BF16),
            pltpu.VMEM((rows, heads * size), BF16),
            pltpu.VMEM((rows, width), F32),
            pltpu.VMEM((rows, width), BF16),
            pltpu.VMEM((rows, ffn), BF16),
            pltpu.VMEM((rows, ffn), BF16),
            pltpu.VMEM((rows, size), F32),
            pltpu.VMEM((rows, width), BF16),
            pltpu.VMEM((rows, row_len), F32),
            pltpu.VMEM((rows, width), F32),
            pltpu.VMEM((FWD_HEADS, rows, row_len), F32),
            pltpu.VMEM((FWD_HEADS, rows, row_len), BF16),
            pltpu.SemaphoreType.DMA((17,)),
        ]
        + [pltpu.SemaphoreType.DMA((8,))] * loading,
        compiler_params=pltpu.CompilerParams(vmem_limit_bytes=12 * MIB),
        cost_estimate=pl.CostEstimate(flops=flops, bytes_accessed=8 * MIB, transcendentals=0),
        name="forward_chunk",
    )(meta, in_hbm(tokens), in_vmem(incoming), gain_attn, gain_ffn, *operands, *saved)
    return out, rest[:len(saved)], rest[len(saved):]


def weight_shapes(given):
    w_query, w_key, w_value, w_out, w_up, w_down = given
    return w_query.shape, (w_key.shape[0], 2 * w_key.shape[1]), w_out.shape, w_up.shape, w_down.shape


BWD_SAVED = ("gbs", "dus", "gms", "dqkvs", "igs", "gains", "carry")


def norm_backward(rows, gain, upstream):
    inverse = inverse_rms(rows)
    unit = rows * inverse
    steered = upstream * gain
    grad = inverse * (steered - unit * jnp.mean(steered * unit, axis=-1, keepdims=True))
    return grad, jnp.sum((upstream * unit).reshape(-1, 8, rows.shape[1]), axis=0)


def backward_kernel(
    geometry, last_call, gates, static_place, spots, meta, cotangent, incoming, hs, qs, ks, kts, vts, mids, slopes, lses,
    gain_attn, gain_ffn, *refs,
):
    rows, row_len, heads, size, segments = geometry
    spot, lengths_spot = spots
    if last_call:
        sources, refs = refs[:6], refs[6:]
        w_query, w_kv, w_out, w_up, w_down, load_sems = refs[-6:]
        refs = refs[:-6]
        weight_loads = weight_copies(sources, (w_query, w_kv, w_out, w_up, w_down), load_sems)
    else:
        w_query, w_kv, w_out, w_up, w_down = refs[:5]
        refs = refs[5:]

    def loaded(*names):
        for name in names if last_call else ():
            weight_loads[name].wait()

    refs = refs[gates:]
    count = len(BWD_SAVED) - last_call
    out, *gbs, dus, gms, dqkvs, igs, gains, carry = refs[count:2 * count + 1]
    (g_v, h_v, q_v, k_v, kt_v, vt_v, mid_v, slope_v, lse_v, du_v, gm_v, do_v, dqkv_v, ig_v, gain_v, carry_v,
     bias_v, total_v, s_v, dp_v, p_v, ds_v, sems) = refs[2 * count + 1:]
    parts = row_len // rows
    active, chunk, first = meta[spot], meta[spot + 1], meta[spot + 2]
    scale = size**-0.5
    width = heads * size

    @pl.when(active == 1)
    def _():
        row = chunk // parts
        at = pl.ds(pl.multiple_of(chunk * rows, rows), rows)
        whole = pl.ds(pl.multiple_of(row * row_len, row_len), row_len)

        @pl.when(first == 1)
        def _():
            pltpu.make_async_copy(cotangent.at[at], g_v, sems.at[0]).start()

        loads = [
            pltpu.make_async_copy(source, target, sems.at[1 + i])
            for i, (source, target) in enumerate((
                (slopes.at[at], slope_v),
                (mids.at[at], mid_v),
                (qs.at[at], q_v),
                (lses.at[at], lse_v),
                (kts.at[row], kt_v),
                (vts.at[row], vt_v),
                (ks.at[whole], k_v),
                (carry, carry_v),
                (hs.at[at], h_v),
            ))
        ]
        for load in loads[:1]:
            load.start()
        for name in BWD_LOADS[:2] if last_call else ():
            weight_loads[name].start()
        for load in loads[1:]:
            load.start()
        for name in BWD_LOADS[2:] if last_call else ():
            weight_loads[name].start()
        pending = []

        def keep(source, target, slot):
            copy = pltpu.make_async_copy(source, target, sems.at[slot])
            copy.start()
            pending.append(copy)

        length = (static_place + 1) * rows
        bias_v[:, :length] = position_bias(
            meta, lengths_spot + row * segments, segments, static_place * rows, rows, length
        )
        @pl.when(first == 1)
        def _():
            pltpu.make_async_copy(cotangent.at[at], g_v, sems.at[0]).wait()

        @pl.when(first == 0)
        def _():
            g_v[...] = incoming[...]

        if not last_call:
            keep(g_v, gbs[0].at[at], 10)
        loads[0].wait()
        ffn = w_up.shape[1]
        tile = min(BWD_TILE, ffn)

        def rise(f):
            cols = pl.ds(pl.multiple_of(f * tile, tile), tile)
            return dot_t(g_v[...], w_down[cols, :])

        def bend(f, da):
            cols = pl.ds(pl.multiple_of(f * tile, tile), tile)
            du_v[:, cols] = (slope_v[:, cols].astype(F32) * da).astype(BF16)

        def fall(f):
            cols = pl.ds(pl.multiple_of(f * tile, tile), tile)
            return dot_t(du_v[:, cols], w_up[:, cols])

        def both(f, carry):
            da = rise(f)
            part = fall(f - 1)
            bend(f, da)
            total_v[...] = jnp.where(f == 1, part, total_v[...] + part)
            return carry

        loaded("down0")
        bend(0, rise(0))
        loaded("up0", "down1")
        lax.fori_loop(1, ffn // tile, both, 0)
        loaded("up1")
        total_v[...] += fall(ffn // tile - 1)
        keep(du_v, dus.at[at], 11)
        loads[1].wait()
        gain_v[...] = jnp.zeros(gain_v.shape, F32)

        def norm_ffn(block):
            dv, dgain = norm_backward(mid_v[block, :], gain_ffn[...].astype(F32), total_v[block, :])
            dmid = g_v[block, :].astype(F32) + dv
            mid_v[block, :] = dmid
            gm_v[block, :] = dmid.astype(BF16)
            gain_v[8:, :] += dgain

        each_block(rows, NORM_BLOCK, norm_ffn, rows // NORM_BLOCK)
        keep(gm_v, gms.at[at], 12)
        loaded("out")
        do_v[...] = dot_t(gm_v[...], w_out[...]).astype(BF16)
        for load in loads[2:8]:
            load.wait()

        if static_place == parts - 1:
            carry_v[...] = jnp.zeros(carry_v.shape, F32)

        def attend():
            lane = lax.broadcasted_iota(jnp.int32, (SOFTMAX_BLOCK, size), 1)

            def some_heads(step, unused):
                group = [step * BWD_HEADS + i for i in range(BWD_HEADS)]
                for i, head in enumerate(group):
                    cols = pl.ds(pl.multiple_of(head * size, size), size)
                    s_v[i, :, :length] = dot(q_v[:, cols], kt_v[:, :length])
                    dp_v[i, :, :length] = dot(do_v[:, cols], vt_v[:, :length])
                for i, head in enumerate(group):
                    cols = pl.ds(pl.multiple_of(head * size, size), size)

                    def steepen(block, i=i, head=head):
                        lse = jnp.sum(jnp.where(lane == head, lse_v[block, :], 0.0), axis=1, keepdims=True)
                        scores = s_v[i, block, :length] * (scale * LOG2E) + bias_v[block, :length]
                        probs = jnp.exp2(scores - lse)
                        p_v[i, block, :length] = probs.astype(BF16)
                        dprobs = dp_v[i, block, :length]
                        mean = jnp.sum(probs * dprobs, axis=1, keepdims=True)
                        ds_v[i, block, :length] = (probs * (dprobs - mean)).astype(BF16)

                    each_block(rows, SOFTMAX_BLOCK, steepen, rows // SOFTMAX_BLOCK)
                    dqkv_v[:, cols] = (dot(ds_v[i, :, :length], k_v[:length, :]) * scale).astype(BF16)
                    carry_v[:size, :length] += dot(q_v[:, cols].T, ds_v[i, :, :length])
                    carry_v[size:, :length] += dot(do_v[:, cols].T, p_v[i, :, :length])
                return unused

            lax.fori_loop(0, heads // BWD_HEADS, some_heads, 0)
            own = slice(length - rows, length)
            dqkv_v[:, width:width + size] = (carry_v[:size, own].T * scale).astype(BF16)
            dqkv_v[:, width + size:] = carry_v[size:, own].T.astype(BF16)

        attend()

        keep(carry_v, carry, 13)
        keep(dqkv_v, dqkvs.at[at], 14)
        loaded("query", "key", "value")
        dn1 = dot_t(dqkv_v[:, :width], w_query[...]) + dot_t(dqkv_v[:, width:], w_kv[...])
        loads[8].wait()
        total_v[...] = dn1

        def norm_attn(block):
            dv, dgain = norm_backward(h_v[block, :].astype(F32), gain_attn[...].astype(F32), total_v[block, :])
            ig_v[block, :] = (mid_v[block, :] + dv).astype(BF16)
            gain_v[:8, :] += dgain

        each_block(rows, NORM_BLOCK, norm_attn, rows // NORM_BLOCK)
        out[...] = ig_v[...]
        keep(ig_v, igs.at[at], 16)
        keep(gain_v, gains.at[chunk], 17)
        for copy in pending:
            copy.wait()


def backward_chunk(geometry, last_call, static_place, spots, meta, cotangent, incoming, kept, weights, saved, gates=()):
    rows, row_len, heads, size, unused = geometry
    gain_attn, gain_ffn, *matrices = weights
    width = cotangent.shape[1]
    ffn = matrices[4 if last_call else 3].shape[1]
    vmem = pl.BlockSpec(memory_space=pltpu.VMEM)
    hbm = pl.BlockSpec(memory_space=pltpu.HBM)
    lead = 3 + len(kept) + len(weights) + len(gates)
    flops = 2 * rows * (2 * width * heads * size + 2 * width * size + 2 * width * ffn + 3 * row_len * heads * size)
    return pl.pallas_call(
        functools.partial(backward_kernel, geometry, last_call, len(gates), static_place, spots),
        out_shape=[jax.ShapeDtypeStruct((rows, width), BF16)]
        + [pltpu.HBM(array.shape, array.dtype) for array in saved],
        in_specs=[pl.BlockSpec(memory_space=pltpu.SMEM), hbm, vmem]
        + [hbm] * len(kept) + [vmem] * 2 + [hbm if last_call else vmem] * len(matrices)
        + [pl.BlockSpec(memory_space=pl.ANY)] * len(gates) + [hbm] * len(saved),
        out_specs=[vmem] + [hbm] * len(saved),
        input_output_aliases={lead + i: 1 + i for i in range(len(saved))},
        scratch_shapes=[
            pltpu.VMEM((rows, width), BF16),
            pltpu.VMEM((rows, width), BF16),
            pltpu.VMEM((rows, heads * size), BF16),
            pltpu.VMEM((row_len, size), BF16),
            pltpu.VMEM((size, row_len), BF16),
            pltpu.VMEM((size, row_len), BF16),
            pltpu.VMEM((rows, width), F32),
            pltpu.VMEM((rows, ffn), BF16),
            pltpu.VMEM((rows, size), F32),
            pltpu.VMEM((rows, ffn), BF16),
            pltpu.VMEM((rows, width), BF16),
            pltpu.VMEM((rows, heads * size), BF16),
            pltpu.VMEM((rows, (heads + 2) * size), BF16),
            pltpu.VMEM((rows, width), BF16),
            pltpu.VMEM((16, width), F32),
            pltpu.VMEM((2 * size, row_len), F32),
            pltpu.VMEM((rows, row_len), F32),
            pltpu.VMEM((rows, width), F32),
            pltpu.VMEM((BWD_HEADS, rows, row_len), F32),
            pltpu.VMEM((BWD_HEADS, rows, row_len), F32),
            pltpu.VMEM((BWD_HEADS, rows, row_len), BF16),
            pltpu.VMEM((BWD_HEADS, rows, row_len), BF16),
            pltpu.SemaphoreType.DMA((18,)),
        ]
        + [pltpu.VMEM(shape, BF16) for shape in (weight_shapes(matrices) if last_call else ())]
        + [pltpu.SemaphoreType.DMA((8,))] * last_call,
        compiler_params=pltpu.CompilerParams(vmem_limit_bytes=(42 if last_call else 20) * MIB),
        cost_estimate=pl.CostEstimate(
            flops=1024 if last_call else flops, bytes_accessed=1024 if last_call else 8 * MIB, transcendentals=0
        ),
        name="backward_chunk",
    )(
        meta, in_hbm(cotangent), in_vmem(incoming), *map(in_hbm, kept), gain_attn, gain_ffn,
        *map(in_hbm if last_call else in_vmem, matrices), *gates, *saved,
    )


def unwritten(shapes):
    return pl.pallas_call(
        lambda *refs: None,
        out_shape=shapes,
        out_specs=[pl.BlockSpec(memory_space=pltpu.HBM)] * len(shapes),
        compiler_params=pltpu.CompilerParams(vmem_limit_bytes=2 * MIB),
        name="unwritten",
    )()


def dest_chip(step):
    chips = lax.axis_size("dp") // 2
    return lax.rem(lax.axis_index("dp") // 2 + 2 * chips - 1 - step, chips)


def swap_cores(block):
    return lax.ppermute(block, "dp", [(i, i ^ 1) for i in range(lax.axis_size("dp"))])


def next_chip(block):
    devices = lax.axis_size("dp")
    return lax.ppermute(block, "dp", [(i, (i + 2) % devices) for i in range(devices)])


def largest_tile(width, most):
    return max(tile for tile in range(128, most + 1, 128) if width % tile == 0)


def product_kernel(pairs, offsets, gates, share, spots, meta, *refs):
    refs = refs[gates:]
    lefts, rights, refs = refs[:pairs], refs[pairs:2 * pairs], refs[2 * pairs:]
    extras = refs[:1] if pairs > 1 else ()
    refs = refs[len(extras):]
    added, refs = refs[:len(offsets)], refs[len(offsets):]
    outs, refs = refs[:len(refs) - 2 * pairs - 2], refs[len(refs) - 2 * pairs - 2:]
    lefts_v, rights_v, left_sems, right_sems = refs[:pairs], refs[pairs:2 * pairs], refs[-2], refs[-1]
    blocks = lefts_v[0].shape[0]
    left_copies, right_copies = [], []
    for i in range(pairs):
        for b in range(blocks):
            source = lefts[i]
            if source.shape[1] != share:
                source = source.at[:, pl.ds(pl.multiple_of(meta[spots[b]] * share, 128), share)]
            left_copies.append(pltpu.make_async_copy(source, lefts_v[i].at[b], left_sems.at[i * blocks + b]))
            left_copies[-1].start()
        wide = largest_tile(rights[i].shape[1], 1280)
        for n in range(rights[i].shape[1] // wide):
            cols = slice(n * wide, (n + 1) * wide)
            copy = pltpu.make_async_copy(rights[i].at[:, cols], rights_v[i].at[:, cols], right_sems.at[len(right_copies)])
            copy.start()
            right_copies.append((copy, i, n, wide))

    def put(row, depth, col, value):
        cols = slice(col, col + value.shape[1])
        if row < outs[0].shape[0]:
            for more, offset in zip(added, offsets):
                value = value + more[offset + row:offset + row + depth, cols].astype(F32)
            outs[0][row:row + depth, cols] = value.astype(outs[0].dtype)
        else:
            row -= outs[0].shape[0]
            outs[1][row:row + depth, cols] = value.astype(outs[1].dtype)

    deep = min(share, 256)
    first_col = 0
    for copy, i, n, wide in right_copies:
        copy.wait()
        for b in range(blocks):
            if n == 0:
                left_copies[i * blocks + b].wait()
            for m in range(share // deep):
                value = lax.dot_general(
                    lefts_v[i][b, :, m * deep:(m + 1) * deep], rights_v[i][:, n * wide:(n + 1) * wide],
                    (((0,), (0,)), ((), ())), preferred_element_type=F32,
                )
                put(b * share + m * deep, deep, first_col, value)
        first_col += wide
    if extras:
        gains = extras[0]
        for b in range(blocks):
            own = gains[...]
            if gains.shape[2] != share:
                own = gains[:, :, pl.ds(pl.multiple_of(meta[spots[b]] * share, 128), share)]
            own = jnp.sum(own, axis=0).reshape(2, 8, share)
            own = jnp.concatenate([jnp.sum(own, axis=1), jnp.zeros((GAIN_COLS - 2, share), F32)], axis=0)
            put(b * share, share, first_col, own.T)


def products(share, spots, meta, lefts, rights, extra, added, dtype, gates, split, cost):
    vmem = pl.BlockSpec(memory_space=pltpu.VMEM)
    hbm = pl.BlockSpec(memory_space=pltpu.HBM)
    count = len(spots)
    if share % 128:
        blocks = [[lax.dynamic_slice_in_dim(left, meta[spot] * share, share, 1) for spot in spots] for left in lefts]
        if count > 1:
            parts = [
                products(
                    share, spots[b:b + 1], meta, lefts, rights, extra,
                    [] if split and b else [(more, at + b * share) for more, at in added], dtype, gates, False, cost,
                )[0]
                for b in range(count)
            ]
            return parts if split else [jnp.concatenate(parts, axis=0)]
        lefts = [block[0] for block in blocks]
        extra = None if extra is None else lax.dynamic_slice_in_dim(extra, meta[spots[0]] * share, share, 2)
    depth = lefts[0].shape[0]
    extras = [] if extra is None else [extra]
    total = sum(right.shape[1] for right in rights) + GAIN_COLS * len(extras)
    return pl.pallas_call(
        functools.partial(product_kernel, len(lefts), tuple(at for unused, at in added), len(gates), share, spots),
        out_shape=[jax.ShapeDtypeStruct((share if split else count * share, total), dtype)] * (2 if split else 1),
        in_specs=[pl.BlockSpec(memory_space=pltpu.SMEM)] + [pl.BlockSpec(memory_space=pl.ANY)] * len(gates)
        + [hbm] * (2 * len(lefts)) + [vmem] * (len(extras) + len(added)),
        out_specs=[vmem] * (2 if split else 1),
        scratch_shapes=[pltpu.VMEM((count, depth, share), BF16) for _ in lefts]
        + [pltpu.VMEM(right.shape, BF16) for right in rights]
        + [pltpu.SemaphoreType.DMA((len(lefts) * count,)), pltpu.SemaphoreType.DMA((8,))],
        compiler_params=pltpu.CompilerParams(vmem_limit_bytes=24 * MIB),
        cost_estimate=pl.CostEstimate(flops=cost, bytes_accessed=1024, transcendentals=0),
        name="products",
    )(
        meta, *gates, *map(in_hbm, lefts), *map(in_hbm, rights), *extras,
        *(more for more, unused in added),
    )


def add_kernel(offset, kept, come, *outs):
    start = 0
    for out in outs:
        cols = slice(start, start + out.shape[1])
        out[...] = (kept[offset:offset + out.shape[0], cols].astype(F32) + come[:, cols].astype(F32)).astype(out.dtype)
        start += out.shape[1]


def add(kept, offset, come, dtype, widths):
    vmem = pl.BlockSpec(memory_space=pltpu.VMEM)
    return pl.pallas_call(
        functools.partial(add_kernel, offset),
        out_shape=[jax.ShapeDtypeStruct((come.shape[0], width), dtype) for width in widths or [come.shape[1]]],
        in_specs=[vmem, vmem],
        out_specs=[vmem] * len(widths or [1]),
        compiler_params=pltpu.CompilerParams(vmem_limit_bytes=4 * MIB),
        cost_estimate=pl.CostEstimate(flops=10**11, bytes_accessed=1024, transcendentals=0),
        name="add",
    )(kept, come)


class RowSums:
    def __init__(self, meta, spot, lefts, rights, extra=None):
        self.meta, self.spot, self.lefts, self.rights, self.extra = meta, spot, lefts, rights, extra
        self.share = lefts[0].shape[1] // lax.axis_size("dp")

    def blocks(self, steps, half, gates, added, dtype, cost):
        spots = [self.spot + 2 * step + half for step in steps]
        return products(self.share, spots, self.meta, self.lefts, self.rights, self.extra, added, dtype, gates, False, cost)

    def other(self, steps, gates=(), cost=LIGHT):
        return self.blocks(steps, 1, gates, [], BF16, cost)[0]

    def own_and_other(self, own_step, other_step, added):
        spots = [self.spot + 2 * own_step, self.spot + 2 * other_step + 1]
        return products(
            self.share, spots, self.meta, self.lefts, self.rights, self.extra, added, BF16, (), True, LIGHT
        )

    def own(self, steps, gates, added, dtype=BF16, cost=LIGHT):
        return self.blocks(steps, 0, gates, added, dtype, cost)[0]


def keep_last_kernel(rows, spot, meta, incoming, unused, gbs, sem):
    @pl.when(meta[spot] == 1)
    def _():
        at = pl.ds(pl.multiple_of(meta[spot + 1] * rows, rows), rows)
        copy = pltpu.make_async_copy(incoming, gbs.at[at], sem)
        copy.start()
        copy.wait()


def keep_last(spot, meta, incoming, gbs):
    anywhere = pl.BlockSpec(memory_space=pltpu.HBM)
    return pl.pallas_call(
        functools.partial(keep_last_kernel, incoming.shape[0], spot),
        out_shape=pltpu.HBM(gbs.shape, gbs.dtype),
        in_specs=[pl.BlockSpec(memory_space=pltpu.SMEM), pl.BlockSpec(memory_space=pl.ANY), anywhere],
        out_specs=anywhere,
        input_output_aliases={2: 0},
        scratch_shapes=[pltpu.SemaphoreType.DMA],
        compiler_params=pltpu.CompilerParams(vmem_limit_bytes=2 * MIB),
        name="keep_last",
    )(meta, incoming, gbs)


def body(
    tokens, lengths, gain_attn, w_query, w_key, w_value, w_out, gain_ffn, w_up, w_down, cotangent
):
    micro, row_len, width = tokens.shape
    size = w_key.shape[2]
    heads = w_query.shape[2] // size
    ffn = w_up.shape[2]
    count = micro * row_len
    sections = lax.axis_size("section")
    place = lax.axis_index("section")
    gains = [gain_attn, gain_ffn]
    given = [w_query[0], w_key[0], w_value[0], w_out[0], w_up[0], w_down[0]]
    weights = gains
    token_rows = tokens.reshape(count, width)
    cotangent_rows = cotangent.reshape(count, width)
    segments = lengths.shape[2]

    def empty(*shape, dtype=BF16):
        return pltpu.HBM(shape, dtype)

    def meta_of(tick, chunks, rank, order):
        step = tick - SKEW * rank
        active = (step >= 0) & (step < chunks)
        return [active, order(jnp.clip(step, 0, chunks - 1)), rank == 0]

    def hop(block, tick, chunks, rank_of, shift):
        route = [
            (s, s + shift)
            for s in range(sections)
            if 0 <= s + shift < sections and 0 <= tick - SKEW * rank_of(s) < chunks
        ]
        return lax.ppermute(block, "section", route) if route else None

    fwd_geometry = (FWD_ROWS, row_len, heads, size, segments)
    fwd_chunks = count // FWD_ROWS
    fwd_ticks = fwd_chunks + SKEW * (sections - 1)
    bwd_geometry = (BWD_ROWS, row_len, heads, size, segments)
    bwd_chunks = count // BWD_ROWS
    bwd_ticks = bwd_chunks + SKEW * (sections - 1)
    parts = row_len // BWD_ROWS
    chips = lax.axis_size("dp") // 2
    core = lax.axis_index("dp") % 2
    meta = []
    for tick in range(fwd_ticks):
        meta += meta_of(tick, fwd_chunks, place, lambda step: step)
    for tick in range(bwd_ticks):
        meta += meta_of(
            tick, bwd_chunks, sections - 1 - place, lambda step: step // parts * parts + parts - 1 - step % parts
        )
    for step in range(chips):
        meta += [dest_chip(step) * 2 + core, dest_chip(step) * 2 + 1 - core]
    blocks_spot = 3 * (fwd_ticks + bwd_ticks)
    lengths_spot = len(meta)
    meta = jnp.concatenate([jnp.stack([jnp.asarray(entry, jnp.int32) for entry in meta]), lengths.reshape(-1)])
    saved = [
        empty(count, width), empty(count, width), empty(count, heads * size), empty(count, size), empty(count, size),
        empty(micro, size, row_len), empty(micro, size, row_len), empty(count, heads * size),
        empty(count, width, dtype=F32), empty(count, width), empty(count, ffn), empty(count, ffn),
        empty(count, size, dtype=F32), empty(count, width),
    ]
    saved = unwritten(saved)
    received = {}
    nothing = jnp.zeros((FWD_ROWS, width), BF16)
    for tick in range(fwd_ticks):
        incoming = received.pop(tick - SKEW, None)
        at_work = [tick - SKEW * s for s in range(sections) if 0 <= tick - SKEW * s < fwd_chunks]
        places = sorted({chunk % (row_len // FWD_ROWS) for chunk in at_work})
        out, saved, loads = forward_chunk(
            fwd_geometry, places, (3 * tick, lengths_spot), meta, token_rows, nothing if incoming is None else incoming, weights, saved,
            None if tick else given,
        )
        weights = weights + loads
        received[tick] = hop(out, tick, fwd_chunks, lambda s: s, 1)

    kept = dict(zip(FWD_SAVED, saved))
    layer_outs = kept["outs"]
    needed = [kept[name] for name in ("hs", "qs", "ks", "kts", "vts", "mids", "slopes", "lses")]
    saved = unwritten([
        empty(count, width), empty(count, ffn), empty(count, width), empty(count, (heads + 2) * size),
        empty(count, width), empty(bwd_chunks, 16, width, dtype=F32), empty(2 * size, row_len, dtype=F32),
    ])
    received = {}
    nothing = jnp.zeros((BWD_ROWS, width), BF16)
    down_sums = None
    for tick in range(bwd_ticks):
        spot = 3 * (fwd_ticks + tick)
        static_place = parts - 1 - tick % parts
        incoming = received.pop(tick - SKEW, None)
        if incoming is None:
            incoming = nothing
        if tick == bwd_ticks - 1:
            gbs = keep_last(spot, meta, incoming, saved[0])
            down_sums = RowSums(meta, blocks_spot, [kept["acts"]], [gbs])
            swapped = swap_cores(down_sums.other([0]))
            first_total, ready = down_sums.own_and_other(0, 1, [(swapped, 0)])
            down_ring = next_chip(first_total)
            swapped = swap_cores(ready)
            out, *rest = backward_chunk(
                bwd_geometry, True, static_place, (spot, lengths_spot), meta, cotangent_rows, incoming, needed, gains + given, saved[1:],
                [first_total, ready],
            )
            saved = [gbs] + rest
            continue
        out, *saved = backward_chunk(
            bwd_geometry, False, static_place, (spot, lengths_spot), meta, cotangent_rows, incoming, needed, weights, saved
        )
        received[tick] = hop(out, tick, bwd_chunks, lambda s: sections - 1 - s, -1)
    done = dict(zip(BWD_SAVED, saved))

    rest_sums = RowSums(
        meta, blocks_spot, [kept["n2s"], kept["n1s"], kept["os"]], [done["dus"], done["dqkvs"], done["gms"]], done["gains"]
    )
    later = list(range(1, chips))
    widths = [ffn, heads * size, size, size, width, 128]

    rest_other = rest_sums.other([0])
    down = down_sums.own([1], [rest_other], [(swapped, 0), (down_ring, 0)], BF16 if chips > 2 else F32)
    if chips > 2:
        down_ring = next_chip(down)
    swapped = swap_cores(rest_other)
    down_others = down_sums.other(later[1:], [down]) if chips > 2 else None
    rest = rest_sums.own([0], [down] if down_others is None else [down_others], [(swapped, 0)], cost=HEAVY)
    rest_ring = next_chip(rest)
    if chips > 2:
        down_swapped = swap_cores(down_others)
    if chips > 2:
        down_kept = down_sums.own(later[1:], [rest], [(down_swapped, 0)], cost=HEAVY)
    rest_others = rest_sums.other(later, [rest, down_ring], cost=HEAVY)
    rest_swapped = swap_cores(rest_others)
    rest_kept = None
    for step in range(1, chips):
        if step + 1 < chips:
            last = step + 1 == chips - 1
            down = add(down_kept, (step - 1) * down_sums.share, down_ring, F32 if last else BF16, None)[0]
            if not last:
                down_ring = next_chip(down)
        if rest_kept is None:
            rest_kept = rest_sums.own(later, [down], [(rest_swapped, 0)], cost=HEAVY)
        last = step == chips - 1
        rest = add(
            rest_kept, (step - 1) * rest_sums.share, rest_ring, F32 if last else BF16, widths if last else None
        )
        if not last:
            rest_ring = next_chip(rest[0])
    up, query, key, value, out, gains = rest
    shares = (gains[:, 0], query, key, value, out, gains[:, 1], up, down)
    shape = (1, micro, row_len, width)
    return (layer_outs.reshape(shape), done["igs"].reshape(shape)) + tuple(share[None] for share in shares)


def solution(mesh):
    return jax.shard_map(
        body,
        mesh=mesh,
        in_specs=(
            P(None, "dp", None),
            P(None, "dp", None),
            P("section", None),
            P("section", None, None),
            P("section", None, None),
            P("section", None, None),
            P("section", None, None),
            P("section", None),
            P("section", None, None),
            P("section", None, None),
            P(None, "dp", None),
        ),
        out_specs=(
            P("section", None, "dp", None),
            P("section", None, "dp", None),
            P("section", "dp"),
            P("section", "dp", None),
            P("section", "dp", None),
            P("section", "dp", None),
            P("section", "dp", None),
            P("section", "dp"),
            P("section", "dp", None),
            P("section", "dp", None),
        ),
        check_vma=False,
    )
```

```python
import functools

import jax
import jax.numpy as jnp
from jax import lax
from jax.experimental import pallas as pl
from jax.experimental.pallas import tpu as pltpu
from jax.sharding import PartitionSpec as P

NORM_EPS = 1e-06
MASKED = -1e30
LOG2E = 1.4426950408889634
FWD_ROWS = 128
BWD_ROWS = 256
FFN_TILE = 2048
BWD_TILE = 2048
SKEW = 2
FWD_HEADS = 8
BWD_HEADS = 4
NORM_BLOCK = 128
NORM_UNROLL = 2
SOFTMAX_BLOCK = 128
SOFTMAX_UNROLL = 2
SIDE_TILE = 512
MIB = 1 << 20
GAIN_COLS = 128
LIGHT = 5 * 10**9
HEAVY = 10**11

BF16 = jnp.bfloat16
F32 = jnp.float32


def in_hbm(array):
    return pltpu.with_memory_space_constraint(array, pltpu.HBM)


def in_vmem(array):
    return pltpu.with_memory_space_constraint(array, pltpu.VMEM)


def dot(left, right):
    return jnp.dot(left, right, preferred_element_type=F32)


def dot_t(left, right):
    return lax.dot_general(left, right, (((1,), (1,)), ((), ())), preferred_element_type=F32)


def inverse_rms(rows):
    return lax.rsqrt(jnp.mean(rows * rows, axis=-1, keepdims=True) + NORM_EPS)


def gelu_parts(u):
    t = pl.reciprocal(1.0 + jnp.abs(u) * 0.23164190, approx=True)
    bell = jnp.exp2(u * u * (-0.5 * LOG2E))
    poly = t * (0.127414796 + t * (-0.142248368 + t * (0.7107068705 + t * (-0.7265760135 + t * 0.5307027145))))
    tail = poly * bell
    cdf = jnp.where(u >= 0, 1.0 - tail, tail)
    return u * cdf, cdf + u * bell * 0.3989422804014327


def each_block(rows, block, work, unroll=1):
    def step(i, unused):
        work(pl.ds(pl.multiple_of(i * block, block), block))
        return unused

    lax.fori_loop(0, rows // block, step, 0, unroll=unroll)


def weight_copies(sources, targets, sems):
    w_query, w_key, w_value, w_out, w_up, w_down = sources
    w_query_v, w_kv_v, w_out_v, w_up_v, w_down_v = targets
    size = w_key.shape[1]
    half = w_up.shape[1] // 2
    low, high = slice(0, half), slice(half, 2 * half)
    pieces = {
        "query": (w_query, w_query_v),
        "key": (w_key, w_kv_v.at[:, :size]),
        "value": (w_value, w_kv_v.at[:, size:]),
        "out": (w_out, w_out_v),
        "up0": (w_up.at[:, low], w_up_v.at[:, low]),
        "up1": (w_up.at[:, high], w_up_v.at[:, high]),
        "down0": (w_down.at[low, :], w_down_v.at[low, :]),
        "down1": (w_down.at[high, :], w_down_v.at[high, :]),
    }
    return {name: pltpu.make_async_copy(*piece, sems.at[i]) for i, (name, piece) in enumerate(pieces.items())}


FWD_LOADS = ("query", "key", "value", "out", "up0", "up1", "down0", "down1")
BWD_LOADS = ("down0", "up0", "down1", "up1", "out", "query", "key", "value")


def position_bias(meta, spot, count, first_row, rows, length):
    place = first_row + lax.broadcasted_iota(jnp.int32, (rows, 1), 0)
    start = jnp.zeros((rows, 1), jnp.int32)
    end = 0
    for i in range(count - 1):
        end = end + meta[spot + i]
        start = jnp.where(place >= end, end, start)
    start = jnp.where(place >= end, place, start)
    own = first_row + lax.broadcasted_iota(jnp.int32, (rows, length), 0)
    other = lax.broadcasted_iota(jnp.int32, (rows, length), 1)
    return jnp.where((other >= start) & (other <= own), 0.0, MASKED)


def forward_kernel(geometry, loading, places, spots, meta, tokens, incoming, gain_attn, gain_ffn, *refs):
    rows, row_len, heads, size, segments = geometry
    spot, lengths_spot = spots
    if loading:
        sources, refs = refs[:6], refs[6:]
        load_sems = refs[-1]
        w_query, w_kv, w_out, w_up, w_down = refs[2 * len(FWD_SAVED) + 1:2 * len(FWD_SAVED) + 6]
        refs = refs[:2 * len(FWD_SAVED) + 1] + refs[2 * len(FWD_SAVED) + 6:-1]
        weight_loads = weight_copies(sources, (w_query, w_kv, w_out, w_up, w_down), load_sems)
        for name in FWD_LOADS:
            weight_loads[name].start()
    else:
        w_query, w_kv, w_out, w_up, w_down = refs[:5]
        refs = refs[5:]

    def loaded(*names):
        for name in names if loading else ():
            weight_loads[name].wait()

    saved = refs[len(FWD_SAVED):2 * len(FWD_SAVED) + 1]
    out, hs, n1s, qs, ks, vs, kts, vts, os_, mids, n2s, acts, slopes, lses, outs = saved
    (h_v, n1_v, q_v, k_v, v_v, kt_v, vt_v, o_v, mid_v, n2_v, act_v, slope_v, lse_v, out_v, bias_v, total_v, s_v, p_v, sems) = (
        refs[2 * len(FWD_SAVED) + 1:]
    )
    parts = row_len // rows
    active, chunk, first = meta[spot], meta[spot + 1], meta[spot + 2]
    width = heads * size
    scale = size**-0.5 * LOG2E

    @pl.when(active == 0)
    def _():
        loaded(*FWD_LOADS)

    @pl.when(active == 1)
    def _():
        row = chunk // parts
        place = chunk % parts
        at = pl.ds(pl.multiple_of(chunk * rows, rows), rows)
        within = pl.ds(pl.multiple_of(place * rows, rows), rows)
        whole = pl.ds(pl.multiple_of(row * row_len, row_len), row_len)

        @pl.when(first == 1)
        def _():
            pltpu.make_async_copy(tokens.at[at], h_v, sems.at[0]).start()

        load_v = pltpu.make_async_copy(vs.at[whole], v_v, sems.at[1])
        load_kt = pltpu.make_async_copy(kts.at[row], kt_v, sems.at[2])
        load_v.start()
        load_kt.start()
        pending = []

        def keep(source, target, slot):
            copy = pltpu.make_async_copy(source, target, sems.at[slot])
            copy.start()
            pending.append(copy)

        @pl.when(first == 1)
        def _():
            pltpu.make_async_copy(tokens.at[at], h_v, sems.at[0]).wait()

        @pl.when(first == 0)
        def _():
            h_v[...] = incoming[...]

        keep(h_v, hs.at[at], 3)

        def norm_attn(block):
            h = h_v[block, :].astype(F32)
            n1_v[block, :] = (h * inverse_rms(h) * gain_attn[...].astype(F32)).astype(BF16)

        each_block(rows, NORM_BLOCK, norm_attn, rows // NORM_BLOCK)
        keep(n1_v, n1s.at[at], 4)
        loaded("query", "key", "value")
        kv = dot(n1_v[...], w_kv[...]).astype(BF16)
        q_v[...] = dot(n1_v[...], w_query[...]).astype(BF16)
        k_v[...] = kv[:, :size]
        keep(k_v, ks.at[at], 5)
        keep(q_v, qs.at[at], 6)
        load_v.wait()
        load_kt.wait()
        v_v[within, :] = kv[:, size:]
        kt_v[:, within] = kv[:, :size].T
        vt_v[...] = kv[:, size:].T
        keep(v_v.at[within], vs.at[at], 7)
        keep(kt_v.at[:, within], kts.at[row, :, within], 8)
        keep(vt_v, vts.at[row, :, within], 9)

        lse_v[...] = jnp.zeros((rows, size), F32)

        def attend(static_place):
            length = (static_place + 1) * rows
            lane = lax.broadcasted_iota(jnp.int32, (SOFTMAX_BLOCK, size), 1)
            bias_v[:, :length] = position_bias(
                meta, lengths_spot + row * segments, segments, static_place * rows, rows, length
            )

            def some_heads(step, carry):
                group = [step * FWD_HEADS + i for i in range(FWD_HEADS)]
                for i, head in enumerate(group):
                    cols = pl.ds(pl.multiple_of(head * size, size), size)
                    s_v[i, :, :length] = dot(q_v[:, cols], kt_v[:, :length])
                for i, head in enumerate(group):
                    cols = pl.ds(pl.multiple_of(head * size, size), size)

                    def soften(block, i=i, head=head):
                        scores = s_v[i, block, :length] * scale + bias_v[block, :length]
                        top = jnp.max(scores, axis=1, keepdims=True)
                        weights = jnp.exp2(scores - top)
                        total = jnp.sum(weights, axis=1, keepdims=True)
                        p_v[i, block, :length] = (weights * (1.0 / total)).astype(BF16)
                        lse_v[block, :] = jnp.where(lane == head, top + jnp.log2(total), lse_v[block, :])

                    each_block(rows, SOFTMAX_BLOCK, soften, rows // SOFTMAX_BLOCK)
                    o_v[:, cols] = dot(p_v[i, :, :length], v_v[:length, :]).astype(BF16)
                return carry

            lax.fori_loop(0, heads // FWD_HEADS, some_heads, 0)

        for static_place in places:
            if len(places) == 1:
                attend(static_place)
            else:
                pl.when(place == static_place)(functools.partial(attend, static_place))

        keep(lse_v, lses.at[at], 10)
        keep(o_v, os_.at[at], 11)
        loaded("out")
        total_v[...] = dot(o_v[...], w_out[...])

        def norm_ffn(block):
            mid = h_v[block, :].astype(F32) + total_v[block, :]
            mid_v[block, :] = mid
            total_v[block, :] = mid
            n2_v[block, :] = (mid * inverse_rms(mid) * gain_ffn[...].astype(F32)).astype(BF16)

        each_block(rows, NORM_BLOCK, norm_ffn, rows // NORM_BLOCK)
        keep(mid_v, mids.at[at], 12)
        keep(n2_v, n2s.at[at], 13)
        ffn = w_up.shape[1]
        tile = min(FFN_TILE, ffn)


        def columns(f):
            return pl.ds(pl.multiple_of(f * tile, tile), tile)

        def rise(f):
            return dot(n2_v[...], w_up[:, columns(f)])

        def bend(f, u):
            act, slope = gelu_parts(u)
            act_v[:, columns(f)] = act.astype(BF16)
            slope_v[:, columns(f)] = slope.astype(BF16)
            pltpu.make_async_copy(act_v.at[:, columns(f)], acts.at[at, columns(f)], sems.at[14]).start()
            pltpu.make_async_copy(slope_v.at[:, columns(f)], slopes.at[at, columns(f)], sems.at[15]).start()

        def fall(f):
            return dot(act_v[:, columns(f)], w_down[columns(f), :])

        def both(f, carry):
            u = rise(f)
            part = fall(f - 1)
            bend(f, u)
            total_v[...] += part
            return carry

        loaded("up0")
        bend(0, rise(0))
        loaded("up1", "down0")
        lax.fori_loop(1, ffn // tile, both, 0)
        loaded("down1")
        total_v[...] += fall(ffn // tile - 1)
        total = total_v[...]
        pending.append(pltpu.make_async_copy(act_v, acts.at[at], sems.at[14]))
        pending.append(pltpu.make_async_copy(slope_v, slopes.at[at], sems.at[15]))
        result = total.astype(BF16)
        out[...] = result
        out_v[...] = result
        keep(out_v, outs.at[at], 16)
        for copy in pending:
            copy.wait()


FWD_SAVED = ("hs", "n1s", "qs", "ks", "vs", "kts", "vts", "os", "mids", "n2s", "acts", "slopes", "lses", "outs")


def forward_chunk(geometry, places, spots, meta, tokens, incoming, weights, saved, given=None):
    rows, row_len, heads, size, unused = geometry
    gain_attn, gain_ffn, *matrices = weights
    loading = given is not None
    width = tokens.shape[1]
    ffn = (given[4] if loading else matrices[3]).shape[1]
    vmem = pl.BlockSpec(memory_space=pltpu.VMEM)
    hbm = pl.BlockSpec(memory_space=pltpu.HBM)
    loads = [pltpu.VMEM(shape, BF16) for shape in weight_shapes(given)] if loading else []
    operands = list(map(in_hbm, given)) if loading else list(map(in_vmem, matrices))
    lead = 5 + len(operands)
    flops = 2 * rows * (2 * width * heads * size + 2 * width * size + 2 * width * ffn + row_len * heads * size)
    out, *rest = pl.pallas_call(
        functools.partial(forward_kernel, geometry, loading, places, spots),
        out_shape=[jax.ShapeDtypeStruct((rows, width), BF16)]
        + [pltpu.HBM(array.shape, array.dtype) for array in saved] + loads,
        in_specs=[pl.BlockSpec(memory_space=pltpu.SMEM), hbm, vmem, vmem, vmem]
        + [hbm if loading else vmem] * len(operands) + [hbm] * len(saved),
        out_specs=[vmem] + [hbm] * len(saved) + [vmem] * len(loads),
        input_output_aliases={lead + i: 1 + i for i in range(len(saved))},
        scratch_shapes=[
            pltpu.VMEM((rows, width), BF16),
            pltpu.VMEM((rows, width), BF16),
            pltpu.VMEM((rows, heads * size), BF16),
            pltpu.VMEM((rows, size), BF16),
            pltpu.VMEM((row_len, size), BF16),
            pltpu.VMEM((size, row_len), BF16),
            pltpu.VMEM((size, rows), BF16),
            pltpu.VMEM((rows, heads * size), BF16),
            pltpu.VMEM((rows, width), F32),
            pltpu.VMEM((rows, width), BF16),
            pltpu.VMEM((rows, ffn), BF16),
            pltpu.VMEM((rows, ffn), BF16),
            pltpu.VMEM((rows, size), F32),
            pltpu.VMEM((rows, width), BF16),
            pltpu.VMEM((rows, row_len), F32),
            pltpu.VMEM((rows, width), F32),
            pltpu.VMEM((FWD_HEADS, rows, row_len), F32),
            pltpu.VMEM((FWD_HEADS, rows, row_len), BF16),
            pltpu.SemaphoreType.DMA((17,)),
        ]
        + [pltpu.SemaphoreType.DMA((8,))] * loading,
        compiler_params=pltpu.CompilerParams(vmem_limit_bytes=12 * MIB),
        cost_estimate=pl.CostEstimate(flops=flops, bytes_accessed=8 * MIB, transcendentals=0),
        name="forward_chunk",
    )(meta, in_hbm(tokens), in_vmem(incoming), gain_attn, gain_ffn, *operands, *saved)
    return out, rest[:len(saved)], rest[len(saved):]


def weight_shapes(given):
    w_query, w_key, w_value, w_out, w_up, w_down = given
    return w_query.shape, (w_key.shape[0], 2 * w_key.shape[1]), w_out.shape, w_up.shape, w_down.shape


BWD_SAVED = ("gbs", "dus", "gms", "dqkvs", "igs", "gains", "carry")


def norm_backward(rows, gain, upstream):
    inverse = inverse_rms(rows)
    unit = rows * inverse
    steered = upstream * gain
    grad = inverse * (steered - unit * jnp.mean(steered * unit, axis=-1, keepdims=True))
    return grad, jnp.sum((upstream * unit).reshape(-1, 8, rows.shape[1]), axis=0)


def backward_kernel(
    geometry, last_call, gates, static_place, spots, meta, cotangent, incoming, hs, qs, ks, kts, vts, mids, slopes, lses,
    gain_attn, gain_ffn, *refs,
):
    rows, row_len, heads, size, segments = geometry
    spot, lengths_spot = spots
    if last_call:
        sources, refs = refs[:6], refs[6:]
        w_query, w_kv, w_out, w_up, w_down, load_sems = refs[-6:]
        refs = refs[:-6]
        weight_loads = weight_copies(sources, (w_query, w_kv, w_out, w_up, w_down), load_sems)
    else:
        w_query, w_kv, w_out, w_up, w_down = refs[:5]
        refs = refs[5:]

    def loaded(*names):
        for name in names if last_call else ():
            weight_loads[name].wait()

    refs = refs[gates:]
    count = len(BWD_SAVED) - last_call
    out, *gbs, dus, gms, dqkvs, igs, gains, carry = refs[count:2 * count + 1]
    (g_v, h_v, q_v, k_v, kt_v, vt_v, mid_v, slope_v, lse_v, du_v, gm_v, do_v, dqkv_v, ig_v, gain_v, carry_v,
     bias_v, total_v, s_v, dp_v, p_v, ds_v, sems) = refs[2 * count + 1:]
    parts = row_len // rows
    active, chunk, first = meta[spot], meta[spot + 1], meta[spot + 2]
    scale = size**-0.5
    width = heads * size

    @pl.when(active == 1)
    def _():
        row = chunk // parts
        at = pl.ds(pl.multiple_of(chunk * rows, rows), rows)
        whole = pl.ds(pl.multiple_of(row * row_len, row_len), row_len)

        @pl.when(first == 1)
        def _():
            pltpu.make_async_copy(cotangent.at[at], g_v, sems.at[0]).start()

        loads = [
            pltpu.make_async_copy(source, target, sems.at[1 + i])
            for i, (source, target) in enumerate((
                (slopes.at[at], slope_v),
                (mids.at[at], mid_v),
                (qs.at[at], q_v),
                (lses.at[at], lse_v),
                (kts.at[row], kt_v),
                (vts.at[row], vt_v),
                (ks.at[whole], k_v),
                (carry, carry_v),
                (hs.at[at], h_v),
            ))
        ]
        for load in loads[:1]:
            load.start()
        for name in BWD_LOADS[:2] if last_call else ():
            weight_loads[name].start()
        for load in loads[1:]:
            load.start()
        for name in BWD_LOADS[2:] if last_call else ():
            weight_loads[name].start()
        pending = []

        def keep(source, target, slot):
            copy = pltpu.make_async_copy(source, target, sems.at[slot])
            copy.start()
            pending.append(copy)

        length = (static_place + 1) * rows
        bias_v[:, :length] = position_bias(
            meta, lengths_spot + row * segments, segments, static_place * rows, rows, length
        )
        @pl.when(first == 1)
        def _():
            pltpu.make_async_copy(cotangent.at[at], g_v, sems.at[0]).wait()

        @pl.when(first == 0)
        def _():
            g_v[...] = incoming[...]

        if not last_call:
            keep(g_v, gbs[0].at[at], 10)
        loads[0].wait()
        ffn = w_up.shape[1]
        tile = min(BWD_TILE, ffn)

        def rise(f):
            cols = pl.ds(pl.multiple_of(f * tile, tile), tile)
            return dot_t(g_v[...], w_down[cols, :])

        def bend(f, da):
            cols = pl.ds(pl.multiple_of(f * tile, tile), tile)
            du_v[:, cols] = (slope_v[:, cols].astype(F32) * da).astype(BF16)

        def fall(f):
            cols = pl.ds(pl.multiple_of(f * tile, tile), tile)
            return dot_t(du_v[:, cols], w_up[:, cols])

        def both(f, carry):
            da = rise(f)
            part = fall(f - 1)
            bend(f, da)
            total_v[...] = jnp.where(f == 1, part, total_v[...] + part)
            return carry

        loaded("down0")
        bend(0, rise(0))
        loaded("up0", "down1")
        lax.fori_loop(1, ffn // tile, both, 0)
        loaded("up1")
        total_v[...] += fall(ffn // tile - 1)
        keep(du_v, dus.at[at], 11)
        loads[1].wait()
        gain_v[...] = jnp.zeros(gain_v.shape, F32)

        def norm_ffn(block):
            dv, dgain = norm_backward(mid_v[block, :], gain_ffn[...].astype(F32), total_v[block, :])
            dmid = g_v[block, :].astype(F32) + dv
            mid_v[block, :] = dmid
            gm_v[block, :] = dmid.astype(BF16)
            gain_v[8:, :] += dgain

        each_block(rows, NORM_BLOCK, norm_ffn, rows // NORM_BLOCK)
        keep(gm_v, gms.at[at], 12)
        loaded("out")
        do_v[...] = dot_t(gm_v[...], w_out[...]).astype(BF16)
        for load in loads[2:8]:
            load.wait()

        if static_place == parts - 1:
            carry_v[...] = jnp.zeros(carry_v.shape, F32)

        def attend():
            lane = lax.broadcasted_iota(jnp.int32, (SOFTMAX_BLOCK, size), 1)

            def some_heads(step, unused):
                group = [step * BWD_HEADS + i for i in range(BWD_HEADS)]
                for i, head in enumerate(group):
                    cols = pl.ds(pl.multiple_of(head * size, size), size)
                    s_v[i, :, :length] = dot(q_v[:, cols], kt_v[:, :length])
                    dp_v[i, :, :length] = dot(do_v[:, cols], vt_v[:, :length])
                for i, head in enumerate(group):
                    cols = pl.ds(pl.multiple_of(head * size, size), size)

                    def steepen(block, i=i, head=head):
                        lse = jnp.sum(jnp.where(lane == head, lse_v[block, :], 0.0), axis=1, keepdims=True)
                        scores = s_v[i, block, :length] * (scale * LOG2E) + bias_v[block, :length]
                        probs = jnp.exp2(scores - lse)
                        p_v[i, block, :length] = probs.astype(BF16)
                        dprobs = dp_v[i, block, :length]
                        mean = jnp.sum(probs * dprobs, axis=1, keepdims=True)
                        ds_v[i, block, :length] = (probs * (dprobs - mean)).astype(BF16)

                    each_block(rows, SOFTMAX_BLOCK, steepen, rows // SOFTMAX_BLOCK)
                    dqkv_v[:, cols] = (dot(ds_v[i, :, :length], k_v[:length, :]) * scale).astype(BF16)
                    carry_v[:size, :length] += dot(q_v[:, cols].T, ds_v[i, :, :length])
                    carry_v[size:, :length] += dot(do_v[:, cols].T, p_v[i, :, :length])
                return unused

            lax.fori_loop(0, heads // BWD_HEADS, some_heads, 0)
            own = slice(length - rows, length)
            dqkv_v[:, width:width + size] = (carry_v[:size, own].T * scale).astype(BF16)
            dqkv_v[:, width + size:] = carry_v[size:, own].T.astype(BF16)

        attend()

        keep(carry_v, carry, 13)
        keep(dqkv_v, dqkvs.at[at], 14)
        loaded("query", "key", "value")
        dn1 = dot_t(dqkv_v[:, :width], w_query[...]) + dot_t(dqkv_v[:, width:], w_kv[...])
        loads[8].wait()
        total_v[...] = dn1

        def norm_attn(block):
            dv, dgain = norm_backward(h_v[block, :].astype(F32), gain_attn[...].astype(F32), total_v[block, :])
            ig_v[block, :] = (mid_v[block, :] + dv).astype(BF16)
            gain_v[:8, :] += dgain

        each_block(rows, NORM_BLOCK, norm_attn, rows // NORM_BLOCK)
        out[...] = ig_v[...]
        keep(ig_v, igs.at[at], 16)
        keep(gain_v, gains.at[chunk], 17)
        for copy in pending:
            copy.wait()


def backward_chunk(geometry, last_call, static_place, spots, meta, cotangent, incoming, kept, weights, saved, gates=()):
    rows, row_len, heads, size, unused = geometry
    gain_attn, gain_ffn, *matrices = weights
    width = cotangent.shape[1]
    ffn = matrices[4 if last_call else 3].shape[1]
    vmem = pl.BlockSpec(memory_space=pltpu.VMEM)
    hbm = pl.BlockSpec(memory_space=pltpu.HBM)
    lead = 3 + len(kept) + len(weights) + len(gates)
    flops = 2 * rows * (2 * width * heads * size + 2 * width * size + 2 * width * ffn + 3 * row_len * heads * size)
    return pl.pallas_call(
        functools.partial(backward_kernel, geometry, last_call, len(gates), static_place, spots),
        out_shape=[jax.ShapeDtypeStruct((rows, width), BF16)]
        + [pltpu.HBM(array.shape, array.dtype) for array in saved],
        in_specs=[pl.BlockSpec(memory_space=pltpu.SMEM), hbm, vmem]
        + [hbm] * len(kept) + [vmem] * 2 + [hbm if last_call else vmem] * len(matrices)
        + [pl.BlockSpec(memory_space=pl.ANY)] * len(gates) + [hbm] * len(saved),
        out_specs=[vmem] + [hbm] * len(saved),
        input_output_aliases={lead + i: 1 + i for i in range(len(saved))},
        scratch_shapes=[
            pltpu.VMEM((rows, width), BF16),
            pltpu.VMEM((rows, width), BF16),
            pltpu.VMEM((rows, heads * size), BF16),
            pltpu.VMEM((row_len, size), BF16),
            pltpu.VMEM((size, row_len), BF16),
            pltpu.VMEM((size, row_len), BF16),
            pltpu.VMEM((rows, width), F32),
            pltpu.VMEM((rows, ffn), BF16),
            pltpu.VMEM((rows, size), F32),
            pltpu.VMEM((rows, ffn), BF16),
            pltpu.VMEM((rows, width), BF16),
            pltpu.VMEM((rows, heads * size), BF16),
            pltpu.VMEM((rows, (heads + 2) * size), BF16),
            pltpu.VMEM((rows, width), BF16),
            pltpu.VMEM((16, width), F32),
            pltpu.VMEM((2 * size, row_len), F32),
            pltpu.VMEM((rows, row_len), F32),
            pltpu.VMEM((rows, width), F32),
            pltpu.VMEM((BWD_HEADS, rows, row_len), F32),
            pltpu.VMEM((BWD_HEADS, rows, row_len), F32),
            pltpu.VMEM((BWD_HEADS, rows, row_len), BF16),
            pltpu.VMEM((BWD_HEADS, rows, row_len), BF16),
            pltpu.SemaphoreType.DMA((18,)),
        ]
        + [pltpu.VMEM(shape, BF16) for shape in (weight_shapes(matrices) if last_call else ())]
        + [pltpu.SemaphoreType.DMA((8,))] * last_call,
        compiler_params=pltpu.CompilerParams(vmem_limit_bytes=(46 if last_call else 24) * MIB),
        cost_estimate=pl.CostEstimate(
            flops=1024 if last_call else flops, bytes_accessed=1024 if last_call else 8 * MIB, transcendentals=0
        ),
        name="backward_chunk",
    )(
        meta, in_hbm(cotangent), in_vmem(incoming), *map(in_hbm, kept), gain_attn, gain_ffn,
        *map(in_hbm if last_call else in_vmem, matrices), *gates, *saved,
    )


def unwritten(shapes):
    return pl.pallas_call(
        lambda *refs: None,
        out_shape=shapes,
        out_specs=[pl.BlockSpec(memory_space=pltpu.HBM)] * len(shapes),
        compiler_params=pltpu.CompilerParams(vmem_limit_bytes=2 * MIB),
        name="unwritten",
    )()


def dest_chip(step):
    chips = lax.axis_size("dp") // 2
    return lax.rem(lax.axis_index("dp") // 2 + 2 * chips - 1 - step, chips)


def swap_cores(block):
    return lax.ppermute(block, "dp", [(i, i ^ 1) for i in range(lax.axis_size("dp"))])


def next_chip(block):
    devices = lax.axis_size("dp")
    return lax.ppermute(block, "dp", [(i, (i + 2) % devices) for i in range(devices)])


def largest_tile(width, most):
    return max(tile for tile in range(128, most + 1, 128) if width % tile == 0)


def product_kernel(pairs, offsets, gates, share, spots, meta, *refs):
    refs = refs[gates:]
    lefts, rights, refs = refs[:pairs], refs[pairs:2 * pairs], refs[2 * pairs:]
    extras = refs[:1] if pairs > 1 else ()
    refs = refs[len(extras):]
    added, refs = refs[:len(offsets)], refs[len(offsets):]
    outs, refs = refs[:len(refs) - 2 * pairs - 2], refs[len(refs) - 2 * pairs - 2:]
    lefts_v, rights_v, left_sems, right_sems = refs[:pairs], refs[pairs:2 * pairs], refs[-2], refs[-1]
    blocks = lefts_v[0].shape[0]
    left_copies, right_copies = [], []
    for i in range(pairs):
        for b in range(blocks):
            source = lefts[i]
            if source.shape[1] != share:
                source = source.at[:, pl.ds(pl.multiple_of(meta[spots[b]] * share, 128), share)]
            left_copies.append(pltpu.make_async_copy(source, lefts_v[i].at[b], left_sems.at[i * blocks + b]))
            left_copies[-1].start()
        wide = largest_tile(rights[i].shape[1], 1280)
        for n in range(rights[i].shape[1] // wide):
            cols = slice(n * wide, (n + 1) * wide)
            copy = pltpu.make_async_copy(rights[i].at[:, cols], rights_v[i].at[:, cols], right_sems.at[len(right_copies)])
            copy.start()
            right_copies.append((copy, i, n, wide))

    def put(row, depth, col, value):
        cols = slice(col, col + value.shape[1])
        if row < outs[0].shape[0]:
            for more, offset in zip(added, offsets):
                value = value + more[offset + row:offset + row + depth, cols].astype(F32)
            outs[0][row:row + depth, cols] = value.astype(outs[0].dtype)
        else:
            row -= outs[0].shape[0]
            outs[1][row:row + depth, cols] = value.astype(outs[1].dtype)

    deep = min(share, 256)
    first_col = 0
    for copy, i, n, wide in right_copies:
        copy.wait()
        for b in range(blocks):
            if n == 0:
                left_copies[i * blocks + b].wait()
            for m in range(share // deep):
                value = lax.dot_general(
                    lefts_v[i][b, :, m * deep:(m + 1) * deep], rights_v[i][:, n * wide:(n + 1) * wide],
                    (((0,), (0,)), ((), ())), preferred_element_type=F32,
                )
                put(b * share + m * deep, deep, first_col, value)
        first_col += wide
    if extras:
        gains = extras[0]
        for b in range(blocks):
            own = gains[...]
            if gains.shape[2] != share:
                own = gains[:, :, pl.ds(pl.multiple_of(meta[spots[b]] * share, 128), share)]
            own = jnp.sum(own, axis=0).reshape(2, 8, share)
            own = jnp.concatenate([jnp.sum(own, axis=1), jnp.zeros((GAIN_COLS - 2, share), F32)], axis=0)
            put(b * share, share, first_col, own.T)


def products(share, spots, meta, lefts, rights, extra, added, dtype, gates, split, cost):
    vmem = pl.BlockSpec(memory_space=pltpu.VMEM)
    hbm = pl.BlockSpec(memory_space=pltpu.HBM)
    count = len(spots)
    if share % 128:
        blocks = [[lax.dynamic_slice_in_dim(left, meta[spot] * share, share, 1) for spot in spots] for left in lefts]
        if count > 1:
            parts = [
                products(
                    share, spots[b:b + 1], meta, lefts, rights, extra,
                    [] if split and b else [(more, at + b * share) for more, at in added], dtype, gates, False, cost,
                )[0]
                for b in range(count)
            ]
            return parts if split else [jnp.concatenate(parts, axis=0)]
        lefts = [block[0] for block in blocks]
        extra = None if extra is None else lax.dynamic_slice_in_dim(extra, meta[spots[0]] * share, share, 2)
    depth = lefts[0].shape[0]
    extras = [] if extra is None else [extra]
    total = sum(right.shape[1] for right in rights) + GAIN_COLS * len(extras)
    return pl.pallas_call(
        functools.partial(product_kernel, len(lefts), tuple(at for unused, at in added), len(gates), share, spots),
        out_shape=[jax.ShapeDtypeStruct((share if split else count * share, total), dtype)] * (2 if split else 1),
        in_specs=[pl.BlockSpec(memory_space=pltpu.SMEM)] + [pl.BlockSpec(memory_space=pl.ANY)] * len(gates)
        + [hbm] * (2 * len(lefts)) + [vmem] * (len(extras) + len(added)),
        out_specs=[vmem] * (2 if split else 1),
        scratch_shapes=[pltpu.VMEM((count, depth, share), BF16) for _ in lefts]
        + [pltpu.VMEM(right.shape, BF16) for right in rights]
        + [pltpu.SemaphoreType.DMA((len(lefts) * count,)), pltpu.SemaphoreType.DMA((8,))],
        compiler_params=pltpu.CompilerParams(vmem_limit_bytes=24 * MIB),
        cost_estimate=pl.CostEstimate(flops=cost, bytes_accessed=1024, transcendentals=0),
        name="products",
    )(
        meta, *gates, *map(in_hbm, lefts), *map(in_hbm, rights), *extras,
        *(more for more, unused in added),
    )


def add_kernel(offset, kept, come, *outs):
    start = 0
    for out in outs:
        cols = slice(start, start + out.shape[1])
        out[...] = (kept[offset:offset + out.shape[0], cols].astype(F32) + come[:, cols].astype(F32)).astype(out.dtype)
        start += out.shape[1]


def add(kept, offset, come, dtype, widths):
    vmem = pl.BlockSpec(memory_space=pltpu.VMEM)
    return pl.pallas_call(
        functools.partial(add_kernel, offset),
        out_shape=[jax.ShapeDtypeStruct((come.shape[0], width), dtype) for width in widths or [come.shape[1]]],
        in_specs=[vmem, vmem],
        out_specs=[vmem] * len(widths or [1]),
        compiler_params=pltpu.CompilerParams(vmem_limit_bytes=4 * MIB),
        cost_estimate=pl.CostEstimate(flops=10**11, bytes_accessed=1024, transcendentals=0),
        name="add",
    )(kept, come)


class RowSums:
    def __init__(self, meta, spot, lefts, rights, extra=None):
        self.meta, self.spot, self.lefts, self.rights, self.extra = meta, spot, lefts, rights, extra
        self.share = lefts[0].shape[1] // lax.axis_size("dp")

    def blocks(self, steps, half, gates, added, dtype, cost):
        spots = [self.spot + 2 * step + half for step in steps]
        return products(self.share, spots, self.meta, self.lefts, self.rights, self.extra, added, dtype, gates, False, cost)

    def other(self, steps, gates=(), cost=LIGHT):
        return self.blocks(steps, 1, gates, [], BF16, cost)[0]

    def own_and_other(self, own_step, other_step, added):
        spots = [self.spot + 2 * own_step, self.spot + 2 * other_step + 1]
        return products(
            self.share, spots, self.meta, self.lefts, self.rights, self.extra, added, BF16, (), True, LIGHT
        )

    def own(self, steps, gates, added, dtype=BF16, cost=LIGHT):
        return self.blocks(steps, 0, gates, added, dtype, cost)[0]


def keep_last_kernel(rows, spot, meta, incoming, unused, gbs, sem):
    @pl.when(meta[spot] == 1)
    def _():
        at = pl.ds(pl.multiple_of(meta[spot + 1] * rows, rows), rows)
        copy = pltpu.make_async_copy(incoming, gbs.at[at], sem)
        copy.start()
        copy.wait()


def keep_last(spot, meta, incoming, gbs):
    anywhere = pl.BlockSpec(memory_space=pltpu.HBM)
    return pl.pallas_call(
        functools.partial(keep_last_kernel, incoming.shape[0], spot),
        out_shape=pltpu.HBM(gbs.shape, gbs.dtype),
        in_specs=[pl.BlockSpec(memory_space=pltpu.SMEM), pl.BlockSpec(memory_space=pl.ANY), anywhere],
        out_specs=anywhere,
        input_output_aliases={2: 0},
        scratch_shapes=[pltpu.SemaphoreType.DMA],
        compiler_params=pltpu.CompilerParams(vmem_limit_bytes=2 * MIB),
        name="keep_last",
    )(meta, incoming, gbs)


def body(
    tokens, lengths, gain_attn, w_query, w_key, w_value, w_out, gain_ffn, w_up, w_down, cotangent
):
    micro, row_len, width = tokens.shape
    size = w_key.shape[2]
    heads = w_query.shape[2] // size
    ffn = w_up.shape[2]
    count = micro * row_len
    sections = lax.axis_size("section")
    place = lax.axis_index("section")
    gains = [gain_attn, gain_ffn]
    given = [w_query[0], w_key[0], w_value[0], w_out[0], w_up[0], w_down[0]]
    weights = gains
    token_rows = tokens.reshape(count, width)
    cotangent_rows = cotangent.reshape(count, width)
    segments = lengths.shape[2]

    def empty(*shape, dtype=BF16):
        return pltpu.HBM(shape, dtype)

    def meta_of(tick, chunks, rank, order):
        step = tick - SKEW * rank
        active = (step >= 0) & (step < chunks)
        return [active, order(jnp.clip(step, 0, chunks - 1)), rank == 0]

    def hop(block, tick, chunks, rank_of, shift):
        route = [
            (s, s + shift)
            for s in range(sections)
            if 0 <= s + shift < sections and 0 <= tick - SKEW * rank_of(s) < chunks
        ]
        return lax.ppermute(block, "section", route) if route else None

    fwd_geometry = (FWD_ROWS, row_len, heads, size, segments)
    fwd_chunks = count // FWD_ROWS
    fwd_ticks = fwd_chunks + SKEW * (sections - 1)
    bwd_geometry = (BWD_ROWS, row_len, heads, size, segments)
    bwd_chunks = count // BWD_ROWS
    bwd_ticks = bwd_chunks + SKEW * (sections - 1)
    parts = row_len // BWD_ROWS
    chips = lax.axis_size("dp") // 2
    core = lax.axis_index("dp") % 2
    meta = []
    for tick in range(fwd_ticks):
        meta += meta_of(tick, fwd_chunks, place, lambda step: step)
    for tick in range(bwd_ticks):
        meta += meta_of(
            tick, bwd_chunks, sections - 1 - place, lambda step: step // parts * parts + parts - 1 - step % parts
        )
    for step in range(chips):
        meta += [dest_chip(step) * 2 + core, dest_chip(step) * 2 + 1 - core]
    blocks_spot = 3 * (fwd_ticks + bwd_ticks)
    lengths_spot = len(meta)
    meta = jnp.concatenate([jnp.stack([jnp.asarray(entry, jnp.int32) for entry in meta]), lengths.reshape(-1)])
    saved = [
        empty(count, width), empty(count, width), empty(count, heads * size), empty(count, size), empty(count, size),
        empty(micro, size, row_len), empty(micro, size, row_len), empty(count, heads * size),
        empty(count, width, dtype=F32), empty(count, width), empty(count, ffn), empty(count, ffn),
        empty(count, size, dtype=F32), empty(count, width),
    ]
    saved = unwritten(saved)
    received = {}
    nothing = jnp.zeros((FWD_ROWS, width), BF16)
    for tick in range(fwd_ticks):
        incoming = received.pop(tick - SKEW, None)
        at_work = [tick - SKEW * s for s in range(sections) if 0 <= tick - SKEW * s < fwd_chunks]
        places = sorted({chunk % (row_len // FWD_ROWS) for chunk in at_work})
        out, saved, loads = forward_chunk(
            fwd_geometry, places, (3 * tick, lengths_spot), meta, token_rows, nothing if incoming is None else incoming, weights, saved,
            None if tick else given,
        )
        weights = weights + loads
        received[tick] = hop(out, tick, fwd_chunks, lambda s: s, 1)

    kept = dict(zip(FWD_SAVED, saved))
    layer_outs = kept["outs"]
    needed = [kept[name] for name in ("hs", "qs", "ks", "kts", "vts", "mids", "slopes", "lses")]
    saved = unwritten([
        empty(count, width), empty(count, ffn), empty(count, width), empty(count, (heads + 2) * size),
        empty(count, width), empty(bwd_chunks, 16, width, dtype=F32), empty(2 * size, row_len, dtype=F32),
    ])
    received = {}
    nothing = jnp.zeros((BWD_ROWS, width), BF16)
    down_sums = None
    for tick in range(bwd_ticks):
        spot = 3 * (fwd_ticks + tick)
        static_place = parts - 1 - tick % parts
        incoming = received.pop(tick - SKEW, None)
        if incoming is None:
            incoming = nothing
        if tick == bwd_ticks - 1:
            gbs = keep_last(spot, meta, incoming, saved[0])
            down_sums = RowSums(meta, blocks_spot, [kept["acts"]], [gbs])
            swapped = swap_cores(down_sums.other([0]))
            first_total, ready = down_sums.own_and_other(0, 1, [(swapped, 0)])
            down_ring = next_chip(first_total)
            swapped = swap_cores(ready)
            out, *rest = backward_chunk(
                bwd_geometry, True, static_place, (spot, lengths_spot), meta, cotangent_rows, incoming, needed, gains + given, saved[1:],
                [first_total, ready],
            )
            saved = [gbs] + rest
            continue
        out, *saved = backward_chunk(
            bwd_geometry, False, static_place, (spot, lengths_spot), meta, cotangent_rows, incoming, needed, weights, saved
        )
        received[tick] = hop(out, tick, bwd_chunks, lambda s: sections - 1 - s, -1)
    done = dict(zip(BWD_SAVED, saved))

    rest_sums = RowSums(
        meta, blocks_spot, [kept["n2s"], kept["n1s"], kept["os"]], [done["dus"], done["dqkvs"], done["gms"]], done["gains"]
    )
    later = list(range(1, chips))
    widths = [ffn, heads * size, size, size, width, 128]

    rest_other = rest_sums.other([0])
    down = down_sums.own([1], [rest_other], [(swapped, 0), (down_ring, 0)], BF16 if chips > 2 else F32)
    if chips > 2:
        down_ring = next_chip(down)
    swapped = swap_cores(rest_other)
    down_others = down_sums.other(later[1:], [down]) if chips > 2 else None
    rest = rest_sums.own([0], [down] if down_others is None else [down_others], [(swapped, 0)], cost=HEAVY)
    rest_ring = next_chip(rest)
    if chips > 2:
        down_swapped = swap_cores(down_others)
    if chips > 2:
        down_kept = down_sums.own(later[1:], [rest], [(down_swapped, 0)], cost=HEAVY)
    rest_others = rest_sums.other(later, [rest, down_ring], cost=HEAVY)
    rest_swapped = swap_cores(rest_others)
    rest_kept = None
    for step in range(1, chips):
        if step + 1 < chips:
            last = step + 1 == chips - 1
            down = add(down_kept, (step - 1) * down_sums.share, down_ring, F32 if last else BF16, None)[0]
            if not last:
                down_ring = next_chip(down)
        if rest_kept is None:
            rest_kept = rest_sums.own(later, [down], [(rest_swapped, 0)], cost=HEAVY)
        last = step == chips - 1
        rest = add(
            rest_kept, (step - 1) * rest_sums.share, rest_ring, F32 if last else BF16, widths if last else None
        )
        if not last:
            rest_ring = next_chip(rest[0])
    up, query, key, value, out, gains = rest
    shares = (gains[:, 0], query, key, value, out, gains[:, 1], up, down)
    shape = (1, micro, row_len, width)
    return (layer_outs.reshape(shape), done["igs"].reshape(shape)) + tuple(share[None] for share in shares)


def solution(mesh):
    return jax.shard_map(
        body,
        mesh=mesh,
        in_specs=(
            P(None, "dp", None),
            P(None, "dp", None),
            P("section", None),
            P("section", None, None),
            P("section", None, None),
            P("section", None, None),
            P("section", None, None),
            P("section", None),
            P("section", None, None),
            P("section", None, None),
            P(None, "dp", None),
        ),
        out_specs=(
            P("section", None, "dp", None),
            P("section", None, "dp", None),
            P("section", "dp"),
            P("section", "dp", None),
            P("section", "dp", None),
            P("section", "dp", None),
            P("section", "dp", None),
            P("section", "dp"),
            P("section", "dp", None),
            P("section", "dp", None),
        ),
        check_vma=False,
    )
```
